32 devices in a mesh: fsdp: 8 (over y, x, core), tp: 4 (over z).
Axes of the slice: x: 2, y: 2, z: 4, core: 2. Of those that a mesh axis runs over, the one named last changes fastest.
Arguments:
- tokens: bfloat16 [7168, 2048], P('fsdp', 'tp'), may hold values from -6 to 6
- cotangent: bfloat16 [7168, 2048], P('fsdp', 'tp'), may hold values from -6 to 6
- w_query: bfloat16 [2048, 2048], P('fsdp', 'tp'), may hold values from -0.25 to 0.25
- w_key: bfloat16 [2048, 2048], P('fsdp', 'tp'), may hold values from -0.125 to 0.125
- w_value: bfloat16 [2048, 2048], P('fsdp', 'tp'), may hold values from -0.125 to 0.125
- w_out: bfloat16 [2048, 2048], P(('tp', 'fsdp')), may hold values from -0.75 to 0.75
- w_gate: bfloat16 [2048, 8192], P('fsdp', 'tp'), may hold values from -0.125 to 0.125
- w_up: bfloat16 [2048, 8192], P('fsdp', 'tp'), may hold values from -0.125 to 0.125
- w_down: bfloat16 [8192, 2048], P(('tp', 'fsdp')), may hold values from -0.0625 to 0.0625
- seq_lengths: int32 [8, 4], replicated, may hold values from 0 to 1024, as said below
- deal: int32 [8], replicated, may hold values from 0 to 7, as said below
- row_dest: int32 [7168], P('fsdp'), may hold values from 0 to 8191, as said below
Outputs:
- output: bfloat16 [7168, 2048], P('fsdp', 'tp')
- input_grad: bfloat16 [7168, 2048], P('fsdp', 'tp')
- grad_query: float32 [2048, 2048], P('fsdp', 'tp')
- grad_key: float32 [2048, 2048], P('fsdp', 'tp')
- grad_value: float32 [2048, 2048], P('fsdp', 'tp')
- grad_out: float32 [2048, 2048], P(('tp', 'fsdp'))
- grad_gate: float32 [2048, 8192], P('fsdp', 'tp')
- grad_up: float32 [2048, 8192], P('fsdp', 'tp')
- grad_down: float32 [8192, 2048], P(('tp', 'fsdp'))
The draws below stay inside these ranges and needn't reach their ends.
Inputs may be any that keep to these rules, and one draw needn't show every extreme that they name: `seq_lengths`: row k lists, in buffer order, the lengths of the sequences of the group deal[k], zero for an absent sequence. Each row sums to a multiple of 32 of at most 1024; in every draw one row is a single sequence of exactly 1024. `deal`: every group appears exactly once. `row_dest`: A value g * 1024 + j names slot j of group g's buffer; no slot is named twice, and the named slots of group g are its first ones, as many as its list of lengths sums to. The 896 given rows of one index of fsdp name at most 128 slots of one group; in every draw some group receives exactly 128 rows from every index of fsdp.
All inputs are finite; a program needn't handle non-finite values.
Results may differ from the reference program's by a relative error of at most 0.018.
Values may be sent and summed in bfloat16 or wider, within the bound.
No kernel may reach another device: no remote copies, remote signals or barrier semaphores. Data moves between devices by JAX's collectives and lax.ppermute only.
A program may use at most 256 MiB of HBM per device.

```python
import jax
import jax.numpy as jnp
from jax import lax

D = 2048
HEADS = 16
FF = 8192
HEAD_DIM = 128
GROUP_CAP = 1024
SEQ_SLOTS = 4
BLOCK = 32
TOK_GRP = 896
TOKENS = 7168
N_FSDP = 8


def dealing(key):
    base_key = jax.random.fold_in(key, 1234)
    key_load, key_deal, key_turn, key_shuffle, key_first, key_long, key_split = jax.random.split(base_key, 7)
    list_count = N_FSDP
    per_list = 32
    per_source = 28
    list_index = jnp.arange(list_count, dtype=jnp.int32)
    swing_half = jax.random.randint(key_load, (list_count // 2,), -2, 3)
    list_loads = 28 + jnp.stack([swing_half, -swing_half], axis=1).reshape(list_count)
    list_loads = jnp.where(list_index == 0, per_list, jnp.where(list_index == 1, 28, list_loads))
    list_loads = (list_loads - ((list_index >= 2) & (list_index < 6)).astype(jnp.int32)).astype(jnp.int32)
    deal_order = jax.random.permutation(key_deal, list_count).astype(jnp.int32)
    load_ends = jnp.cumsum(list_loads).astype(jnp.int32)
    starts = load_ends - list_loads
    item_index = jnp.arange(list_count * per_source, dtype=jnp.int32)
    owner_list = jnp.sum((item_index[:, None] >= load_ends[None, :]).astype(jnp.int32), axis=1).astype(jnp.int32)
    rotation = jax.random.randint(key_turn, (), 0, list_count)
    source = ((item_index + rotation) % list_count).astype(jnp.int32)
    round_index = item_index // list_count
    shuffles = jax.vmap(lambda sub_key: jax.random.permutation(sub_key, per_source))(jax.random.split(key_shuffle, list_count)).astype(jnp.int32)
    local_block = shuffles[source, round_index]
    offsets = jnp.arange(BLOCK, dtype=jnp.int32)
    given_rows = (source * TOK_GRP + local_block * BLOCK)[:, None] + offsets[None, :]
    owner_hit = owner_list[:, None] == list_index[None, :]
    owner_start = jnp.sum(jnp.where(owner_hit, starts[None, :], 0), axis=1)
    group_of = jnp.sum(jnp.where(owner_hit, deal_order[None, :], 0), axis=1)
    slot_rows = (group_of * GROUP_CAP + (item_index - owner_start) * BLOCK)[:, None] + offsets[None, :]
    row_dest = jnp.zeros((TOKENS,), jnp.int32).at[given_rows.reshape(-1)].set(slot_rows.reshape(-1).astype(jnp.int32))
    rows_load = list_loads * BLOCK
    first_len = jax.random.randint(key_first, (list_count,), 1, GROUP_CAP // 8 + 1)
    long_low = 3 * GROUP_CAP // 4 - first_len + 1
    long_len = jax.random.randint(key_long, (list_count,), long_low, rows_load - first_len + 1)
    rest_rows = rows_load - first_len - long_len
    third_len = jax.random.randint(key_split, (list_count,), 0, rest_rows + 1)
    fourth_len = rest_rows - third_len
    lengths = jnp.stack([first_len, long_len, third_len, fourth_len], axis=1)
    nothing = jnp.zeros_like(rows_load)
    single = jnp.stack([rows_load, nothing, nothing, nothing], axis=1)
    lengths = jnp.where((rows_load == GROUP_CAP)[:, None], single, lengths).astype(jnp.int32)
    return (row_dest, lengths, deal_order)


def draw_seq_lengths(key, part):
    return dealing(key)[1]


def draw_deal(key, part):
    return dealing(key)[2]


def draw_row_dest(key, part):
    return dealing(key)[0]


def shard_levels(rng, extent, pieces, least, top_value):
    def one(dim, shards_of):
        heights = jax.random.uniform(jax.random.fold_in(jax.random.fold_in(rng, 6), dim), (shards_of,), jnp.float32, least / len(pieces), top_value / len(pieces))
        return jnp.repeat(jnp.exp(heights), extent[dim] // shards_of).reshape((-1,) + (1,) * (len(extent) - dim - 1))

    gain = one(*pieces[0])
    for cut in pieces[1:]:
        gain = gain * one(*cut)
    return gain


def gaussian(rng, dims, width, reach, pieces=(), kind=jnp.bfloat16):
    gain = shard_levels(rng, dims, pieces, -0.22, 0.18) if pieces else 1.0
    values = jax.random.normal(rng, dims, jnp.float32) * width * gain
    return jnp.minimum(jnp.maximum(values, -reach), reach).astype(kind)


def setup_inputs(seed: int = 0) -> dict:
    keys = jax.random.split(jax.random.key(seed), 13)
    return {
        "tokens": gaussian(keys[0], (TOKENS, D), 1.0, 6.0, ((0, 8), (1, 4))),
        "cotangent": gaussian(keys[1], (TOKENS, D), 1.0, 6.0, ((0, 8), (1, 4))),
        "w_query": gaussian(keys[2], (D, D), (D // 4) ** -0.5, 0.25, ((0, 8), (1, 4))),
        "w_key": gaussian(keys[3], (D, D), D ** -0.5, 0.125, ((0, 8), (1, 4))),
        "w_value": gaussian(keys[4], (D, D), D ** -0.5, 0.125, ((0, 8), (1, 4))),
        "w_out": gaussian(keys[5], (D, D), (D // 32) ** -0.5, 0.75, ((0, 32),)),
        "w_gate": gaussian(keys[6], (D, FF), D ** -0.5, 0.125, ((0, 8), (1, 4))),
        "w_up": gaussian(keys[7], (D, FF), D ** -0.5, 0.125, ((0, 8), (1, 4))),
        "w_down": gaussian(keys[8], (FF, D), FF ** -0.5, 0.0625, ((0, 32),)),
        "seq_lengths": draw_seq_lengths(jax.random.fold_in(keys[12], 71), 0),
        "deal": draw_deal(jax.random.fold_in(keys[12], 71), 0),
        "row_dest": draw_row_dest(jax.random.fold_in(keys[12], 71), 0),
    }


@jax.custom_vjp
def low(v):
    return lax.optimization_barrier(v.astype(jnp.bfloat16)).astype(jnp.float32)

@jax.custom_vjp
def low_back(v):
    return v

def low_keep(v):
    return (low(v), None)

def low_pass(kept, grad):
    return (grad,)

def back_keep(v):
    return (v, None)

def back_low(kept, grad):
    return (low(grad),)
low.defvjp(low_keep, low_pass)
low_back.defvjp(back_keep, back_low)
norm_eps = 1e-05
rope_base = 10000.0
highest = lax.Precision.HIGHEST

def matmul(left, right):
    return jnp.dot(left, right, precision=highest, preferred_element_type=jnp.float32)

def layer_norm(values_in):
    row_mean = lax.optimization_barrier(jnp.mean(values_in, axis=-1, keepdims=True))
    centered = values_in - row_mean
    variance = lax.optimization_barrier(jnp.mean(centered * centered, axis=-1, keepdims=True))
    return centered * lax.rsqrt(variance + norm_eps)

def rope_tables(position, head_dim):
    half_dim = head_dim // 2
    frequency = rope_base ** (-(jnp.arange(half_dim, dtype=jnp.float32) * 2.0) / head_dim)
    angles = position.astype(jnp.float32)[:, None] * frequency[None, :]
    return (jnp.cos(angles), jnp.sin(angles))

def rotate(values_in, cosine, sine_table):
    half_dim = values_in.shape[-1] // 2
    first_half = values_in[..., :half_dim]
    second_half = values_in[..., half_dim:]
    cos_rows = cosine[:, None, :]
    sin_rows = sine_table[:, None, :]
    return jnp.concatenate([first_half * cos_rows - second_half * sin_rows, second_half * cos_rows + first_half * sin_rows], axis=-1)

def segments(lengths):
    load_ends = jnp.cumsum(lengths).astype(jnp.int32)
    row_index = jnp.arange(GROUP_CAP, dtype=jnp.int32)
    segment = lax.optimization_barrier(jnp.sum((row_index[:, None] >= load_ends[None, :]).astype(jnp.int32), axis=1)).astype(jnp.int32)
    seg_starts = jnp.concatenate([jnp.zeros((1,), jnp.int32), load_ends])
    slot_ids = jnp.arange(SEQ_SLOTS + 1, dtype=jnp.int32)
    begin_row = lax.optimization_barrier(jnp.sum(jnp.where(segment[:, None] == slot_ids[None, :], seg_starts[None, :], 0), axis=1)).astype(jnp.int32)
    return (segment, (row_index - begin_row).astype(jnp.int32))

def group_layer(buffer_rows, segment, position, weights):
    w_query, w_key, w_value, w_out, w_gate, w_up, w_down = weights
    normed_one = low(layer_norm(buffer_rows))
    cosine, sine_table = rope_tables(position, HEAD_DIM)
    query_pre = low_back(matmul(normed_one, w_query)).reshape(GROUP_CAP, HEADS, HEAD_DIM)
    key_pre = low_back(matmul(normed_one, w_key)).reshape(GROUP_CAP, HEADS, HEAD_DIM)
    value_rows = low(low_back(matmul(normed_one, w_value))).reshape(GROUP_CAP, HEADS, HEAD_DIM)
    queries = low(rotate(query_pre, cosine, sine_table))
    key_rows = low(rotate(key_pre, cosine, sine_table))
    row_index = jnp.arange(GROUP_CAP, dtype=jnp.int32)
    allowed = (segment[:, None] == segment[None, :]) & (row_index[None, :] <= row_index[:, None])
    scores = low_back(jnp.einsum('qhd,khd->hqk', queries, key_rows, precision=highest) * HEAD_DIM ** (-0.5))
    scores = jnp.where(allowed[None], scores, -1e+30)
    prob_low = low(jax.nn.softmax(scores, axis=-1))
    attended = low(low_back(jnp.einsum('hqk,khd->qhd', prob_low, value_rows, precision=highest))).reshape(GROUP_CAP, D)
    hidden = buffer_rows + low_back(matmul(attended, w_out))
    normed_two = low(layer_norm(hidden))
    gate_pre = low_back(matmul(normed_two, w_gate))
    up_pre = low_back(matmul(normed_two, w_up))
    activated = low(jax.nn.silu(gate_pre) * up_pre)
    return hidden + low_back(matmul(activated, w_down))

def reference(tokens, cotangent, w_query, w_key, w_value, w_out, w_gate, w_up, w_down, seq_lengths, deal, row_dest):
    group_count = deal.shape[0]
    slot_count = group_count * GROUP_CAP
    row_ids = jnp.arange(TOKENS, dtype=jnp.int32)
    source = jnp.zeros((slot_count,), jnp.int32).at[row_dest].set(row_ids)
    filled = jnp.zeros((slot_count,), jnp.float32).at[row_dest].set(1.0)
    group_ids = jnp.arange(group_count, dtype=jnp.int32)
    list_of = lax.optimization_barrier(jnp.sum(jnp.where(deal[None, :] == group_ids[:, None], group_ids[None, :], 0), axis=1)).astype(jnp.int32)
    group_lengths = seq_lengths[list_of]
    segment, position = jax.vmap(segments)(group_lengths)
    checked_layer = jax.checkpoint(group_layer)

    def forward(inputs, weights):
        buffers = (inputs[source] * filled[:, None]).reshape(group_count, GROUP_CAP, D)

        def visit(carry_in, group_item):
            return (carry_in, checked_layer(group_item[0], group_item[1], group_item[2], weights))
        unused, results = lax.scan(visit, jnp.zeros((), jnp.float32), (buffers, segment, position))
        return results.reshape(slot_count, D)[row_dest]
    weights = (w_query.astype(jnp.float32), w_key.astype(jnp.float32), w_value.astype(jnp.float32), w_out.astype(jnp.float32), w_gate.astype(jnp.float32), w_up.astype(jnp.float32), w_down.astype(jnp.float32))
    result, pullback = jax.vjp(forward, tokens.astype(jnp.float32), weights)
    input_grad, weight_grads = pullback(cotangent.astype(jnp.float32))
    return (result.astype(jnp.bfloat16), input_grad.astype(jnp.bfloat16), weight_grads[0], weight_grads[1], weight_grads[2], weight_grads[3], weight_grads[4], weight_grads[5], weight_grads[6])
```

```python
import jax
import jax.numpy as jnp
from jax import lax
from jax.sharding import PartitionSpec as P

HEAD_DIM = 128
GROUP_CAP = 1024
SEQ_SLOTS = 4

norm_eps = 1e-05
rope_base = 10000.0
bf16 = jnp.bfloat16
f32 = jnp.float32


def matmul(left, right):
    return jnp.dot(left, right, preferred_element_type=f32)


def times_transposed(left, right):
    return lax.dot_general(
        left, right, (((1,), (1,)), ((), ())), preferred_element_type=f32
    )


def transposed_times(left, right):
    return lax.dot_general(
        left, right, (((0,), (0,)), ((), ())), preferred_element_type=f32
    )


def norm_parts(values_in):
    row_mean = jnp.mean(values_in, axis=-1, keepdims=True)
    centered = values_in - row_mean
    variance = jnp.mean(centered * centered, axis=-1, keepdims=True)
    inverse = lax.rsqrt(variance + norm_eps)
    return centered * inverse, inverse


def norm_back(values_in, grad_in):
    unit_rows, inverse = norm_parts(values_in)
    return inverse * (
        grad_in
        - jnp.mean(grad_in, axis=-1, keepdims=True)
        - unit_rows * jnp.mean(grad_in * unit_rows, axis=-1, keepdims=True)
    )


def rope_tables(position, head_dim):
    half_dim = head_dim // 2
    frequency = rope_base ** (-(jnp.arange(half_dim, dtype=f32) * 2.0) / head_dim)
    angles = position.astype(f32)[:, None] * frequency[None, :]
    return (jnp.cos(angles), jnp.sin(angles))


def rotate(values_in, cosine, sine_table):
    half_dim = values_in.shape[-1] // 2
    first_half = values_in[..., :half_dim]
    second_half = values_in[..., half_dim:]
    cos_rows = cosine[:, None, :]
    sin_rows = sine_table[:, None, :]
    return jnp.concatenate(
        [
            first_half * cos_rows - second_half * sin_rows,
            second_half * cos_rows + first_half * sin_rows,
        ],
        axis=-1,
    )


def rotate_back(grad_in, cosine, sine_table):
    return rotate(grad_in, cosine, -sine_table)


def segments(lengths):
    row_index = jnp.arange(GROUP_CAP, dtype=jnp.int32)
    slot_ids = jnp.arange(SEQ_SLOTS, dtype=jnp.int32)
    ends = jnp.sum(
        jnp.where(slot_ids[:, None] <= slot_ids[None, :], lengths[:, None], 0), axis=0
    )
    passed = row_index[:, None] >= ends[None, :]
    segment = jnp.sum(passed.astype(jnp.int32), axis=1)
    begin_row = jnp.max(jnp.where(passed, ends[None, :], 0), axis=1)
    return (segment, row_index - begin_row)


def chain_gather(block, axis, size):
    me = lax.axis_index(axis)
    from_low, from_high = [block], [block]
    for step in range(1, size):
        up = [(i, i + 1) for i in range(step - 1, size - 1)]
        down = [(i, i - 1) for i in range(size - step, 0, -1)]
        from_low.append(lax.ppermute(from_low[-1], axis, up))
        from_high.append(lax.ppermute(from_high[-1], axis, down))
    whole = []
    for owner in range(size):
        piece = block
        for step in range(1, size):
            if owner + step < size:
                piece = jnp.where(me == owner + step, from_low[step], piece)
            if owner - step >= 0:
                piece = jnp.where(me == owner - step, from_high[step], piece)
        whole.append(piece)
    return whole


def direct_scatter(pieces_of, axis, size):
    me = lax.axis_index(axis)
    total = None
    order = sorted(range(1, size), key=lambda step: -min(step, size - step))
    for step in order:
        term = pieces_of(lax.rem(me + step, size)).astype(bf16)
        came = lax.ppermute(term, axis, [(i, (i + step) % size) for i in range(size)])
        total = came.astype(f32) if total is None else total + came.astype(f32)
    return total + pieces_of(me)


def on_device(
    tokens,
    cotangent,
    w_query,
    w_key,
    w_value,
    w_out,
    w_gate,
    w_up,
    w_down,
    seq_lengths,
    deal,
    row_dest,
):
    groups = lax.axis_size("fsdp")
    shards = lax.axis_size("tp")
    own_group = lax.axis_index("fsdp")
    own_shard = lax.axis_index("tp")
    capacity = GROUP_CAP
    per_pair = capacity // groups
    quarter = capacity // shards
    head_dim = HEAD_DIM
    given = tokens.shape[0]
    width = tokens.shape[1]
    model = width * shards

    full_qkv = lax.all_gather(
        jnp.concatenate([w_query, w_key, w_value], axis=1), "fsdp", axis=0, tiled=True
    )
    out_rows = jnp.stack(chain_gather(w_out, "tp", shards))
    full_out = lax.all_gather(out_rows, "fsdp", axis=1, tiled=True).reshape(model, model)
    full_gate, full_up, full_down = lax.all_gather(
        jnp.stack([w_gate, w_up, w_down]), "fsdp", axis=1, tiled=True
    )

    target = row_dest // capacity
    within = row_dest - target * capacity
    given_index = jnp.arange(given, dtype=jnp.int32)
    earlier = (target[:, None] == target[None, :]) & (
        given_index[None, :] < given_index[:, None]
    )
    slot_of = target * per_pair + jnp.sum(earlier.astype(jnp.int32), axis=1)
    slots = jnp.arange(capacity, dtype=jnp.int32)
    deal_hit = slots[:, None] == slot_of[None, :]
    deal_out = deal_hit.astype(bf16)
    send_place = jnp.sum(jnp.where(deal_hit, within[None, :] + 1, 0), axis=1) - 1
    recv_place = lax.all_to_all(send_place, "fsdp", split_axis=0, concat_axis=0, tiled=True)
    place_in = (slots[:, None] == recv_place[None, :]).astype(bf16)

    def to_group(rows):
        sent = matmul(deal_out, rows).astype(bf16)
        came = lax.all_to_all(sent, "fsdp", split_axis=0, concat_axis=0, tiled=True)
        return matmul(place_in, came).astype(bf16)

    def to_home(rows):
        sent = transposed_times(place_in, rows).astype(bf16)
        came = lax.all_to_all(sent, "fsdp", split_axis=0, concat_axis=0, tiled=True)
        return transposed_times(deal_out, came).astype(bf16)

    buffer_rows = to_group(tokens)
    buffer_grads = to_group(cotangent)
    full_rows = jnp.concatenate(chain_gather(buffer_rows, "tp", shards), axis=1)

    list_index = jnp.sum(jnp.where(deal == own_group, jnp.arange(groups, dtype=jnp.int32), 0))
    lengths = lax.dynamic_index_in_dim(seq_lengths, list_index, 0, keepdims=False)
    segment, position = segments(lengths)
    row_start = own_shard * quarter

    normed_one = norm_parts(full_rows.astype(f32))[0].astype(bf16)
    cosine, sine_table = rope_tables(position, head_dim)
    local_width = w_query.shape[1]
    local_heads = local_width // head_dim
    qkv = matmul(normed_one, full_qkv)
    query_pre = qkv[:, :local_width].reshape(capacity, local_heads, head_dim)
    key_pre = qkv[:, local_width : 2 * local_width].reshape(capacity, local_heads, head_dim)
    value_rows = qkv[:, 2 * local_width :].astype(bf16).reshape(capacity, local_heads, head_dim)
    queries = rotate(query_pre, cosine, sine_table).astype(bf16)
    key_rows = rotate(key_pre, cosine, sine_table).astype(bf16)
    block_rows = min(512, capacity)
    score_scale = head_dim ** (-0.5)
    row_index = jnp.arange(capacity, dtype=jnp.int32)
    outputs = []
    log_parts = []
    for row_first in range(0, capacity, block_rows):
        q_rows = queries[row_first : row_first + block_rows]
        allowed = (segment[row_first : row_first + block_rows, None] == segment[None, :]) & (
            row_index[None, :] <= row_index[row_first : row_first + block_rows, None]
        )
        scores = (
            jnp.einsum("qhd,khd->hqk", q_rows, key_rows, preferred_element_type=f32)
            * score_scale
        )
        scores = jnp.where(allowed[None], scores, -1e30)
        row_max = jnp.max(scores, axis=-1, keepdims=True)
        exponent = jnp.exp(scores - row_max)
        row_total = jnp.sum(exponent, axis=-1, keepdims=True)
        prob_low = (exponent / row_total).astype(bf16)
        outputs.append(
            jnp.einsum(
                "hqk,khd->qhd", prob_low, value_rows, preferred_element_type=f32
            ).astype(bf16)
        )
        log_parts.append(row_max + jnp.log(row_total))
    attended = jnp.concatenate(outputs, axis=0).reshape(capacity, local_width)

    full_attended = jnp.concatenate(chain_gather(attended, "tp", shards), axis=1)
    full_grads = jnp.concatenate(chain_gather(buffer_grads, "tp", shards), axis=1)
    hidden = full_rows.astype(f32) + matmul(full_attended, full_out)
    normed_two = norm_parts(hidden)[0].astype(bf16)
    gate_pre = matmul(normed_two, full_gate)
    up_pre = matmul(normed_two, full_up)
    activated = (jax.nn.silu(gate_pre) * up_pre).astype(bf16)
    down_grad = times_transposed(full_grads, full_down)
    sigmoid_gate = jax.nn.sigmoid(gate_pre)
    gate_grad = (
        down_grad * up_pre * sigmoid_gate * (1.0 + gate_pre * (1.0 - sigmoid_gate))
    ).astype(bf16)
    up_grad = (down_grad * gate_pre * sigmoid_gate).astype(bf16)

    normed_two_grad = (
        times_transposed(gate_grad, full_gate) + times_transposed(up_grad, full_up)
    ).astype(bf16)
    two_grad_here = direct_scatter(
        lambda owner: lax.dynamic_slice_in_dim(
            normed_two_grad, owner * quarter, quarter, 0
        ).astype(f32),
        "tp",
        shards,
    )

    def own_rows(rows):
        return lax.dynamic_slice_in_dim(rows, row_start, quarter, 0)

    hidden_grad = own_rows(full_grads).astype(f32) + norm_back(own_rows(hidden), two_grad_here)
    hidden_grad_low = hidden_grad.astype(bf16)
    att_grad_here = times_transposed(hidden_grad_low, full_out).astype(bf16)
    attended_grad = lax.all_to_all(
        att_grad_here, "tp", split_axis=1, concat_axis=0, tiled=True
    ).reshape(capacity, local_heads, head_dim)

    grad_mlp = jnp.stack(
        [
            transposed_times(normed_two, gate_grad).astype(bf16),
            transposed_times(normed_two, up_grad).astype(bf16),
            transposed_times(activated, full_grads).astype(bf16),
        ]
    )
    sum_gate, sum_up, sum_down = lax.psum_scatter(
        grad_mlp, "fsdp", scatter_dimension=1, tiled=True
    ).astype(f32)

    mlp_part = matmul(activated, full_down).astype(bf16)

    def own_features(rows, owner):
        return lax.dynamic_slice_in_dim(rows, owner * width, width, 1)

    mlp_here = direct_scatter(
        lambda owner: own_features(mlp_part, owner).astype(f32), "tp", shards
    )
    output_here = (own_features(hidden, own_shard) + mlp_here).astype(bf16)
    output = to_home(output_here)

    grad_out = transposed_times(own_rows(full_attended), hidden_grad_low).astype(bf16)
    hidden_grad_features = lax.all_to_all(
        hidden_grad_low, "tp", split_axis=1, concat_axis=0, tiled=True
    )

    query_parts = []
    key_sum = jnp.zeros((capacity, local_heads, head_dim), f32)
    value_sum = jnp.zeros((capacity, local_heads, head_dim), f32)
    for part_index, row_first in enumerate(range(0, capacity, block_rows)):
        q_rows = queries[row_first : row_first + block_rows]
        grad_rows = attended_grad[row_first : row_first + block_rows]
        allowed = (segment[row_first : row_first + block_rows, None] == segment[None, :]) & (
            row_index[None, :] <= row_index[row_first : row_first + block_rows, None]
        )
        scores = (
            jnp.einsum("qhd,khd->hqk", q_rows, key_rows, preferred_element_type=f32)
            * score_scale
        )
        probs = jnp.where(allowed[None], jnp.exp(scores - log_parts[part_index]), 0.0)
        prob_low = probs.astype(bf16)
        prob_grad = jnp.einsum("qhd,khd->hqk", grad_rows, value_rows, preferred_element_type=f32)
        row_delta = jnp.sum(prob_grad * probs, axis=-1, keepdims=True)
        score_grad = (probs * (prob_grad - row_delta)).astype(bf16)
        query_parts.append(
            jnp.einsum("hqk,khd->qhd", score_grad, key_rows, preferred_element_type=f32)
            * score_scale
        )
        key_sum = (
            key_sum
            + jnp.einsum("hqk,qhd->khd", score_grad, q_rows, preferred_element_type=f32)
            * score_scale
        )
        value_sum = value_sum + jnp.einsum(
            "hqk,qhd->khd", prob_low, grad_rows, preferred_element_type=f32
        )
    query_grad = rotate_back(jnp.concatenate(query_parts, axis=0), cosine, sine_table)
    key_grad = rotate_back(key_sum, cosine, sine_table)
    qkv_grad = jnp.concatenate(
        [
            part.astype(bf16).reshape(capacity, local_width)
            for part in (query_grad, key_grad, value_sum)
        ],
        axis=1,
    )

    normed_one_grad = times_transposed(qkv_grad, full_qkv)
    unit_one, inverse_one = norm_parts(full_rows.astype(f32))
    row_sums = jnp.stack(
        [jnp.sum(normed_one_grad, axis=1), jnp.sum(normed_one_grad * unit_one, axis=1)]
    )
    sums_here = row_sums
    for step in range(1, shards):
        sums_here = sums_here + lax.ppermute(
            row_sums, "tp", [(i, (i + step) % shards) for i in range(shards)]
        )
    one_grad_low = normed_one_grad.astype(bf16)
    one_grad_here = direct_scatter(
        lambda owner: own_features(one_grad_low, owner).astype(f32), "tp", shards
    )
    means = sums_here / model
    back_here = inverse_one * (
        one_grad_here
        - means[0][:, None]
        - own_features(unit_one, own_shard) * means[1][:, None]
    )
    input_grad = to_home((hidden_grad_features.astype(f32) + back_here).astype(bf16))

    grad_qkv = transposed_times(normed_one, qkv_grad).astype(bf16)
    sum_qkv = lax.psum_scatter(grad_qkv, "fsdp", scatter_dimension=0, tiled=True)
    out_part = lax.psum_scatter(
        grad_out.reshape(shards, model // shards, model), "fsdp", scatter_dimension=1, tiled=True
    )
    sum_out = direct_scatter(
        lambda owner: lax.dynamic_index_in_dim(out_part, owner, 0, keepdims=False).astype(f32),
        "tp",
        shards,
    )
    sum_qkv = sum_qkv.astype(f32)
    return (
        output,
        input_grad,
        sum_qkv[:, :local_width],
        sum_qkv[:, local_width : 2 * local_width],
        sum_qkv[:, 2 * local_width :],
        sum_out,
        sum_gate,
        sum_up,
        sum_down,
    )


def solution(mesh):
    in_specs = (
        P("fsdp", "tp"),
        P("fsdp", "tp"),
        P("fsdp", "tp"),
        P("fsdp", "tp"),
        P("fsdp", "tp"),
        P(("tp", "fsdp"), None),
        P("fsdp", "tp"),
        P("fsdp", "tp"),
        P(("tp", "fsdp"), None),
        P(),
        P(),
        P("fsdp"),
    )
    out_specs = (
        P("fsdp", "tp"),
        P("fsdp", "tp"),
        P("fsdp", "tp"),
        P("fsdp", "tp"),
        P("fsdp", "tp"),
        P(("tp", "fsdp"), None),
        P("fsdp", "tp"),
        P("fsdp", "tp"),
        P(("tp", "fsdp"), None),
    )
    return jax.shard_map(
        on_device, mesh=mesh, in_specs=in_specs, out_specs=out_specs, check_vma=False
    )
```

```python
import jax
import jax.numpy as jnp
from jax import lax
from jax.experimental import pallas as pl
from jax.experimental.pallas import tpu as pltpu
from jax.sharding import PartitionSpec as P

HEAD_DIM = 128
GROUP_CAP = 1024
SEQ_SLOTS = 4

norm_eps = 1e-05
rope_base = 10000.0
bf16 = jnp.bfloat16
f32 = jnp.float32


def matmul(left, right):
    return jnp.dot(left, right, preferred_element_type=f32)


def times_transposed(left, right):
    return lax.dot_general(
        left, right, (((1,), (1,)), ((), ())), preferred_element_type=f32
    )


def transposed_times(left, right):
    return lax.dot_general(
        left, right, (((0,), (0,)), ((), ())), preferred_element_type=f32
    )


def norm_parts(values_in):
    row_mean = jnp.mean(values_in, axis=-1, keepdims=True)
    centered = values_in - row_mean
    variance = jnp.mean(centered * centered, axis=-1, keepdims=True)
    inverse = lax.rsqrt(variance + norm_eps)
    return centered * inverse, inverse


def rope_tables(position, head_dim):
    half_dim = head_dim // 2
    frequency = rope_base ** (-(jnp.arange(half_dim, dtype=f32) * 2.0) / head_dim)
    angles = position.astype(f32)[:, None] * frequency[None, :]
    cosine, sine = jnp.cos(angles), jnp.sin(angles)
    return (
        jnp.concatenate([cosine, cosine], axis=1),
        jnp.concatenate([-sine, sine], axis=1),
    )


def segments(lengths):
    row_index = jnp.arange(GROUP_CAP, dtype=jnp.int32)
    slot_ids = jnp.arange(SEQ_SLOTS, dtype=jnp.int32)
    ends = jnp.sum(
        jnp.where(slot_ids[:, None] <= slot_ids[None, :], lengths[:, None], 0), axis=0
    )
    passed = row_index[:, None] >= ends[None, :]
    segment = jnp.sum(passed.astype(jnp.int32), axis=1)
    begin_row = jnp.max(jnp.where(passed, ends[None, :], 0), axis=1)
    return (segment, row_index - begin_row)


VMEM_LIMIT = 58 * 1024 * 1024
BLOCK = 256


def params():
    return pltpu.CompilerParams(vmem_limit_bytes=VMEM_LIMIT)


def cost(flops, read, transcendentals=0):
    return pl.CostEstimate(
        flops=int(flops), bytes_accessed=int(read), transcendentals=int(transcendentals)
    )


def half_turn(values_in):
    return pltpu.roll(values_in, HEAD_DIM // 2, 1)


def qkv_kernel(rows_ref, weight_ref, cos_ref, sin_ref, out_ref):
    for first in range(0, rows_ref.shape[0], BLOCK):
        rows = pl.ds(first, BLOCK)
        pre = matmul(rows_ref[rows, :], weight_ref[...])
        for part in range(3):
            piece = pre[:, part * HEAD_DIM : (part + 1) * HEAD_DIM]
            if part < 2:
                piece = piece * cos_ref[rows, :] + half_turn(piece) * sin_ref[rows, :]
            out_ref[rows, part * HEAD_DIM : (part + 1) * HEAD_DIM] = piece.astype(bf16)


def project_qkv(rows, weight, cosine, sine):
    count, model = rows.shape
    columns = weight.shape[1]
    step = 3 * HEAD_DIM
    whole = lambda h: (0, 0)
    return pl.pallas_call(
        qkv_kernel,
        grid=(columns // step,),
        in_specs=[
            pl.BlockSpec((count, model), whole),
            pl.BlockSpec((model, step), lambda h: (0, h)),
            pl.BlockSpec((count, HEAD_DIM), whole),
            pl.BlockSpec((count, HEAD_DIM), whole),
        ],
        out_specs=pl.BlockSpec((count, step), lambda h: (0, h)),
        out_shape=jax.ShapeDtypeStruct((count, columns), bf16),
        compiler_params=params(),
        cost_estimate=cost(2 * count * model * columns, 2 * model * (count + columns)),
        name="qkv",
    )(rows, weight, cosine, sine)


def masked_softmax(q_rows, k_rows, seg_column, seg_row, row_first):
    scores = times_transposed(q_rows, k_rows) * HEAD_DIM ** (-0.5)
    row = lax.broadcasted_iota(jnp.int32, scores.shape, 0) + row_first
    column = lax.broadcasted_iota(jnp.int32, scores.shape, 1)
    allowed = (seg_column == seg_row) & (column <= row)
    scores = jnp.where(allowed, scores, -1e30)
    exponent = jnp.exp(scores - jnp.max(scores, axis=-1, keepdims=True))
    return exponent * (1.0 / jnp.sum(exponent, axis=-1, keepdims=True))


def attend_kernel(q_ref, k_ref, v_ref, column_ref, row_ref, out_ref):
    block = pl.program_id(1)
    for index in range(k_ref.shape[0] // BLOCK):

        @pl.when(block == index)
        def _(index=index):
            seen = (index + 1) * BLOCK
            prob = masked_softmax(
                q_ref[...], k_ref[:seen, :], column_ref[...], row_ref[:, :seen], index * BLOCK
            )
            out_ref[...] = matmul(prob.astype(bf16), v_ref[:seen, :]).astype(bf16)


def attend(qkv, segment):
    count = qkv.shape[0]
    heads = qkv.shape[1] // (3 * HEAD_DIM)
    return pl.pallas_call(
        attend_kernel,
        grid=(heads, count // BLOCK),
        in_specs=[
            pl.BlockSpec((BLOCK, HEAD_DIM), lambda h, i: (i, 3 * h)),
            pl.BlockSpec((count, HEAD_DIM), lambda h, i: (0, 3 * h + 1)),
            pl.BlockSpec((count, HEAD_DIM), lambda h, i: (0, 3 * h + 2)),
            pl.BlockSpec((BLOCK, 1), lambda h, i: (i, 0)),
            pl.BlockSpec((1, count), lambda h, i: (0, 0)),
        ],
        out_specs=pl.BlockSpec((BLOCK, HEAD_DIM), lambda h, i: (i, h)),
        out_shape=jax.ShapeDtypeStruct((count, heads * HEAD_DIM), bf16),
        compiler_params=params(),
        cost_estimate=cost(
            4 * heads * count * count * HEAD_DIM, 8 * count * heads * HEAD_DIM, heads * count * count
        ),
        name="attend",
    )(qkv, qkv, qkv, segment[:, None], segment[None, :])


def attend_back_kernel(
    q_ref, k_ref, v_ref, grad_ref, column_ref, row_ref, cos_ref, sin_ref, out_ref, total
):
    block = pl.program_id(1)
    scale = HEAD_DIM ** (-0.5)
    blocks = k_ref.shape[0] // BLOCK

    @pl.when(block == 0)
    def _():
        total[...] = jnp.zeros_like(total)

    for index in range(blocks):

        @pl.when(block == index)
        def _(index=index):
            seen = (index + 1) * BLOCK
            q_rows, k_rows, grad = q_ref[...], k_ref[:seen, :], grad_ref[...]
            prob = masked_softmax(
                q_rows, k_rows, column_ref[...], row_ref[:, :seen], index * BLOCK
            )
            prob_grad = times_transposed(grad, v_ref[:seen, :])
            delta = jnp.sum(prob_grad * prob, axis=-1, keepdims=True)
            score_grad = (prob * (prob_grad - delta)).astype(bf16)
            total[0, index * BLOCK : seen, :] = matmul(score_grad, k_rows) * scale
            total[1, :seen, :] += transposed_times(score_grad, q_rows) * scale
            total[2, :seen, :] += transposed_times(prob.astype(bf16), grad)

    @pl.when(block == blocks - 1)
    def _():
        for part in range(3):
            piece = total[part]
            if part < 2:
                piece = piece * cos_ref[...] - half_turn(piece) * sin_ref[...]
            out_ref[:, part * HEAD_DIM : (part + 1) * HEAD_DIM] = piece.astype(bf16)


def attend_back(qkv, grad, segment, cosine, sine):
    count = qkv.shape[0]
    heads = qkv.shape[1] // (3 * HEAD_DIM)
    return pl.pallas_call(
        attend_back_kernel,
        grid=(heads, count // BLOCK),
        in_specs=[
            pl.BlockSpec((BLOCK, HEAD_DIM), lambda h, i: (i, 3 * h)),
            pl.BlockSpec((count, HEAD_DIM), lambda h, i: (0, 3 * h + 1)),
            pl.BlockSpec((count, HEAD_DIM), lambda h, i: (0, 3 * h + 2)),
            pl.BlockSpec((BLOCK, HEAD_DIM), lambda h, i: (i, h)),
            pl.BlockSpec((BLOCK, 1), lambda h, i: (i, 0)),
            pl.BlockSpec((1, count), lambda h, i: (0, 0)),
            pl.BlockSpec((count, HEAD_DIM), lambda h, i: (0, 0)),
            pl.BlockSpec((count, HEAD_DIM), lambda h, i: (0, 0)),
        ],
        out_specs=pl.BlockSpec((count, 3 * HEAD_DIM), lambda h, i: (0, h)),
        out_shape=jax.ShapeDtypeStruct(qkv.shape, bf16),
        scratch_shapes=[pltpu.VMEM((3, count, HEAD_DIM), f32)],
        compiler_params=params(),
        cost_estimate=cost(
            10 * heads * count * count * HEAD_DIM, 14 * count * heads * HEAD_DIM, heads * count * count
        ),
        name="attend_back",
    )(qkv, qkv, qkv, grad, segment[:, None], segment[None, :], cosine, sine)


def hidden_kernel(att_ref, weight_ref, rows_ref, hidden_ref, normed_ref):
    hidden = rows_ref[...].astype(f32) + matmul(att_ref[...], weight_ref[...])
    hidden_ref[...] = hidden
    normed_ref[...] = norm_parts(hidden)[0].astype(bf16)


def hidden_and_norm(attended, weight, rows):
    count, model = rows.shape
    here = lambda i: (i, 0)
    return pl.pallas_call(
        hidden_kernel,
        grid=(count // BLOCK,),
        in_specs=[
            pl.BlockSpec((BLOCK, model), here),
            pl.BlockSpec((model, model), lambda i: (0, 0)),
            pl.BlockSpec((BLOCK, model), here),
        ],
        out_specs=[pl.BlockSpec((BLOCK, model), here)] * 2,
        out_shape=[
            jax.ShapeDtypeStruct((count, model), f32),
            jax.ShapeDtypeStruct((count, model), bf16),
        ],
        compiler_params=params(),
        cost_estimate=cost(2 * count * model * model, 2 * model * model + 10 * count * model),
        name="hidden",
    )(attended, weight, rows)


def up_kernel(rows_ref, gate_ref, up_ref, gate_out, up_out, act_ref):
    for first in range(0, rows_ref.shape[0], BLOCK):
        rows = pl.ds(first, BLOCK)
        gate = matmul(rows_ref[rows, :], gate_ref[0])
        up = matmul(rows_ref[rows, :], up_ref[0])
        gate_out[rows, :] = gate
        up_out[rows, :] = up
        act_ref[rows, :] = (gate / (1.0 + jnp.exp(-gate)) * up).astype(bf16)


def mlp_up(rows, weights):
    count, model = rows.shape
    hidden_units = weights.shape[2]
    wide = jax.ShapeDtypeStruct((count, hidden_units), f32)
    return pl.pallas_call(
        up_kernel,
        grid=(hidden_units // BLOCK,),
        in_specs=[
            pl.BlockSpec((count, model), lambda j: (0, 0)),
            pl.BlockSpec((1, model, BLOCK), lambda j: (0, 0, j)),
            pl.BlockSpec((1, model, BLOCK), lambda j: (1, 0, j)),
        ],
        out_specs=[pl.BlockSpec((count, BLOCK), lambda j: (0, j))] * 3,
        out_shape=[wide, wide, jax.ShapeDtypeStruct((count, hidden_units), bf16)],
        compiler_params=params(),
        cost_estimate=cost(
            4 * count * model * hidden_units,
            4 * model * hidden_units + 2 * count * model + 10 * count * hidden_units,
            count * hidden_units,
        ),
        name="mlp_up",
    )(rows, weights, weights)


def down_back_kernel(grad_ref, down_ref, gate_in, up_in, dgate_ref, dup_ref):
    for first in range(0, grad_ref.shape[0], BLOCK):
        rows = pl.ds(first, BLOCK)
        down = times_transposed(grad_ref[rows, :], down_ref[0])
        gate = gate_in[rows, :]
        sigmoid = 1.0 / (1.0 + jnp.exp(-gate))
        silu = gate * sigmoid
        dgate_ref[rows, :] = (
            down * up_in[rows, :] * (sigmoid + silu * (1.0 - sigmoid))
        ).astype(bf16)
        dup_ref[rows, :] = (down * silu).astype(bf16)


def mlp_down_back(grads, weights, gate, up):
    count, model = grads.shape
    hidden_units = weights.shape[2]
    part = pl.BlockSpec((count, BLOCK), lambda j: (0, j))
    out = jax.ShapeDtypeStruct((count, hidden_units), bf16)
    return pl.pallas_call(
        down_back_kernel,
        grid=(hidden_units // BLOCK,),
        in_specs=[
            pl.BlockSpec((count, model), lambda j: (0, 0)),
            pl.BlockSpec((1, BLOCK, model), lambda j: (2, j, 0)),
            part,
            part,
        ],
        out_specs=[part] * 2,
        out_shape=[out] * 2,
        compiler_params=params(),
        cost_estimate=cost(
            2 * count * model * hidden_units,
            2 * model * hidden_units + 2 * count * model + 12 * count * hidden_units,
            count * hidden_units,
        ),
        name="mlp_down_back",
    )(grads, weights, gate, up)


def norm_back(values_in, grad_in):
    unit_rows, inverse = norm_parts(values_in)
    return inverse * (
        grad_in
        - jnp.mean(grad_in, axis=-1, keepdims=True)
        - unit_rows * jnp.mean(grad_in * unit_rows, axis=-1, keepdims=True)
    )


def two_grad_kernel(order_ref, *refs):
    *row_refs, gate_ref, up_ref, out_ref, total = refs
    step = pl.program_id(0)
    columns = pl.ds(pl.multiple_of(step * BLOCK, BLOCK), BLOCK)
    pieces = out_ref.shape[0]
    for piece in range(pieces):
        total[piece, :, columns] = times_transposed(
            row_refs[3 * piece][...], gate_ref[0]
        ) + times_transposed(row_refs[3 * piece + 1][...], up_ref[0])

    @pl.when(step == pl.num_programs(0) - 1)
    def _():
        for piece in range(pieces):
            out_ref[piece] = norm_back(row_refs[3 * piece + 2][...], total[piece]).astype(bf16)


def two_grad_pieces(order, dgate, dup, weights, hidden, quarter):
    pieces = order.shape[0]
    hidden_units = dgate.shape[1]
    model = weights.shape[1]
    rows = []
    for p in range(pieces):
        here = lambda j, order, p=p: (order[p], 0)
        rows += [pl.BlockSpec((quarter, hidden_units), here)] * 2
        rows += [pl.BlockSpec((quarter, model), here, pipeline_mode=pl.Buffered(1))]
    return pl.pallas_call(
        two_grad_kernel,
        grid_spec=pltpu.PrefetchScalarGridSpec(
            num_scalar_prefetch=1,
            grid=(model // BLOCK,),
            in_specs=[
                *rows,
                pl.BlockSpec((1, BLOCK, hidden_units), lambda j, order: (0, j, 0)),
                pl.BlockSpec((1, BLOCK, hidden_units), lambda j, order: (1, j, 0)),
            ],
            out_specs=pl.BlockSpec((pieces, quarter, model), lambda j, order: (0, 0, 0)),
            scratch_shapes=[pltpu.VMEM((pieces, quarter, model), f32)],
        ),
        out_shape=jax.ShapeDtypeStruct((pieces, quarter, model), bf16),
        compiler_params=params(),
        cost_estimate=cost(
            4 * pieces * quarter * model * hidden_units, 4 * model * hidden_units
        ),
        name="two_grad",
    )(order, *([dgate, dup, hidden] * pieces), weights, weights)


def one_grad_kernel(place_ref, grad_ref, weight_ref, rows_ref, out_ref):
    grad = norm_back(
        rows_ref[...].astype(f32), times_transposed(grad_ref[...], weight_ref[...])
    ).astype(bf16)
    width = out_ref.shape[2]
    for piece in range(out_ref.shape[0]):
        out_ref[place_ref[piece]] = grad[:, piece * width : (piece + 1) * width]


def one_grad_pieces(place, qkv_grad, weight, rows):
    count, columns = qkv_grad.shape
    pieces = place.shape[0]
    model = rows.shape[1]
    here = lambda i, place: (i, 0)
    return pl.pallas_call(
        one_grad_kernel,
        grid_spec=pltpu.PrefetchScalarGridSpec(
            num_scalar_prefetch=1,
            grid=(count // BLOCK,),
            in_specs=[
                pl.BlockSpec((BLOCK, columns), here),
                pl.BlockSpec((model, columns), lambda i, place: (0, 0)),
                pl.BlockSpec((BLOCK, model), here),
            ],
            out_specs=pl.BlockSpec(
                (pieces, BLOCK, model // pieces), lambda i, place: (0, i, 0)
            ),
        ),
        out_shape=jax.ShapeDtypeStruct((pieces, count, model // pieces), bf16),
        compiler_params=params(),
        cost_estimate=cost(
            2 * count * model * columns, 2 * columns * model + 6 * count * columns
        ),
        name="one_grad",
    )(place, qkv_grad, weight, rows)


def att_grads_kernel(normed_ref, qkv_ref, att_ref, hidden_ref, out_ref):
    owner = pl.program_id(0)
    columns = qkv_ref.shape[1]
    out_ref[0, :, :columns] = transposed_times(normed_ref[...], qkv_ref[...]).astype(bf16)
    model = hidden_ref.shape[1]
    rest = model - columns
    pieces = model // rest
    height = out_ref.shape[1] // pieces
    per_tile = HEAD_DIM // height
    product = transposed_times(att_ref[...], hidden_ref[...]).astype(bf16)
    for place in range(per_tile):

        @pl.when(lax.rem(owner, per_tile) == place)
        def _(place=place):
            for piece in range(pieces):
                out_ref[0, piece * height : (piece + 1) * height, columns:] = product[
                    place * height : (place + 1) * height, piece * rest : (piece + 1) * rest
                ]


def att_grads(normed, qkv_grad, attended, hidden_grad, groups):
    count, model = normed.shape
    columns = qkv_grad.shape[1]
    local = attended.shape[1]
    tall = model // groups
    per_tile = HEAD_DIM // (local // groups)
    once = pl.Buffered(1)
    whole = lambda i: (0, 0)
    if tall % HEAD_DIM == 0:
        normed_spec = pl.BlockSpec((count, tall), lambda i: (0, i))
        operand = normed
    else:
        normed_spec = pl.BlockSpec((None, count, tall), lambda i: (i, 0, 0))
        operand = normed.reshape(count, groups, tall).swapaxes(0, 1)
    return pl.pallas_call(
        att_grads_kernel,
        grid=(groups,),
        in_specs=[
            normed_spec,
            pl.BlockSpec((count, columns), whole, pipeline_mode=once),
            pl.BlockSpec((count, HEAD_DIM), lambda i: (0, i // per_tile)),
            pl.BlockSpec((count, model), whole, pipeline_mode=once),
        ],
        out_specs=pl.BlockSpec((1, tall, model), lambda i: (i, 0, 0)),
        out_shape=jax.ShapeDtypeStruct((groups, tall, model), bf16),
        compiler_params=params(),
        cost_estimate=cost(
            2 * count * model * columns + 2 * count * groups * HEAD_DIM * model,
            2 * model * model + 4 * count * model + 2 * count * columns,
        ),
        name="att_grads",
    )(operand, qkv_grad, attended, hidden_grad)


def mlp_grads_kernel(left_ref, act_ref, dgate_ref, dup_ref, grad_ref, out_ref):
    which = pl.program_id(0)
    for index, (left, right) in enumerate(
        ((left_ref, dgate_ref), (left_ref, dup_ref), (act_ref, grad_ref))
    ):

        @pl.when(which == index)
        def _(left=left, right=right):
            out_ref[0] = transposed_times(left[...], right[...]).astype(bf16)


def mlp_grads(normed, act, dgate, dup, grads):
    count, model = normed.shape
    hidden_units = act.shape[1]
    whole = lambda w, i: (0, 0)
    once = pl.Buffered(1)
    return pl.pallas_call(
        mlp_grads_kernel,
        grid=(3, model // BLOCK),
        in_specs=[
            pl.BlockSpec((count, BLOCK), lambda w, i: (0, jnp.where(w < 2, i, 0))),
            pl.BlockSpec((count, BLOCK), lambda w, i: (0, jnp.where(w < 2, 0, i))),
            pl.BlockSpec((count, hidden_units), whole, pipeline_mode=once),
            pl.BlockSpec((count, hidden_units), whole, pipeline_mode=once),
            pl.BlockSpec((count, model), whole, pipeline_mode=once),
        ],
        out_specs=pl.BlockSpec((1, BLOCK, hidden_units), lambda w, i: (w, i, 0)),
        out_shape=jax.ShapeDtypeStruct((3, model, hidden_units), bf16),
        compiler_params=params(),
        cost_estimate=cost(
            6 * count * model * hidden_units, 6 * model * hidden_units + 10 * count * model
        ),
        name="mlp_grads",
    )(normed, act, dgate, dup, grads)


def after(value, *others):
    return lax.optimization_barrier((value, *others))[0]


def line_step(block, axis, size, step):
    from_low, from_high = block
    up = [(i, i + 1) for i in range(step - 1, size - 1)]
    down = [(i, i - 1) for i in range(size - step, 0, -1)]
    return lax.ppermute(from_low, axis, up), lax.ppermute(from_high, axis, down)


def line_whole(own, arrived, axis, size):
    me = lax.axis_index(axis)
    whole = []
    for owner in range(size):
        piece = own
        for step in range(1, size):
            if owner + step < size:
                piece = jnp.where(me == owner + step, arrived[step - 1][0], piece)
            if owner - step >= 0:
                piece = jnp.where(me == owner - step, arrived[step - 1][1], piece)
        whole.append(piece)
    return whole


def chain_gather(block, axis, size, begun=None):
    arrived = list(begun or [])
    for step in range(len(arrived) + 1, size):
        arrived.append(line_step(arrived[-1] if arrived else (block, block), axis, size, step))
    return line_whole(block, arrived, axis, size)


def far_first(size):
    return sorted(range(1, size), key=lambda step: -min(step, size - step))


def sent_on(term, axis, size, step):
    return lax.ppermute(term, axis, [(i, (i + step) % size) for i in range(size)])


def added(own, came):
    for piece in came:
        own = own + piece.astype(f32)
    return own


def on_device(
    tokens,
    cotangent,
    w_query,
    w_key,
    w_value,
    w_out,
    w_gate,
    w_up,
    w_down,
    seq_lengths,
    deal,
    row_dest,
):
    groups = lax.axis_size("fsdp")
    shards = lax.axis_size("tp")
    own_group = lax.axis_index("fsdp")
    own_shard = lax.axis_index("tp")
    capacity = GROUP_CAP
    per_pair = capacity // groups
    quarter = capacity // shards
    head_dim = HEAD_DIM
    given, width = tokens.shape
    model = width * shards
    local_width = w_query.shape[1]
    heads = local_width // head_dim
    shard_rows = w_query.shape[0]

    steps = far_first(shards)
    order = jnp.stack([lax.rem(own_shard + step, shards) for step in (*steps, 0)])
    place_of = [0] * shards
    for index, step in enumerate((*steps, 0)):
        place_of[step] = index
    place = jnp.stack(
        [
            sum(
                jnp.where(lax.rem(own_shard + step, shards) == j, place_of[step], 0)
                for step in range(shards)
            )
            for j in range(shards)
        ]
    )

    target = row_dest // capacity
    within = row_dest - target * capacity
    given_index = jnp.arange(given, dtype=jnp.int32)
    earlier = (target[:, None] == target[None, :]) & (
        given_index[None, :] < given_index[:, None]
    )
    slot_of = target * per_pair + jnp.sum(earlier.astype(jnp.int32), axis=1)
    slots = jnp.arange(capacity, dtype=jnp.int32)
    deal_hit = slots[:, None] == slot_of[None, :]
    deal_out = deal_hit.astype(bf16)
    place_high, place_low = (within + 1) // 32, (within + 1) % 32
    lane = jnp.arange(HEAD_DIM, dtype=jnp.int32)[None, :]
    place_columns = jnp.where(
        lane == 0, place_high[:, None], jnp.where(lane == 1, place_low[:, None], 0)
    ).astype(bf16)

    def over_fsdp(rows):
        return lax.all_to_all(rows, "fsdp", split_axis=0, concat_axis=0, tiled=True)

    def to_home(rows):
        sent = transposed_times(place_in, rows).astype(bf16)
        return transposed_times(deal_out, over_fsdp(sent)).astype(bf16)

    sent_rows = matmul(deal_out, jnp.concatenate([tokens, place_columns], axis=1)).astype(bf16)
    sent_grads = matmul(deal_out, cotangent).astype(bf16)

    qkv_shard = jnp.stack(
        [w.reshape(shard_rows, heads, head_dim) for w in (w_query, w_key, w_value)], axis=2
    ).reshape(shard_rows, 3 * local_width)
    full_qkv = lax.all_gather(qkv_shard, "fsdp", axis=0, tiled=True)
    out_came = [sent_on(w_out, "tp", shards, step) for step in range(1, shards)]
    came_rows = over_fsdp(sent_rows)
    *out_came, came_rows, sent_grads = lax.optimization_barrier(
        (*out_came, came_rows, sent_grads)
    )
    came_place = came_rows[:, width : width + 2].astype(jnp.int32)
    recv_place = came_place[:, 0] * 32 + came_place[:, 1] - 1
    place_in = (slots[:, None] == recv_place[None, :]).astype(bf16)
    out_came = [w_out] + out_came
    out_rows = []
    for owner in range(shards):
        piece = w_out
        for step in range(1, shards):
            piece = jnp.where(own_shard == (owner + step) % shards, out_came[step], piece)
        out_rows.append(piece)
    out_rows = jnp.stack(out_rows)
    full_out = lax.all_gather(out_rows, "fsdp", axis=1, tiled=True).reshape(model, model)
    full_mlp = lax.all_gather(
        jnp.stack([w_gate, w_up, w_down]), "fsdp", axis=1, tiled=True
    )

    buffer_rows = matmul(place_in, came_rows[:, :width]).astype(bf16)
    buffer_grads = matmul(place_in, over_fsdp(after(sent_grads, buffer_rows))).astype(bf16)
    full_rows = jnp.concatenate(chain_gather(buffer_rows, "tp", shards), axis=1)
    full_rows, first_grads = lax.optimization_barrier((full_rows, buffer_grads))

    list_index = jnp.sum(jnp.where(deal == own_group, jnp.arange(groups, dtype=jnp.int32), 0))
    lengths = lax.dynamic_index_in_dim(seq_lengths, list_index, 0, keepdims=False)
    segment, position = segments(lengths)
    cosine, sine = rope_tables(position, head_dim)

    normed_one = norm_parts(full_rows.astype(f32))[0].astype(bf16)
    grads_begun = line_step((first_grads, first_grads), "tp", shards, 1)
    qkv = project_qkv(normed_one, full_qkv, cosine, sine)
    attended = attend(qkv, segment)
    attended, *grads_begun = lax.optimization_barrier((attended, *grads_begun))
    full_attended = jnp.concatenate(chain_gather(attended, "tp", shards), axis=1)
    *grads_begun, full_attended = lax.optimization_barrier((*grads_begun, full_attended))
    grads_begun = [grads_begun, line_step(grads_begun, "tp", shards, 2)]
    hidden, normed_two = hidden_and_norm(full_attended, full_out, full_rows)
    *grads_begun[1], normed_two = lax.optimization_barrier((*grads_begun[1], normed_two))
    grads_begun.append(line_step(grads_begun[1], "tp", shards, 3))
    gate, up, activated = mlp_up(normed_two, full_mlp)
    *grads_begun[2], activated = lax.optimization_barrier((*grads_begun[2], activated))
    full_grads = jnp.concatenate(
        chain_gather(first_grads, "tp", shards, grads_begun), axis=1
    )

    def rows_of(rows, owner):
        return lax.dynamic_slice_in_dim(rows, owner * quarter, quarter, 0)

    def features_of(rows, owner):
        return lax.dynamic_slice_in_dim(rows, owner * width, width, 1)

    mlp_part = matmul(activated, full_mlp[2]).astype(bf16)
    mlp_terms = [features_of(mlp_part, order[index]) for index in range(shards)]
    full_grads, *mlp_terms = lax.optimization_barrier((full_grads, *mlp_terms))
    mlp_first = sent_on(mlp_terms[0], "tp", shards, steps[0])
    gate_grad, up_grad = mlp_down_back(full_grads, full_mlp, gate, up)
    two_first = two_grad_pieces(order[:1], gate_grad, up_grad, full_mlp, hidden, quarter)
    two_first, mlp_first, up_late = lax.optimization_barrier((two_first, mlp_first, up_grad))
    two_rest = two_grad_pieces(order[1:], gate_grad, up_late, full_mlp, hidden, quarter)
    two_came = [sent_on(two_first[0], "tp", shards, steps[0])] + [
        sent_on(two_rest[index], "tp", shards, step) for index, step in enumerate(steps[1:])
    ]
    grad_mlp = mlp_grads(normed_two, activated, gate_grad, up_grad, full_grads)
    *two_came, grad_mlp = lax.optimization_barrier((*two_came, grad_mlp))
    sum_mlp = lax.psum_scatter(grad_mlp, "fsdp", scatter_dimension=1, tiled=True)

    hidden_grad = added(
        rows_of(full_grads, own_shard).astype(f32) + two_rest[-1].astype(f32), two_came
    )
    hidden_grad_low = hidden_grad.astype(bf16)
    full_hidden_grad = jnp.concatenate(
        chain_gather(hidden_grad_low, "tp", shards), axis=0
    )
    own_out = lax.dynamic_slice_in_dim(full_out, own_shard * local_width, local_width, 0)
    attended_grad = times_transposed(full_hidden_grad, own_out).astype(bf16)

    *mlp_terms, full_hidden_grad = lax.optimization_barrier((*mlp_terms, full_hidden_grad))
    mlp_came = [mlp_first] + [
        sent_on(mlp_terms[index], "tp", shards, step)
        for index, step in enumerate(steps)
        if index
    ]
    qkv_grad = attend_back(qkv, attended_grad, segment, cosine, sine)
    *mlp_came, qkv_grad = lax.optimization_barrier((*mlp_came, qkv_grad))
    one_terms = one_grad_pieces(place, qkv_grad, full_qkv, full_rows)
    one_came = [
        sent_on(one_terms[index], "tp", shards, step) for index, step in enumerate(steps)
    ]
    grad_att = att_grads(
        normed_one, after(qkv_grad, one_terms), attended, full_hidden_grad, groups
    )
    sum_mlp, grad_att = lax.optimization_barrier((sum_mlp, grad_att))
    sum_att = lax.psum_scatter(grad_att, "fsdp", scatter_dimension=0, tiled=False)

    output_here = added(
        features_of(hidden, own_shard) + mlp_terms[-1].astype(f32), mlp_came
    )
    output = to_home(output_here.astype(bf16))

    back_here = added(one_terms[-1].astype(f32), one_came)
    input_grad = to_home(
        (features_of(full_hidden_grad, own_shard).astype(f32) + back_here).astype(bf16)
    )

    sum_att = sum_att.astype(f32)
    sum_qkv = sum_att[:, : 3 * local_width].reshape(shard_rows, heads, 3, head_dim)
    out_part = sum_att[:, 3 * local_width :]
    out_pieces = model // out_part.shape[1]
    out_height = shard_rows // out_pieces
    sum_out = jnp.concatenate(
        [out_part[i * out_height : (i + 1) * out_height] for i in range(out_pieces)], axis=1
    )
    sum_gate, sum_up, sum_down = sum_mlp.astype(f32)
    return (
        output,
        input_grad,
        sum_qkv[:, :, 0].reshape(shard_rows, local_width),
        sum_qkv[:, :, 1].reshape(shard_rows, local_width),
        sum_qkv[:, :, 2].reshape(shard_rows, local_width),
        sum_out,
        sum_gate,
        sum_up,
        sum_down,
    )


def solution(mesh):
    in_specs = (
        P("fsdp", "tp"),
        P("fsdp", "tp"),
        P("fsdp", "tp"),
        P("fsdp", "tp"),
        P("fsdp", "tp"),
        P(("tp", "fsdp"), None),
        P("fsdp", "tp"),
        P("fsdp", "tp"),
        P(("tp", "fsdp"), None),
        P(),
        P(),
        P("fsdp"),
    )
    out_specs = (
        P("fsdp", "tp"),
        P("fsdp", "tp"),
        P("fsdp", "tp"),
        P("fsdp", "tp"),
        P("fsdp", "tp"),
        P(("tp", "fsdp"), None),
        P("fsdp", "tp"),
        P("fsdp", "tp"),
        P(("tp", "fsdp"), None),
    )
    return jax.shard_map(
        on_device, mesh=mesh, in_specs=in_specs, out_specs=out_specs, check_vma=False
    )
```

```python
import jax
import jax.numpy as jnp
from jax import lax
from jax.experimental import pallas as pl
from jax.experimental.pallas import tpu as pltpu
from jax.sharding import PartitionSpec as P

HEAD_DIM = 128
GROUP_CAP = 1024
SEQ_SLOTS = 4

norm_eps = 1e-05
rope_base = 10000.0
bf16 = jnp.bfloat16
f32 = jnp.float32


def matmul(left, right):
    return jnp.dot(left, right, preferred_element_type=f32)


def times_transposed(left, right):
    return lax.dot_general(
        left, right, (((1,), (1,)), ((), ())), preferred_element_type=f32
    )


def transposed_times(left, right):
    return lax.dot_general(
        left, right, (((0,), (0,)), ((), ())), preferred_element_type=f32
    )


def norm_parts(values_in):
    row_mean = jnp.mean(values_in, axis=-1, keepdims=True)
    centered = values_in - row_mean
    variance = jnp.mean(centered * centered, axis=-1, keepdims=True)
    inverse = lax.rsqrt(variance + norm_eps)
    return centered * inverse, inverse


def rope_tables(position, head_dim):
    half_dim = head_dim // 2
    frequency = rope_base ** (-(jnp.arange(half_dim, dtype=f32) * 2.0) / head_dim)
    angles = position.astype(f32)[:, None] * frequency[None, :]
    cosine, sine = jnp.cos(angles), jnp.sin(angles)
    return (
        jnp.concatenate([cosine, cosine], axis=1),
        jnp.concatenate([-sine, sine], axis=1),
    )


def segments(lengths):
    row_index = jnp.arange(GROUP_CAP, dtype=jnp.int32)
    slot_ids = jnp.arange(SEQ_SLOTS, dtype=jnp.int32)
    ends = jnp.sum(
        jnp.where(slot_ids[:, None] <= slot_ids[None, :], lengths[:, None], 0), axis=0
    )
    passed = row_index[:, None] >= ends[None, :]
    segment = jnp.sum(passed.astype(jnp.int32), axis=1)
    begin_row = jnp.max(jnp.where(passed, ends[None, :], 0), axis=1)
    return (segment, row_index - begin_row)


VMEM_LIMIT = 58 * 1024 * 1024
BLOCK = 256
WIDE = 512


def params():
    return pltpu.CompilerParams(vmem_limit_bytes=VMEM_LIMIT)


def cost(flops, read, transcendentals=0):
    return pl.CostEstimate(
        flops=int(flops), bytes_accessed=int(read), transcendentals=int(transcendentals)
    )


def half_turn(values_in):
    return pltpu.roll(values_in, HEAD_DIM // 2, 1)


def pick(me, owner, own, low, high):
    piece = own
    for step, (lower, higher) in enumerate(zip(low, high), start=1):
        piece = jnp.where(me == owner + step, lower, piece)
        piece = jnp.where(me == owner - step, higher, piece)
    return piece


def flat(own, arrived):
    return [own, *[low for low, _ in arrived], *[high for _, high in arrived]]


def picked(me, owner, refs):
    steps = len(refs) // 2
    blocks = [ref[...] for ref in refs]
    return pick(me, owner, blocks[0], blocks[1 : 1 + steps], blocks[1 + steps :])


def norm_kernel(me_ref, *refs):
    *come_refs, rows_ref, normed_ref = refs
    size = len(come_refs) // 2 + 1
    rows = jnp.concatenate([picked(me_ref[0], j, come_refs) for j in range(size)], axis=1)
    rows_ref[...] = rows
    normed_ref[...] = norm_parts(rows.astype(f32))[0].astype(bf16)


def gathered_norm(me, own, arrived):
    count, width = own.shape
    operands = flat(own, arrived)
    model = width * (len(operands) // 2 + 1)
    here = lambda i, me: (i, 0)
    out = jax.ShapeDtypeStruct((count, model), bf16)
    return pl.pallas_call(
        norm_kernel,
        grid_spec=pltpu.PrefetchScalarGridSpec(
            num_scalar_prefetch=1,
            grid=(count // BLOCK,),
            in_specs=[pl.BlockSpec((BLOCK, width), here)] * len(operands),
            out_specs=[pl.BlockSpec((BLOCK, model), here)] * 2,
        ),
        out_shape=[out, out],
        compiler_params=params(),
        cost_estimate=cost(20 * count * model, 8 * count * model),
        name="gathered_norm",
    )(me, *operands)


def qkv_kernel(rows_ref, wq_ref, wk_ref, wv_ref, cos_ref, sin_ref, *out_refs):
    weight = jnp.concatenate([wq_ref[...], wk_ref[...], wv_ref[...]], axis=1)
    for first in range(0, rows_ref.shape[0], BLOCK):
        rows = pl.ds(first, BLOCK)
        pre = matmul(rows_ref[rows, :], weight)
        for part in range(3):
            piece = pre[:, part * HEAD_DIM : (part + 1) * HEAD_DIM]
            if part < 2:
                piece = piece * cos_ref[rows, :] + half_turn(piece) * sin_ref[rows, :]
            out_refs[part][rows, :] = piece.astype(bf16)


def head_specs(model, heads):
    return [
        pl.BlockSpec((model, HEAD_DIM), lambda h, part=part: (0, part * heads + h))
        for part in range(3)
    ]


def project_qkv(rows, weight, cosine, sine):
    count, model = rows.shape
    columns = weight.shape[1]
    heads = columns // (3 * HEAD_DIM)
    whole = lambda h: (0, 0)
    return pl.pallas_call(
        qkv_kernel,
        grid=(heads,),
        in_specs=[
            pl.BlockSpec((count, model), whole),
            *head_specs(model, heads),
            pl.BlockSpec((count, HEAD_DIM), whole),
            pl.BlockSpec((count, HEAD_DIM), whole),
        ],
        out_specs=[pl.BlockSpec((count, HEAD_DIM), lambda h: (0, h))] * 3,
        out_shape=[jax.ShapeDtypeStruct((count, heads * HEAD_DIM), bf16)] * 3,
        compiler_params=params(),
        cost_estimate=cost(2 * count * model * columns, 2 * model * (count + columns)),
        name="qkv",
    )(rows, weight, weight, weight, cosine, sine)


def masked_softmax(q_rows, k_rows, seg_column, seg_row, row_first):
    scores = times_transposed(q_rows, k_rows) * HEAD_DIM ** (-0.5)
    row = lax.broadcasted_iota(jnp.int32, scores.shape, 0) + row_first
    column = lax.broadcasted_iota(jnp.int32, scores.shape, 1)
    allowed = (seg_column == seg_row) & (column <= row)
    scores = jnp.where(allowed, scores, -1e30)
    exponent = jnp.exp(scores - jnp.max(scores, axis=-1, keepdims=True))
    return exponent * (1.0 / jnp.sum(exponent, axis=-1, keepdims=True))


def attend_kernel(q_ref, k_ref, v_ref, column_ref, row_ref, out_ref):
    block = pl.program_id(1)
    for index in range(k_ref.shape[0] // BLOCK):

        @pl.when(block == index)
        def _(index=index):
            seen = (index + 1) * BLOCK
            prob = masked_softmax(
                q_ref[...], k_ref[:seen, :], column_ref[...], row_ref[:, :seen], index * BLOCK
            )
            out_ref[...] = matmul(prob.astype(bf16), v_ref[:seen, :]).astype(bf16)


def attend(qkv, segment):
    count = qkv[0].shape[0]
    heads = qkv[0].shape[1] // HEAD_DIM
    return pl.pallas_call(
        attend_kernel,
        grid=(heads, count // BLOCK),
        in_specs=[
            pl.BlockSpec((BLOCK, HEAD_DIM), lambda h, i: (i, h)),
            pl.BlockSpec((count, HEAD_DIM), lambda h, i: (0, h)),
            pl.BlockSpec((count, HEAD_DIM), lambda h, i: (0, h)),
            pl.BlockSpec((BLOCK, 1), lambda h, i: (i, 0)),
            pl.BlockSpec((1, count), lambda h, i: (0, 0)),
        ],
        out_specs=pl.BlockSpec((BLOCK, HEAD_DIM), lambda h, i: (i, h)),
        out_shape=jax.ShapeDtypeStruct((count, heads * HEAD_DIM), bf16),
        compiler_params=params(),
        cost_estimate=cost(
            4 * heads * count * count * HEAD_DIM, 8 * count * heads * HEAD_DIM, heads * count * count
        ),
        name="attend",
    )(*qkv, segment[:, None], segment[None, :])


def attend_back_kernel(
    q_ref, k_ref, v_ref, grad_ref, column_ref, row_ref, cos_ref, sin_ref, dq_ref, dk_ref, dv_ref, total
):
    block = pl.program_id(1)
    scale = HEAD_DIM ** (-0.5)
    blocks = k_ref.shape[0] // BLOCK

    @pl.when(block == 0)
    def _():
        total[...] = jnp.zeros_like(total)

    for index in range(blocks):

        @pl.when(block == index)
        def _(index=index):
            seen = (index + 1) * BLOCK
            q_rows, k_rows, grad = q_ref[...], k_ref[:seen, :], grad_ref[...]
            prob = masked_softmax(
                q_rows, k_rows, column_ref[...], row_ref[:, :seen], index * BLOCK
            )
            prob_grad = times_transposed(grad, v_ref[:seen, :])
            delta = jnp.sum(prob_grad * prob, axis=-1, keepdims=True)
            score_grad = (prob * (prob_grad - delta)).astype(bf16)
            total[0, index * BLOCK : seen, :] = matmul(score_grad, k_rows) * scale
            total[1, :seen, :] += transposed_times(score_grad, q_rows) * scale
            total[2, :seen, :] += transposed_times(prob.astype(bf16), grad)

    @pl.when(block == blocks - 1)
    def _():
        for part, out_ref in enumerate((dq_ref, dk_ref, dv_ref)):
            piece = total[part]
            if part < 2:
                piece = piece * cos_ref[...] - half_turn(piece) * sin_ref[...]
            out_ref[...] = piece.astype(bf16)


def attend_back(qkv, grad, segment, cosine, sine):
    count = qkv[0].shape[0]
    heads = qkv[0].shape[1] // HEAD_DIM
    return pl.pallas_call(
        attend_back_kernel,
        grid=(heads, count // BLOCK),
        in_specs=[
            pl.BlockSpec((BLOCK, HEAD_DIM), lambda h, i: (i, h)),
            pl.BlockSpec((count, HEAD_DIM), lambda h, i: (0, h)),
            pl.BlockSpec((count, HEAD_DIM), lambda h, i: (0, h)),
            pl.BlockSpec((BLOCK, HEAD_DIM), lambda h, i: (i, h)),
            pl.BlockSpec((BLOCK, 1), lambda h, i: (i, 0)),
            pl.BlockSpec((1, count), lambda h, i: (0, 0)),
            pl.BlockSpec((count, HEAD_DIM), lambda h, i: (0, 0)),
            pl.BlockSpec((count, HEAD_DIM), lambda h, i: (0, 0)),
        ],
        out_specs=[pl.BlockSpec((count, HEAD_DIM), lambda h, i: (0, h))] * 3,
        out_shape=[jax.ShapeDtypeStruct(qkv[0].shape, bf16)] * 3,
        scratch_shapes=[pltpu.VMEM((3, count, HEAD_DIM), f32)],
        compiler_params=params(),
        cost_estimate=cost(1000, 1000),
        name="attend_back",
    )(*qkv, grad, segment[:, None], segment[None, :], cosine, sine)


def hidden_kernel(me_ref, weight_ref, rows_ref, *refs):
    *come_refs, hidden_ref, normed_ref = refs
    size = len(come_refs) // 2 + 1
    attended = jnp.concatenate([picked(me_ref[0], j, come_refs) for j in range(size)], axis=1)
    hidden = rows_ref[...].astype(f32) + matmul(attended, weight_ref[...])
    hidden_ref[...] = hidden
    normed_ref[...] = norm_parts(hidden)[0].astype(bf16)


def hidden_and_norm(me, own, arrived, weight, rows):
    count, model = rows.shape
    operands = flat(own, arrived)
    here = lambda i, me: (i, 0)
    return pl.pallas_call(
        hidden_kernel,
        grid_spec=pltpu.PrefetchScalarGridSpec(
            num_scalar_prefetch=1,
            grid=(count // BLOCK,),
            in_specs=[
                pl.BlockSpec((model, model), lambda i, me: (0, 0), pipeline_mode=pl.Buffered(1)),
                pl.BlockSpec((BLOCK, model), here),
                *[pl.BlockSpec((BLOCK, own.shape[1]), here)] * len(operands),
            ],
            out_specs=[pl.BlockSpec((BLOCK, model), here)] * 2,
        ),
        out_shape=[
            jax.ShapeDtypeStruct((count, model), f32),
            jax.ShapeDtypeStruct((count, model), bf16),
        ],
        compiler_params=params(),
        cost_estimate=cost(2 * count * model * model, 2 * model * model + 10 * count * model),
        name="hidden",
    )(me, weight, rows, *operands)


def up_kernel(rows_ref, gate_ref, up_ref, gate_out, up_out, act_ref):
    for first in range(0, rows_ref.shape[0], BLOCK):
        rows = pl.ds(first, BLOCK)
        gate = matmul(rows_ref[rows, :], gate_ref[0])
        up = matmul(rows_ref[rows, :], up_ref[0])
        sigmoid = 1.0 / (1.0 + jnp.exp(-gate))
        silu = gate * sigmoid
        gate_out[rows, :] = (up * (sigmoid + silu * (1.0 - sigmoid))).astype(bf16)
        up_out[rows, :] = silu.astype(bf16)
        act_ref[rows, :] = (silu * up).astype(bf16)


def mlp_up(rows, weights):
    count, model = rows.shape
    hidden_units = weights.shape[2]
    out = jax.ShapeDtypeStruct((count, hidden_units), bf16)
    return pl.pallas_call(
        up_kernel,
        grid=(hidden_units // WIDE,),
        in_specs=[
            pl.BlockSpec((count, model), lambda j: (0, 0)),
            pl.BlockSpec((1, model, WIDE), lambda j: (0, 0, j)),
            pl.BlockSpec((1, model, WIDE), lambda j: (1, 0, j)),
        ],
        out_specs=[pl.BlockSpec((count, WIDE), lambda j: (0, j))] * 3,
        out_shape=[out] * 3,
        compiler_params=params(),
        cost_estimate=cost(
            4 * count * model * hidden_units,
            4 * model * hidden_units + 2 * count * model + 10 * count * hidden_units,
            count * hidden_units,
        ),
        name="mlp_up",
    )(rows, weights, weights)


def down_back_kernel(me_ref, down_ref, gate_in, up_in, *refs):
    *come_refs, grad_ref, dgate_ref, dup_ref = refs
    size = len(come_refs) // 2 + 1
    width = come_refs[0].shape[1]

    @pl.when(pl.program_id(0) == 0)
    def _():
        for owner in range(size):
            grad_ref[:, owner * width : (owner + 1) * width] = picked(
                me_ref[0], owner, come_refs
            )

    for first in range(0, grad_ref.shape[0], BLOCK):
        rows = pl.ds(first, BLOCK)
        down = times_transposed(grad_ref[rows, :], down_ref[0])
        dgate_ref[rows, :] = (down * gate_in[rows, :].astype(f32)).astype(bf16)
        dup_ref[rows, :] = (down * up_in[rows, :].astype(f32)).astype(bf16)


def mlp_down_back(me, own, arrived, weights, gate, up):
    operands = flat(own, arrived)
    count, width = own.shape
    model = width * (len(operands) // 2 + 1)
    hidden_units = weights.shape[2]
    part = pl.BlockSpec((count, WIDE), lambda j, me: (0, j))
    whole = lambda j, me: (0, 0)
    out = jax.ShapeDtypeStruct((count, hidden_units), bf16)
    return pl.pallas_call(
        down_back_kernel,
        grid_spec=pltpu.PrefetchScalarGridSpec(
            num_scalar_prefetch=1,
            grid=(hidden_units // WIDE,),
            in_specs=[
                pl.BlockSpec((1, WIDE, model), lambda j, me: (2, j, 0)),
                part,
                part,
                *[pl.BlockSpec((count, width), whole, pipeline_mode=pl.Buffered(1))]
                * len(operands),
            ],
            out_specs=[pl.BlockSpec((count, model), whole), part, part],
        ),
        out_shape=[jax.ShapeDtypeStruct((count, model), bf16), out, out],
        compiler_params=params(),
        cost_estimate=cost(
            2 * count * model * hidden_units,
            2 * model * hidden_units + 2 * count * model + 12 * count * hidden_units,
            count * hidden_units,
        ),
        name="mlp_down_back",
    )(me, weights, gate, up, *operands)


def mlp_piece_kernel(order_ref, act_ref, down_ref, *out_refs):
    for piece, out_ref in enumerate(out_refs):

        @pl.when(pl.program_id(0) == piece)
        def _(out_ref=out_ref):
            for first in range(0, act_ref.shape[0], BLOCK):
                rows = pl.ds(first, BLOCK)
                out_ref[rows, :] = matmul(act_ref[rows, :], down_ref[0]).astype(bf16)


def mlp_pieces(order, act, weights, width):
    count, hidden_units = act.shape
    pieces = order.shape[0]
    whole = lambda g, order: (0, 0)
    return pl.pallas_call(
        mlp_piece_kernel,
        grid_spec=pltpu.PrefetchScalarGridSpec(
            num_scalar_prefetch=1,
            grid=(pieces,),
            in_specs=[
                pl.BlockSpec((count, hidden_units), whole, pipeline_mode=pl.Buffered(1)),
                pl.BlockSpec((1, hidden_units, width), lambda g, order: (2, 0, order[g])),
            ],
            out_specs=[pl.BlockSpec((count, width), whole)] * pieces,
        ),
        out_shape=[jax.ShapeDtypeStruct((count, width), bf16)] * pieces,
        compiler_params=params(),
        cost_estimate=cost(
            2 * pieces * count * width * hidden_units, 2 * pieces * width * hidden_units
        ),
        name="mlp_piece",
    )(order, act, weights)


def norm_back(values_in, grad_in):
    unit_rows, inverse = norm_parts(values_in)
    return inverse * (
        grad_in
        - jnp.mean(grad_in, axis=-1, keepdims=True)
        - unit_rows * jnp.mean(grad_in * unit_rows, axis=-1, keepdims=True)
    )


def put_at(place, value, refs):
    for index, ref in enumerate(refs):

        @pl.when(place == index)
        def _(ref=ref):
            ref[...] = value


def two_grad_kernel(order_ref, *refs):
    pieces = (len(refs) - 3) // 4
    row_refs = refs[: 3 * pieces]
    gate_ref, up_ref = refs[3 * pieces : 3 * pieces + 2]
    out_refs, total = refs[3 * pieces + 2 : -1], refs[-1]
    step = pl.program_id(0)
    columns = pl.ds(pl.multiple_of(step * WIDE, WIDE), WIDE)
    for piece in range(pieces):
        total[piece, :, columns] = times_transposed(
            row_refs[3 * piece][...], gate_ref[0]
        ) + times_transposed(row_refs[3 * piece + 1][...], up_ref[0])

    @pl.when(step == pl.num_programs(0) - 1)
    def _():
        for piece in range(pieces):
            out_refs[piece][...] = norm_back(
                row_refs[3 * piece + 2][...], total[piece]
            ).astype(bf16)


def two_grad_pieces(order, dgate, dup, weights, hidden, quarter):
    pieces = order.shape[0]
    hidden_units = dgate.shape[1]
    model = weights.shape[1]
    rows = []
    for p in range(pieces):
        here = lambda j, order, p=p: (order[p], 0)
        rows += [pl.BlockSpec((quarter, hidden_units), here)] * 2
        rows += [pl.BlockSpec((quarter, model), here, pipeline_mode=pl.Buffered(1))]
    return pl.pallas_call(
        two_grad_kernel,
        grid_spec=pltpu.PrefetchScalarGridSpec(
            num_scalar_prefetch=1,
            grid=(model // WIDE,),
            in_specs=[
                *rows,
                pl.BlockSpec((1, WIDE, hidden_units), lambda j, order: (0, j, 0)),
                pl.BlockSpec((1, WIDE, hidden_units), lambda j, order: (1, j, 0)),
            ],
            out_specs=[pl.BlockSpec((quarter, model), lambda j, order: (0, 0))] * pieces,
            scratch_shapes=[pltpu.VMEM((pieces, quarter, model), f32)],
        ),
        out_shape=[jax.ShapeDtypeStruct((quarter, model), bf16)] * pieces,
        compiler_params=params(),
        cost_estimate=cost(
            4 * pieces * quarter * model * hidden_units, 4 * model * hidden_units
        ),
        name="two_grad",
    )(order, *([dgate, dup, hidden] * pieces), weights, weights)


def att_grad_kernel(me_ref, weight_ref, *refs):
    *come_refs, whole_ref, out_ref = refs
    rows = picked(me_ref[0], pl.program_id(0), come_refs)
    whole_ref[...] = rows
    out_ref[...] = times_transposed(rows, weight_ref[...]).astype(bf16)


def att_grad_rows(me, own, arrived, weight, local):
    operands = flat(own, arrived)
    share, model = own.shape
    size = len(operands) // 2 + 1
    here = lambda i, me: (i, 0)
    once = pl.Buffered(1)
    return pl.pallas_call(
        att_grad_kernel,
        grid_spec=pltpu.PrefetchScalarGridSpec(
            num_scalar_prefetch=1,
            grid=(size,),
            in_specs=[
                pl.BlockSpec((local, model), lambda i, me: (me[0], 0), pipeline_mode=once),
                *[pl.BlockSpec((share, model), lambda i, me: (0, 0), pipeline_mode=once)]
                * len(operands),
            ],
            out_specs=[
                pl.BlockSpec((share, model), here),
                pl.BlockSpec((share, local), here),
            ],
        ),
        out_shape=[
            jax.ShapeDtypeStruct((share * size, model), bf16),
            jax.ShapeDtypeStruct((share * size, local), bf16),
        ],
        compiler_params=params(),
        cost_estimate=cost(1000, 1000),
        name="att_grad",
    )(me, weight, *operands)


def one_grad_kernel(place_ref, dq_ref, dk_ref, dv_ref, weight_ref, rows_ref, *out_refs):
    columns = jnp.concatenate([dq_ref[...], dk_ref[...], dv_ref[...]], axis=1)
    grad = norm_back(
        rows_ref[...].astype(f32), times_transposed(columns, weight_ref[...])
    ).astype(bf16)
    width = out_refs[0].shape[1]
    for piece in range(len(out_refs)):
        put_at(place_ref[piece], grad[:, piece * width : (piece + 1) * width], out_refs)


def one_grad_pieces(place, grads, weight, rows):
    count, local = grads[0].shape
    columns = 3 * local
    pieces = place.shape[0]
    model = rows.shape[1]
    here = lambda i, place: (i, 0)
    return pl.pallas_call(
        one_grad_kernel,
        grid_spec=pltpu.PrefetchScalarGridSpec(
            num_scalar_prefetch=1,
            grid=(count // BLOCK,),
            in_specs=[
                *[pl.BlockSpec((BLOCK, local), here)] * 3,
                pl.BlockSpec(
                    (model, columns), lambda i, place: (0, 0), pipeline_mode=pl.Buffered(1)
                ),
                pl.BlockSpec((BLOCK, model), here),
            ],
            out_specs=[pl.BlockSpec((BLOCK, model // pieces), here)] * pieces,
        ),
        out_shape=[jax.ShapeDtypeStruct((count, model // pieces), bf16)] * pieces,
        compiler_params=params(),
        cost_estimate=cost(
            2 * count * model * columns, 2 * columns * model + 6 * count * columns
        ),
        name="one_grad",
    )(place, *grads, weight, rows)


def att_grads_kernel(normed_ref, dq_ref, dk_ref, dv_ref, att_ref, hidden_ref, out_ref):
    owner = pl.program_id(0)
    columns = 3 * dq_ref.shape[1]
    grads = jnp.concatenate([dq_ref[...], dk_ref[...], dv_ref[...]], axis=1)
    out_ref[0, :, :columns] = transposed_times(normed_ref[...], grads).astype(bf16)
    model = hidden_ref.shape[1]
    rest = model - columns
    pieces = model // rest
    height = out_ref.shape[1] // pieces
    per_tile = HEAD_DIM // height
    product = transposed_times(att_ref[...], hidden_ref[...]).astype(bf16)
    for place in range(per_tile):

        @pl.when(lax.rem(owner, per_tile) == place)
        def _(place=place):
            for piece in range(pieces):
                out_ref[0, piece * height : (piece + 1) * height, columns:] = product[
                    place * height : (place + 1) * height, piece * rest : (piece + 1) * rest
                ]


def att_grads(normed, qkv_grad, attended, hidden_grad, groups):
    count, model = normed.shape
    local = attended.shape[1]
    columns = 3 * local
    tall = model // groups
    per_tile = HEAD_DIM // (local // groups)
    once = pl.Buffered(1)
    whole = lambda i: (0, 0)
    if tall % HEAD_DIM == 0:
        normed_spec = pl.BlockSpec((count, tall), lambda i: (0, i))
        operand = normed
    else:
        normed_spec = pl.BlockSpec((None, count, tall), lambda i: (i, 0, 0))
        operand = normed.reshape(count, groups, tall).swapaxes(0, 1)
    return pl.pallas_call(
        att_grads_kernel,
        grid=(groups,),
        in_specs=[
            normed_spec,
            *[pl.BlockSpec((count, local), whole, pipeline_mode=once)] * 3,
            pl.BlockSpec((count, HEAD_DIM), lambda i: (0, i // per_tile)),
            pl.BlockSpec((count, model), whole, pipeline_mode=once),
        ],
        out_specs=pl.BlockSpec((1, tall, model), lambda i: (i, 0, 0)),
        out_shape=jax.ShapeDtypeStruct((groups, tall, model), bf16),
        compiler_params=params(),
        cost_estimate=cost(1000, 1000),
        name="att_grads",
    )(operand, *qkv_grad, attended, hidden_grad)


def mlp_grads_kernel(*refs):
    *operands, out_ref = refs
    count = len(operands) // 2
    total = transposed_times(operands[0][...], operands[count][...])
    for part in range(1, count):
        total += transposed_times(operands[part][...], operands[count + part][...])
    out_ref[0] = total.astype(bf16)


def mlp_grads(which, left, right, before=None):
    rows = left[0].shape[0]
    model, hidden_units = left[0].shape[1], right[0].shape[1]
    once = pl.Buffered(1)
    specs = [pl.BlockSpec((rows, BLOCK), lambda i: (0, i)) for _ in left]
    specs += [
        pl.BlockSpec((rows, hidden_units), lambda i: (0, 0), pipeline_mode=once) for _ in right
    ]
    operands = [*left, *right]
    body = mlp_grads_kernel
    aliases = {}
    if before is not None:
        aliases = {len(operands): 0}
        specs.append(pl.BlockSpec(memory_space=pl.ANY))
        operands.append(before)
        body = lambda *refs: mlp_grads_kernel(*refs[:-2], refs[-1])
    count = rows * len(left)
    return pl.pallas_call(
        body,
        grid=(model // BLOCK,),
        in_specs=specs,
        out_specs=pl.BlockSpec((1, BLOCK, hidden_units), lambda i: (which, i, 0)),
        out_shape=jax.ShapeDtypeStruct((3, model, hidden_units), bf16),
        input_output_aliases=aliases,
        compiler_params=params(),
        cost_estimate=cost(
            2 * count * model * hidden_units, 2 * model * hidden_units + 4 * count * model
        ),
        name="mlp_grads",
    )(*operands)


def after(value, *others):
    return lax.optimization_barrier((value, *others))[0]


def line_step(block, axis, size, step):
    from_low, from_high = block
    up = [(i, i + 1) for i in range(step - 1, size - 1)]
    down = [(i, i - 1) for i in range(size - step, 0, -1)]
    return lax.ppermute(from_low, axis, up), lax.ppermute(from_high, axis, down)


def chain_gather(block, axis, size, begun=None):
    arrived = list(begun or [])
    for step in range(len(arrived) + 1, size):
        arrived.append(line_step(arrived[-1] if arrived else (block, block), axis, size, step))
    return arrived


def far_first(size):
    return sorted(range(1, size), key=lambda step: -min(step, size - step))


def sent_on(term, axis, size, step):
    return lax.ppermute(term, axis, [(i, (i + step) % size) for i in range(size)])


def added(own, came):
    for piece in came:
        own = own + piece.astype(f32)
    return own


def on_device(
    tokens,
    cotangent,
    w_query,
    w_key,
    w_value,
    w_out,
    w_gate,
    w_up,
    w_down,
    seq_lengths,
    deal,
    row_dest,
):
    groups = lax.axis_size("fsdp")
    shards = lax.axis_size("tp")
    own_group = lax.axis_index("fsdp")
    own_shard = lax.axis_index("tp")
    capacity = GROUP_CAP
    per_pair = capacity // groups
    quarter = capacity // shards
    head_dim = HEAD_DIM
    given, width = tokens.shape
    model = width * shards
    local_width = w_query.shape[1]
    shard_rows = w_query.shape[0]

    steps = far_first(shards)
    order = jnp.stack([lax.rem(own_shard + step, shards) for step in (*steps, 0)])
    around = jnp.stack([lax.rem(own_shard + step, shards) for step in range(shards)])
    place_of = [0] * shards
    for index, step in enumerate((*steps, 0)):
        place_of[step] = index
    place = jnp.stack(
        [
            sum(
                jnp.where(lax.rem(own_shard + step, shards) == j, place_of[step], 0)
                for step in range(shards)
            )
            for j in range(shards)
        ]
    )

    target = row_dest // capacity
    within = row_dest - target * capacity
    given_index = jnp.arange(given, dtype=jnp.int32)
    earlier = (target[:, None] == target[None, :]) & (
        given_index[None, :] < given_index[:, None]
    )
    slot_of = target * per_pair + jnp.sum(earlier.astype(jnp.int32), axis=1)
    slots = jnp.arange(capacity, dtype=jnp.int32)
    deal_hit = slots[:, None] == slot_of[None, :]
    deal_out = deal_hit.astype(bf16)
    place_high, place_low = (within + 1) // 32, (within + 1) % 32
    lane = jnp.arange(HEAD_DIM, dtype=jnp.int32)[None, :]
    place_columns = jnp.where(
        lane == 0, place_high[:, None], jnp.where(lane == 1, place_low[:, None], 0)
    ).astype(bf16)

    def over_fsdp(rows):
        return lax.all_to_all(rows, "fsdp", split_axis=0, concat_axis=0, tiled=True)

    sent_rows = matmul(deal_out, jnp.concatenate([tokens, place_columns], axis=1)).astype(bf16)
    sent_grads = matmul(deal_out, cotangent).astype(bf16)

    qkv_shard = jnp.concatenate([w_query, w_key, w_value], axis=1)
    full_qkv = lax.all_gather(qkv_shard, "fsdp", axis=0, tiled=True)
    out_came = [sent_on(w_out, "tp", shards, step) for step in range(1, shards)]
    came_rows = over_fsdp(sent_rows)
    mlp_shard = jnp.stack([w_gate, w_up, w_down])
    *out_came, came_rows, sent_grads, mlp_shard = lax.optimization_barrier(
        (*out_came, came_rows, sent_grads, mlp_shard)
    )
    came_place = came_rows[:, width : width + 2].astype(jnp.int32)
    recv_place = came_place[:, 0] * 32 + came_place[:, 1] - 1
    place_in = (slots[:, None] == recv_place[None, :]).astype(bf16)
    out_came = [w_out] + out_came
    out_rows = []
    for owner in range(shards):
        piece = w_out
        for step in range(1, shards):
            piece = jnp.where(own_shard == (owner + step) % shards, out_came[step], piece)
        out_rows.append(piece)
    out_rows = jnp.stack(out_rows)
    full_out = lax.all_gather(out_rows, "fsdp", axis=1, tiled=True).reshape(model, model)

    full_mlp = lax.all_gather(mlp_shard, "fsdp", axis=1, tiled=True)
    buffer_rows = matmul(place_in, came_rows[:, :width]).astype(bf16)
    buffer_grads = matmul(place_in, over_fsdp(after(sent_grads, buffer_rows))).astype(bf16)
    rows_come = chain_gather(buffer_rows, "tp", shards)
    *last, first_grads = lax.optimization_barrier((*rows_come[-1], buffer_grads))
    rows_come[-1] = tuple(last)
    me = own_shard[None].astype(jnp.int32)

    list_index = jnp.sum(jnp.where(deal == own_group, jnp.arange(groups, dtype=jnp.int32), 0))
    lengths = lax.dynamic_index_in_dim(seq_lengths, list_index, 0, keepdims=False)
    segment, position = segments(lengths)
    cosine, sine = rope_tables(position, head_dim)

    full_rows, normed_one = gathered_norm(me, buffer_rows, rows_come)
    first_grads, normed_one = lax.optimization_barrier((first_grads, normed_one))
    grads_begun = line_step((first_grads, first_grads), "tp", shards, 1)
    qkv = project_qkv(normed_one, full_qkv, cosine, sine)
    attended = attend(qkv, segment)
    attended, *grads_begun = lax.optimization_barrier((attended, *grads_begun))
    att_come = chain_gather(attended, "tp", shards)
    *grads_begun, last_low, last_high = lax.optimization_barrier((*grads_begun, *att_come[-1]))
    att_come[-1] = (last_low, last_high)
    grads_come = [grads_begun, line_step(grads_begun, "tp", shards, 2)]
    hidden, normed_two = hidden_and_norm(me, attended, att_come, full_out, full_rows)
    *grads_come[1], normed_two = lax.optimization_barrier((*grads_come[1], normed_two))
    grads_come = chain_gather(first_grads, "tp", shards, grads_come)
    gate, up, activated = mlp_up(normed_two, full_mlp)
    def features_of(rows, owner):
        return lax.dynamic_slice_in_dim(rows, owner * width, width, 1)

    *last, activated = lax.optimization_barrier((*grads_come[-1], activated))
    grads_come[-1] = tuple(last)
    full_grads, gate_grad, up_grad = mlp_down_back(
        me, first_grads, grads_come, full_mlp, gate, up
    )

    def rows_of(rows, owner):
        return lax.dynamic_slice_in_dim(rows, owner * quarter, quarter, 0)

    near = [steps[1], steps[0], *steps[2:], 0]
    near_order = jnp.stack([lax.rem(own_shard + step, shards) for step in near])
    two_first = two_grad_pieces(
        near_order[:1], gate_grad, up_grad, full_mlp, hidden, quarter
    )
    two_rest = two_grad_pieces(
        near_order[1:], gate_grad, after(up_grad, *two_first), full_mlp, hidden, quarter
    )
    two_came = [
        sent_on(term, "tp", shards, step)
        for term, step in zip((*two_first, *two_rest), near[:-1])
    ]
    grad_mlp = mlp_grads(0, [normed_two], [after(gate_grad, *two_rest)])
    grad_mlp = mlp_grads(1, [normed_two], [up_grad], grad_mlp)
    grad_mlp = mlp_grads(2, [activated], [full_grads], grad_mlp)
    *two_came, grad_mlp = lax.optimization_barrier((*two_came, grad_mlp))
    sum_mlp = lax.psum_scatter(grad_mlp, "fsdp", scatter_dimension=1, tiled=True)
    back_low = added(
        rows_of(full_grads, own_shard).astype(f32) + two_rest[-1].astype(f32), two_came
    ).astype(bf16)
    back_come = [line_step((back_low, back_low), "tp", shards, 1)]
    terms = mlp_pieces(around, after(activated, grad_mlp, back_low), full_mlp, width)
    mlp_come = []
    for step in range(1, shards):
        back_come[-1], mlp_come, terms = lax.optimization_barrier(
            (back_come[-1], mlp_come, terms)
        )
        if step < shards - 1:
            back_come.append(line_step(back_come[-1], "tp", shards, step + 1))
        low, high = terms[shards - step], terms[step]
        if mlp_come:
            low, high = (
                (term.astype(f32) + came.astype(f32)).astype(bf16)
                for term, came in zip((low, high), mlp_come)
            )
        up = [(i, i + 1) for i in range(step)]
        down = [(i, i - 1) for i in range(shards - 1, shards - 1 - step, -1)]
        mlp_come = [lax.ppermute(low, "tp", up), lax.ppermute(high, "tp", down)]
    full_hidden_grad, attended_grad = att_grad_rows(
        me, back_low, back_come, full_out, local_width
    )
    qkv_grad = attend_back(qkv, attended_grad, segment, cosine, sine)
    one_terms = one_grad_pieces(place, qkv_grad, full_qkv, full_rows)
    one_came = [sent_on(term, "tp", shards, step) for term, step in zip(one_terms, steps)]
    *mlp_come, late_grad, _ = lax.optimization_barrier(
        (*mlp_come, tuple(qkv_grad), tuple(one_terms[:3]))
    )
    grad_att = att_grads(
        normed_one, late_grad, attended, full_hidden_grad, groups
    )
    sum_mlp, grad_att = lax.optimization_barrier((sum_mlp, grad_att))
    sum_att = lax.psum_scatter(grad_att, "fsdp", scatter_dimension=0, tiled=False)

    output_here = added(
        features_of(hidden, own_shard) + terms[0].astype(f32), mlp_come
    )
    sum_att = sum_att.astype(f32)
    out_part = sum_att[:, 3 * local_width :]
    out_pieces = model // out_part.shape[1]
    out_height = shard_rows // out_pieces
    sum_out = jnp.concatenate(
        [out_part[i * out_height : (i + 1) * out_height] for i in range(out_pieces)], axis=1
    )
    sum_gate, sum_up, sum_down = sum_mlp.astype(f32)
    back_here = added(one_terms[-1].astype(f32), one_came)
    input_here = features_of(full_hidden_grad, own_shard).astype(f32) + back_here
    here = jnp.concatenate([output_here.astype(bf16), input_here.astype(bf16)], axis=1)
    sent_back = transposed_times(place_in, here).astype(bf16)
    sums = (
        sum_att[:, : local_width],
        sum_att[:, local_width : 2 * local_width],
        sum_att[:, 2 * local_width : 3 * local_width],
        sum_out,
        sum_gate,
        sum_up,
        sum_down,
    )
    came_back, *sums = lax.optimization_barrier((over_fsdp(sent_back), *sums))
    home = transposed_times(deal_out, came_back).astype(bf16)
    return (home[:, :width], home[:, width:], *sums)


def solution(mesh):
    in_specs = (
        P("fsdp", "tp"),
        P("fsdp", "tp"),
        P("fsdp", "tp"),
        P("fsdp", "tp"),
        P("fsdp", "tp"),
        P(("tp", "fsdp"), None),
        P("fsdp", "tp"),
        P("fsdp", "tp"),
        P(("tp", "fsdp"), None),
        P(),
        P(),
        P("fsdp"),
    )
    out_specs = (
        P("fsdp", "tp"),
        P("fsdp", "tp"),
        P("fsdp", "tp"),
        P("fsdp", "tp"),
        P("fsdp", "tp"),
        P(("tp", "fsdp"), None),
        P("fsdp", "tp"),
        P("fsdp", "tp"),
        P(("tp", "fsdp"), None),
    )
    return jax.shard_map(
        on_device, mesh=mesh, in_specs=in_specs, out_specs=out_specs, check_vma=False
    )
```

```python
import jax
import jax.numpy as jnp
from jax import lax
from jax.experimental import pallas as pl
from jax.experimental.pallas import tpu as pltpu
from jax.sharding import PartitionSpec as P

HEAD_DIM = 128
GROUP_CAP = 1024
SEQ_SLOTS = 4

norm_eps = 1e-05
rope_base = 10000.0
bf16 = jnp.bfloat16
f32 = jnp.float32


def matmul(left, right):
    return jnp.dot(left, right, preferred_element_type=f32)


def times_transposed(left, right):
    return lax.dot_general(
        left, right, (((1,), (1,)), ((), ())), preferred_element_type=f32
    )


def transposed_times(left, right):
    return lax.dot_general(
        left, right, (((0,), (0,)), ((), ())), preferred_element_type=f32
    )


def norm_parts(values_in):
    row_mean = jnp.mean(values_in, axis=-1, keepdims=True)
    centered = values_in - row_mean
    variance = jnp.mean(centered * centered, axis=-1, keepdims=True)
    inverse = lax.rsqrt(variance + norm_eps)
    return centered * inverse, inverse


def rope_tables(position, head_dim):
    half_dim = head_dim // 2
    frequency = rope_base ** (-(jnp.arange(half_dim, dtype=f32) * 2.0) / head_dim)
    angles = position.astype(f32)[:, None] * frequency[None, :]
    cosine, sine = jnp.cos(angles), jnp.sin(angles)
    return (
        jnp.concatenate([cosine, cosine], axis=1),
        jnp.concatenate([-sine, sine], axis=1),
    )


def segments(lengths):
    row_index = jnp.arange(GROUP_CAP, dtype=jnp.int32)
    slot_ids = jnp.arange(SEQ_SLOTS, dtype=jnp.int32)
    ends = jnp.sum(
        jnp.where(slot_ids[:, None] <= slot_ids[None, :], lengths[:, None], 0), axis=0
    )
    passed = row_index[:, None] >= ends[None, :]
    segment = jnp.sum(passed.astype(jnp.int32), axis=1)
    begin_row = jnp.max(jnp.where(passed, ends[None, :], 0), axis=1)
    return (segment, row_index - begin_row)


VMEM_LIMIT = 58 * 1024 * 1024
BLOCK = 256
WIDE = 512


def params():
    return pltpu.CompilerParams(vmem_limit_bytes=VMEM_LIMIT)


def cost(flops, read, transcendentals=0):
    return pl.CostEstimate(
        flops=int(flops), bytes_accessed=int(read), transcendentals=int(transcendentals)
    )


def half_turn(values_in):
    return pltpu.roll(values_in, HEAD_DIM // 2, 1)


def pick(me, owner, own, low, high):
    piece = own
    for step, (lower, higher) in enumerate(zip(low, high), start=1):
        piece = jnp.where(me == owner + step, lower, piece)
        piece = jnp.where(me == owner - step, higher, piece)
    return piece


def flat(own, arrived):
    return [own, *[low for low, _ in arrived], *[high for _, high in arrived]]


def picked(me, owner, refs):
    steps = len(refs) // 2
    blocks = [ref[...] for ref in refs]
    return pick(me, owner, blocks[0], blocks[1 : 1 + steps], blocks[1 + steps :])


def norm_kernel(me_ref, *refs):
    *come_refs, rows_ref, normed_ref, inverse_ref = refs
    size = len(come_refs) // 2 + 1
    rows = jnp.concatenate([picked(me_ref[0], j, come_refs) for j in range(size)], axis=1)
    rows_ref[...] = rows
    unit, inverse_ref[...] = norm_parts(rows.astype(f32))
    normed_ref[...] = unit.astype(bf16)


def gathered_norm(me, own, arrived):
    count, width = own.shape
    operands = flat(own, arrived)
    model = width * (len(operands) // 2 + 1)
    here = lambda i, me: (i, 0)
    out = jax.ShapeDtypeStruct((count, model), bf16)
    return pl.pallas_call(
        norm_kernel,
        grid_spec=pltpu.PrefetchScalarGridSpec(
            num_scalar_prefetch=1,
            grid=(count // BLOCK,),
            in_specs=[pl.BlockSpec((BLOCK, width), here)] * len(operands),
            out_specs=[
                pl.BlockSpec((BLOCK, model), here),
                pl.BlockSpec((BLOCK, model), here),
                pl.BlockSpec((BLOCK, 1), here),
            ],
        ),
        out_shape=[out, out, jax.ShapeDtypeStruct((count, 1), f32)],
        compiler_params=params(),
        cost_estimate=cost(20 * count * model, 8 * count * model),
        name="gathered_norm",
    )(me, *operands)


def qkv_kernel(rows_ref, wq_ref, wk_ref, wv_ref, cos_ref, sin_ref, *out_refs):
    weight = jnp.concatenate([wq_ref[...], wk_ref[...], wv_ref[...]], axis=1)
    for first in range(0, rows_ref.shape[0], BLOCK):
        rows = pl.ds(first, BLOCK)
        pre = matmul(rows_ref[rows, :], weight)
        for part in range(3):
            piece = pre[:, part * HEAD_DIM : (part + 1) * HEAD_DIM]
            if part < 2:
                piece = piece * cos_ref[rows, :] + half_turn(piece) * sin_ref[rows, :]
            out_refs[part][rows, :] = piece.astype(bf16)


def head_specs(model, heads):
    return [
        pl.BlockSpec((model, HEAD_DIM), lambda h, part=part: (0, part * heads + h))
        for part in range(3)
    ]


def project_qkv(rows, weight, cosine, sine):
    count, model = rows.shape
    columns = weight.shape[1]
    heads = columns // (3 * HEAD_DIM)
    whole = lambda h: (0, 0)
    return pl.pallas_call(
        qkv_kernel,
        grid=(heads,),
        in_specs=[
            pl.BlockSpec((count, model), whole),
            *head_specs(model, heads),
            pl.BlockSpec((count, HEAD_DIM), whole),
            pl.BlockSpec((count, HEAD_DIM), whole),
        ],
        out_specs=[pl.BlockSpec((count, HEAD_DIM), lambda h: (0, h))] * 3,
        out_shape=[jax.ShapeDtypeStruct((count, heads * HEAD_DIM), bf16)] * 3,
        compiler_params=params(),
        cost_estimate=cost(2 * count * model * columns, 2 * model * (count + columns)),
        name="qkv",
    )(rows, weight, weight, weight, cosine, sine)


def masked_softmax(q_rows, k_rows, seg_column, seg_row, row_first):
    scores = times_transposed(q_rows, k_rows) * HEAD_DIM ** (-0.5)
    row = lax.broadcasted_iota(jnp.int32, scores.shape, 0) + row_first
    column = lax.broadcasted_iota(jnp.int32, scores.shape, 1)
    allowed = (seg_column == seg_row) & (column <= row)
    scores = jnp.where(allowed, scores, -1e30)
    exponent = jnp.exp(scores - jnp.max(scores, axis=-1, keepdims=True))
    return exponent * (1.0 / jnp.sum(exponent, axis=-1, keepdims=True))


PAIR = 2 * HEAD_DIM


def attend_kernel(q_ref, k_ref, v_ref, column_ref, row_ref, out_ref):
    block = pl.program_id(1)
    for index in range(k_ref.shape[0] // BLOCK):

        @pl.when(block == index)
        def _(index=index):
            seen = (index + 1) * BLOCK
            for first in range(0, PAIR, HEAD_DIM):
                head = slice(first, first + HEAD_DIM)
                prob = masked_softmax(
                    q_ref[:, head],
                    k_ref[:seen, head],
                    column_ref[...],
                    row_ref[:, :seen],
                    index * BLOCK,
                )
                out_ref[:, head] = matmul(prob.astype(bf16), v_ref[:seen, head]).astype(bf16)


def attend(qkv, segment):
    count, local = qkv[0].shape
    column = lambda h, i: (0, h)
    return pl.pallas_call(
        attend_kernel,
        grid=(local // PAIR, count // BLOCK),
        in_specs=[
            pl.BlockSpec((BLOCK, PAIR), lambda h, i: (i, h)),
            pl.BlockSpec((count, PAIR), column),
            pl.BlockSpec((count, PAIR), column),
            pl.BlockSpec((BLOCK, 1), lambda h, i: (i, 0)),
            pl.BlockSpec((1, count), lambda h, i: (0, 0)),
        ],
        out_specs=pl.BlockSpec((BLOCK, PAIR), lambda h, i: (i, h)),
        out_shape=jax.ShapeDtypeStruct((count, local), bf16),
        compiler_params=params(),
        cost_estimate=cost(4 * count * count * local, 8 * count * local, count * count * 4),
        name="attend",
    )(*qkv, *segment)


def attend_back_kernel(
    me_ref, q_ref, k_ref, v_ref, column_ref, row_ref, cos_ref, sin_ref, *refs
):
    *grad_refs, dq_ref, dk_ref, dv_ref, total = refs
    block = pl.program_id(1)
    scale = HEAD_DIM ** (-0.5)
    blocks = k_ref.shape[0] // BLOCK

    @pl.when(block == 0)
    def _():
        total[...] = jnp.zeros_like(total)

    for index in range(blocks):

        @pl.when(block == index)
        def _(index=index):
            seen = (index + 1) * BLOCK
            grads = picked(me_ref[0], index, grad_refs)
            for first in range(0, PAIR, HEAD_DIM):
                head = slice(first, first + HEAD_DIM)
                q_rows, k_rows, grad = q_ref[:, head], k_ref[:seen, head], grads[:, head]
                prob = masked_softmax(
                    q_rows, k_rows, column_ref[...], row_ref[:, :seen], index * BLOCK
                )
                prob_grad = times_transposed(grad, v_ref[:seen, head])
                delta = jnp.sum(prob_grad * prob, axis=-1, keepdims=True)
                score_grad = (prob * (prob_grad - delta)).astype(bf16)
                total[0, index * BLOCK : seen, head] = matmul(score_grad, k_rows) * scale
                total[1, :seen, head] += transposed_times(score_grad, q_rows) * scale
                total[2, :seen, head] += transposed_times(prob.astype(bf16), grad)

    @pl.when(block == blocks - 1)
    def _():
        for part, out_ref in enumerate((dq_ref, dk_ref, dv_ref)):
            for first in range(0, PAIR, HEAD_DIM):
                head = slice(first, first + HEAD_DIM)
                piece = total[part, :, head]
                if part < 2:
                    piece = piece * cos_ref[...] - half_turn(piece) * sin_ref[...]
                out_ref[:, head] = piece.astype(bf16)


def attend_back(me, qkv, grads, segment, cosine, sine):
    count, local = qkv[0].shape
    whole = lambda h, i, me: (0, 0)
    column = lambda h, i, me: (0, h)
    return pl.pallas_call(
        attend_back_kernel,
        grid_spec=pltpu.PrefetchScalarGridSpec(
            num_scalar_prefetch=1,
            grid=(local // PAIR, count // BLOCK),
            in_specs=[
                pl.BlockSpec((BLOCK, PAIR), lambda h, i, me: (i, h)),
                pl.BlockSpec((count, PAIR), column),
                pl.BlockSpec((count, PAIR), column),
                pl.BlockSpec((BLOCK, 1), lambda h, i, me: (i, 0)),
                pl.BlockSpec((1, count), whole),
                pl.BlockSpec((count, HEAD_DIM), whole),
                pl.BlockSpec((count, HEAD_DIM), whole),
                *[pl.BlockSpec((BLOCK, PAIR), column)] * len(grads),
            ],
            out_specs=[pl.BlockSpec((count, PAIR), column)] * 3,
            scratch_shapes=[pltpu.VMEM((3, count, PAIR), f32)],
        ),
        out_shape=[jax.ShapeDtypeStruct((count, local), bf16)] * 3,
        compiler_params=params(),
        cost_estimate=cost(1000, 1000),
        name="attend_back",
    )(me, *qkv, *segment, cosine, sine, *grads)


def hidden_kernel(me_ref, weight_ref, rows_ref, *refs):
    *come_refs, hidden_ref, normed_ref, inverse_ref = refs
    size = len(come_refs) // 2 + 1
    attended = jnp.concatenate([picked(me_ref[0], j, come_refs) for j in range(size)], axis=1)
    hidden = rows_ref[...].astype(f32) + matmul(attended, weight_ref[...])
    width = hidden_ref.shape[1]
    own = hidden[:, :width]
    for piece in range(1, size):
        own = jnp.where(me_ref[0] == piece, hidden[:, piece * width : (piece + 1) * width], own)
    hidden_ref[...] = own
    unit, inverse_ref[...] = norm_parts(hidden)
    normed_ref[...] = unit.astype(bf16)


def hidden_and_norm(me, own, arrived, weight, rows):
    count, model = rows.shape
    operands = flat(own, arrived)
    here = lambda i, me: (i, 0)
    return pl.pallas_call(
        hidden_kernel,
        grid_spec=pltpu.PrefetchScalarGridSpec(
            num_scalar_prefetch=1,
            grid=(count // BLOCK,),
            in_specs=[
                pl.BlockSpec((model, model), lambda i, me: (0, 0), pipeline_mode=pl.Buffered(1)),
                pl.BlockSpec((BLOCK, model), here),
                *[pl.BlockSpec((BLOCK, own.shape[1]), here)] * len(operands),
            ],
            out_specs=[
                pl.BlockSpec((BLOCK, own.shape[1]), here),
                pl.BlockSpec((BLOCK, model), here),
                pl.BlockSpec((BLOCK, 1), here),
            ],
        ),
        out_shape=[
            jax.ShapeDtypeStruct(own.shape, f32),
            jax.ShapeDtypeStruct((count, model), bf16),
            jax.ShapeDtypeStruct((count, 1), f32),
        ],
        compiler_params=params(),
        cost_estimate=cost(2 * count * model * model, 2 * model * model + 10 * count * model),
        name="hidden",
    )(me, weight, rows, *operands)


def up_kernel(rows_ref, gate_ref, up_ref, gate_out, up_out, act_ref):
    for first in range(0, rows_ref.shape[0], BLOCK):
        rows = pl.ds(first, BLOCK)
        gate = matmul(rows_ref[rows, :], gate_ref[0])
        up = matmul(rows_ref[rows, :], up_ref[0])
        sigmoid = 1.0 / (1.0 + jnp.exp(-gate))
        silu = gate * sigmoid
        gate_out[rows, :] = (up * (sigmoid + silu * (1.0 - sigmoid))).astype(bf16)
        up_out[rows, :] = silu.astype(bf16)
        act_ref[rows, :] = (silu * up).astype(bf16)


def mlp_up(rows, weights):
    count, model = rows.shape
    hidden_units = weights.shape[2]
    out = jax.ShapeDtypeStruct((count, hidden_units), bf16)
    return pl.pallas_call(
        up_kernel,
        grid=(hidden_units // WIDE,),
        in_specs=[
            pl.BlockSpec((count, model), lambda j: (0, 0)),
            pl.BlockSpec((1, model, WIDE), lambda j: (0, 0, j)),
            pl.BlockSpec((1, model, WIDE), lambda j: (1, 0, j)),
        ],
        out_specs=[pl.BlockSpec((count, WIDE), lambda j: (0, j))] * 3,
        out_shape=[out] * 3,
        compiler_params=params(),
        cost_estimate=cost(
            4 * count * model * hidden_units,
            4 * model * hidden_units + 2 * count * model + 10 * count * hidden_units,
            count * hidden_units,
        ),
        name="mlp_up",
    )(rows, weights, weights)


def down_back_kernel(me_ref, down_ref, gate_in, up_in, *refs):
    *come_refs, grad_ref, dgate_ref, dup_ref = refs
    size = len(come_refs) // 2 + 1
    width = come_refs[0].shape[1]

    @pl.when(pl.program_id(0) == 0)
    def _():
        for owner in range(size):
            grad_ref[:, owner * width : (owner + 1) * width] = picked(
                me_ref[0], owner, come_refs
            )

    for first in range(0, grad_ref.shape[0], BLOCK):
        rows = pl.ds(first, BLOCK)
        down = times_transposed(grad_ref[rows, :], down_ref[0])
        dgate_ref[rows, :] = (down * gate_in[rows, :].astype(f32)).astype(bf16)
        dup_ref[rows, :] = (down * up_in[rows, :].astype(f32)).astype(bf16)


def mlp_down_back(me, own, arrived, weights, gate, up):
    operands = flat(own, arrived)
    count, width = own.shape
    model = width * (len(operands) // 2 + 1)
    hidden_units = weights.shape[2]
    part = pl.BlockSpec((count, WIDE), lambda j, me: (0, j))
    whole = lambda j, me: (0, 0)
    out = jax.ShapeDtypeStruct((count, hidden_units), bf16)
    return pl.pallas_call(
        down_back_kernel,
        grid_spec=pltpu.PrefetchScalarGridSpec(
            num_scalar_prefetch=1,
            grid=(hidden_units // WIDE,),
            in_specs=[
                pl.BlockSpec((1, WIDE, model), lambda j, me: (2, j, 0)),
                part,
                part,
                *[pl.BlockSpec((count, width), whole, pipeline_mode=pl.Buffered(1))]
                * len(operands),
            ],
            out_specs=[pl.BlockSpec((count, model), whole), part, part],
        ),
        out_shape=[jax.ShapeDtypeStruct((count, model), bf16), out, out],
        compiler_params=params(),
        cost_estimate=cost(
            2 * count * model * hidden_units,
            2 * model * hidden_units + 2 * count * model + 12 * count * hidden_units,
            count * hidden_units,
        ),
        name="mlp_down_back",
    )(me, weights, gate, up, *operands)


def mlp_piece_kernel(order_ref, act_ref, down_ref, *out_refs):
    for piece, out_ref in enumerate(out_refs):

        @pl.when(pl.program_id(0) == piece)
        def _(out_ref=out_ref):
            for first in range(0, act_ref.shape[0], BLOCK):
                rows = pl.ds(first, BLOCK)
                out_ref[rows, :] = matmul(act_ref[rows, :], down_ref[0]).astype(bf16)


def mlp_pieces(order, act, weights, width):
    count, hidden_units = act.shape
    pieces = order.shape[0]
    whole = lambda g, order: (0, 0)
    return pl.pallas_call(
        mlp_piece_kernel,
        grid_spec=pltpu.PrefetchScalarGridSpec(
            num_scalar_prefetch=1,
            grid=(pieces,),
            in_specs=[
                pl.BlockSpec((count, hidden_units), whole, pipeline_mode=pl.Buffered(1)),
                pl.BlockSpec((1, hidden_units, width), lambda g, order: (2, 0, order[g])),
            ],
            out_specs=[pl.BlockSpec((count, width), whole)] * pieces,
        ),
        out_shape=[jax.ShapeDtypeStruct((count, width), bf16)] * pieces,
        compiler_params=params(),
        cost_estimate=cost(
            2 * pieces * count * width * hidden_units, 2 * pieces * width * hidden_units
        ),
        name="mlp_piece",
    )(order, act, weights)


def norm_back(unit_rows, inverse, grad_in):
    unit_rows = unit_rows.astype(f32)
    return inverse * (
        grad_in
        - jnp.mean(grad_in, axis=-1, keepdims=True)
        - unit_rows * jnp.mean(grad_in * unit_rows, axis=-1, keepdims=True)
    )


def put_at(place, value, refs):
    for index, ref in enumerate(refs):

        @pl.when(place == index)
        def _(ref=ref):
            ref[...] = value


def two_grad_kernel(order_ref, *refs):
    pieces = (len(refs) - 3) // 5
    row_refs = refs[: 4 * pieces]
    gate_ref, up_ref = refs[4 * pieces : 4 * pieces + 2]
    out_refs, total = refs[4 * pieces + 2 : -1], refs[-1]
    step = pl.program_id(0)
    columns = pl.ds(pl.multiple_of(step * WIDE, WIDE), WIDE)
    for piece in range(pieces):
        total[piece, :, columns] = times_transposed(
            row_refs[4 * piece][...], gate_ref[0]
        ) + times_transposed(row_refs[4 * piece + 1][...], up_ref[0])

    @pl.when(step == pl.num_programs(0) - 1)
    def _():
        for piece in range(pieces):
            out_refs[piece][...] = norm_back(
                row_refs[4 * piece + 2][...], row_refs[4 * piece + 3][...], total[piece]
            ).astype(bf16)


def two_grad_pieces(order, dgate, dup, weights, normed, inverse, quarter):
    pieces = order.shape[0]
    hidden_units = dgate.shape[1]
    model = weights.shape[1]
    rows = []
    for p in range(pieces):
        here = lambda j, order, p=p: (order[p], 0)
        rows += [pl.BlockSpec((quarter, hidden_units), here)] * 2
        rows += [pl.BlockSpec((quarter, model), here, pipeline_mode=pl.Buffered(1))]
        rows += [pl.BlockSpec((quarter, 1), here, pipeline_mode=pl.Buffered(1))]
    return pl.pallas_call(
        two_grad_kernel,
        grid_spec=pltpu.PrefetchScalarGridSpec(
            num_scalar_prefetch=1,
            grid=(model // WIDE,),
            in_specs=[
                *rows,
                pl.BlockSpec((1, WIDE, hidden_units), lambda j, order: (0, j, 0)),
                pl.BlockSpec((1, WIDE, hidden_units), lambda j, order: (1, j, 0)),
            ],
            out_specs=[pl.BlockSpec((quarter, model), lambda j, order: (0, 0))] * pieces,
            scratch_shapes=[pltpu.VMEM((pieces, quarter, model), f32)],
        ),
        out_shape=[jax.ShapeDtypeStruct((quarter, model), bf16)] * pieces,
        compiler_params=params(),
        cost_estimate=cost(
            4 * pieces * quarter * model * hidden_units, 4 * model * hidden_units
        ),
        name="two_grad",
    )(order, *([dgate, dup, normed, inverse] * pieces), weights, weights)


def one_grad_kernel(place_ref, dq_ref, dk_ref, dv_ref, weight_ref, unit_ref, inv_ref, *out_refs):
    columns = jnp.concatenate([dq_ref[...], dk_ref[...], dv_ref[...]], axis=1)
    grad = norm_back(
        unit_ref[...], inv_ref[...], times_transposed(columns, weight_ref[...])
    ).astype(bf16)
    width = out_refs[0].shape[1]
    for piece in range(len(out_refs)):
        put_at(place_ref[piece], grad[:, piece * width : (piece + 1) * width], out_refs)


def one_grad_pieces(place, grads, weight, rows, inverse):
    count, local = grads[0].shape
    columns = 3 * local
    pieces = place.shape[0]
    model = rows.shape[1]
    here = lambda i, place: (i, 0)
    return pl.pallas_call(
        one_grad_kernel,
        grid_spec=pltpu.PrefetchScalarGridSpec(
            num_scalar_prefetch=1,
            grid=(count // BLOCK,),
            in_specs=[
                *[pl.BlockSpec((BLOCK, local), here)] * 3,
                pl.BlockSpec(
                    (model, columns), lambda i, place: (0, 0), pipeline_mode=pl.Buffered(1)
                ),
                pl.BlockSpec((BLOCK, model), here),
                pl.BlockSpec((BLOCK, 1), here),
            ],
            out_specs=[pl.BlockSpec((BLOCK, model // pieces), here)] * pieces,
        ),
        out_shape=[jax.ShapeDtypeStruct((count, model // pieces), bf16)] * pieces,
        compiler_params=params(),
        cost_estimate=cost(
            2 * count * model * columns, 2 * columns * model + 6 * count * columns
        ),
        name="one_grad",
    )(place, *grads, weight, rows, inverse)


def att_grads_kernel(normed_ref, dq_ref, dk_ref, dv_ref, att_ref, hidden_ref, out_ref):
    owner = pl.program_id(0)
    columns = 3 * dq_ref.shape[1]
    grads = jnp.concatenate([dq_ref[...], dk_ref[...], dv_ref[...]], axis=1)
    out_ref[0, :, :columns] = transposed_times(normed_ref[...], grads).astype(bf16)
    model = hidden_ref.shape[1]
    rest = model - columns
    pieces = model // rest
    height = out_ref.shape[1] // pieces
    per_tile = HEAD_DIM // height
    product = transposed_times(att_ref[...], hidden_ref[...]).astype(bf16)
    for place in range(per_tile):

        @pl.when(lax.rem(owner, per_tile) == place)
        def _(place=place):
            for piece in range(pieces):
                out_ref[0, piece * height : (piece + 1) * height, columns:] = product[
                    place * height : (place + 1) * height, piece * rest : (piece + 1) * rest
                ]


def att_grads(normed, qkv_grad, attended, hidden_grad, groups):
    count, model = normed.shape
    local = attended.shape[1]
    columns = 3 * local
    tall = model // groups
    per_tile = HEAD_DIM // (local // groups)
    once = pl.Buffered(1)
    whole = lambda i: (0, 0)
    if tall % HEAD_DIM == 0:
        normed_spec = pl.BlockSpec((count, tall), lambda i: (0, i))
        operand = normed
    else:
        normed_spec = pl.BlockSpec((None, count, tall), lambda i: (i, 0, 0))
        operand = normed.reshape(count, groups, tall).swapaxes(0, 1)
    return pl.pallas_call(
        att_grads_kernel,
        grid=(groups,),
        in_specs=[
            normed_spec,
            *[pl.BlockSpec((count, local), whole, pipeline_mode=once)] * 3,
            pl.BlockSpec((count, HEAD_DIM), lambda i: (0, i // per_tile)),
            pl.BlockSpec((count, model), whole, pipeline_mode=once),
        ],
        out_specs=pl.BlockSpec((1, tall, model), lambda i: (i, 0, 0)),
        out_shape=jax.ShapeDtypeStruct((groups, tall, model), bf16),
        compiler_params=params(),
        cost_estimate=cost(1000, 1000),
        name="att_grads",
    )(operand, *qkv_grad, attended, hidden_grad)


def mlp_grads_kernel(*refs):
    *operands, out_ref = refs
    count = len(operands) // 2
    total = transposed_times(operands[0][...], operands[count][...])
    for part in range(1, count):
        total += transposed_times(operands[part][...], operands[count + part][...])
    out_ref[0] = total.astype(bf16)


def mlp_grads(which, left, right, before=None):
    rows = left[0].shape[0]
    model, hidden_units = left[0].shape[1], right[0].shape[1]
    once = pl.Buffered(1)
    specs = [pl.BlockSpec((rows, BLOCK), lambda i: (0, i)) for _ in left]
    specs += [
        pl.BlockSpec((rows, hidden_units), lambda i: (0, 0), pipeline_mode=once) for _ in right
    ]
    operands = [*left, *right]
    body = mlp_grads_kernel
    aliases = {}
    if before is not None:
        aliases = {len(operands): 0}
        specs.append(pl.BlockSpec(memory_space=pl.ANY))
        operands.append(before)
        body = lambda *refs: mlp_grads_kernel(*refs[:-2], refs[-1])
    count = rows * len(left)
    return pl.pallas_call(
        body,
        grid=(model // BLOCK,),
        in_specs=specs,
        out_specs=pl.BlockSpec((1, BLOCK, hidden_units), lambda i: (which, i, 0)),
        out_shape=jax.ShapeDtypeStruct((3, model, hidden_units), bf16),
        input_output_aliases=aliases,
        compiler_params=params(),
        cost_estimate=cost(
            2 * count * model * hidden_units, 2 * model * hidden_units + 4 * count * model
        ),
        name="mlp_grads",
    )(*operands)


def after(value, *others):
    return lax.optimization_barrier((value, *others))[0]


def line_step(block, axis, size, step):
    from_low, from_high = block
    up = [(i, i + 1) for i in range(step - 1, size - 1)]
    down = [(i, i - 1) for i in range(size - step, 0, -1)]
    return lax.ppermute(from_low, axis, up), lax.ppermute(from_high, axis, down)


def chain_gather(block, axis, size, begun=None):
    arrived = list(begun or [])
    for step in range(len(arrived) + 1, size):
        arrived.append(line_step(arrived[-1] if arrived else (block, block), axis, size, step))
    return arrived


def line_whole(own, arrived, axis, size):
    me = lax.axis_index(axis)
    low, high = [pair[0] for pair in arrived], [pair[1] for pair in arrived]
    return [pick(me, owner, own, low, high) for owner in range(size)]


def far_first(size):
    return sorted(range(1, size), key=lambda step: -min(step, size - step))


def sent_on(term, axis, size, step):
    return lax.ppermute(term, axis, [(i, (i + step) % size) for i in range(size)])


def added(own, came):
    for piece in came:
        own = own + piece.astype(f32)
    return own


def on_device(
    tokens,
    cotangent,
    w_query,
    w_key,
    w_value,
    w_out,
    w_gate,
    w_up,
    w_down,
    seq_lengths,
    deal,
    row_dest,
):
    groups = lax.axis_size("fsdp")
    shards = lax.axis_size("tp")
    own_group = lax.axis_index("fsdp")
    own_shard = lax.axis_index("tp")
    capacity = GROUP_CAP
    per_pair = capacity // groups
    quarter = capacity // shards
    head_dim = HEAD_DIM
    given, width = tokens.shape
    model = width * shards
    local_width = w_query.shape[1]
    shard_rows = w_query.shape[0]

    steps = far_first(shards)
    order = jnp.stack([lax.rem(own_shard + step, shards) for step in (*steps, 0)])
    around = jnp.stack([lax.rem(own_shard + step, shards) for step in range(shards)])
    place_of = [0] * shards
    for index, step in enumerate((*steps, 0)):
        place_of[step] = index
    place = jnp.stack(
        [
            sum(
                jnp.where(lax.rem(own_shard + step, shards) == j, place_of[step], 0)
                for step in range(shards)
            )
            for j in range(shards)
        ]
    )

    target = row_dest // capacity
    within = row_dest - target * capacity
    given_index = jnp.arange(given, dtype=jnp.int32)
    earlier = (target[:, None] == target[None, :]) & (
        given_index[None, :] < given_index[:, None]
    )
    slot_of = target * per_pair + jnp.sum(earlier.astype(jnp.int32), axis=1)
    slots = jnp.arange(capacity, dtype=jnp.int32)
    deal_hit = slots[:, None] == slot_of[None, :]
    deal_out = deal_hit.astype(bf16)
    place_high, place_low = (within + 1) // 32, (within + 1) % 32
    lane = jnp.arange(HEAD_DIM, dtype=jnp.int32)[None, :]
    place_columns = jnp.where(
        lane == 0, place_high[:, None], jnp.where(lane == 1, place_low[:, None], 0)
    ).astype(bf16)

    def over_fsdp(rows):
        return lax.all_to_all(rows, "fsdp", split_axis=0, concat_axis=0, tiled=True)

    sent_rows = matmul(deal_out, jnp.concatenate([tokens, place_columns], axis=1)).astype(bf16)
    sent_grads = matmul(deal_out, cotangent).astype(bf16)

    qkv_shard = jnp.concatenate([w_query, w_key, w_value], axis=1)
    full_qkv = lax.all_gather(qkv_shard, "fsdp", axis=0, tiled=True)
    out_came = [sent_on(w_out, "tp", shards, step) for step in range(1, shards)]
    came_rows = over_fsdp(sent_rows)
    mlp_shard = jnp.stack([w_gate, w_up, w_down])
    *out_came, came_rows, sent_grads, mlp_shard = lax.optimization_barrier(
        (*out_came, came_rows, sent_grads, mlp_shard)
    )
    came_place = came_rows[:, width : width + 2].astype(jnp.int32)
    recv_place = came_place[:, 0] * 32 + came_place[:, 1] - 1
    place_in = (slots[:, None] == recv_place[None, :]).astype(bf16)
    out_came = [w_out] + out_came
    out_rows = []
    for owner in range(shards):
        piece = w_out
        for step in range(1, shards):
            piece = jnp.where(own_shard == (owner + step) % shards, out_came[step], piece)
        out_rows.append(piece)
    out_rows = jnp.stack(out_rows)
    full_out = lax.all_gather(out_rows, "fsdp", axis=1, tiled=True).reshape(model, model)

    full_mlp = lax.all_gather(mlp_shard, "fsdp", axis=1, tiled=True)
    buffer_rows = matmul(place_in, came_rows[:, :width]).astype(bf16)
    buffer_grads = matmul(place_in, over_fsdp(after(sent_grads, buffer_rows))).astype(bf16)
    rows_come = chain_gather(buffer_rows, "tp", shards)
    list_index = jnp.sum(jnp.where(deal == own_group, jnp.arange(groups, dtype=jnp.int32), 0))
    lengths = lax.dynamic_index_in_dim(seq_lengths, list_index, 0, keepdims=False)
    segment, position = segments(lengths)
    cosine, sine = rope_tables(position, head_dim)
    segment_column, segment_row = segment[:, None], segment[None, :]
    rows_come[-1], first_grads, segment_column, segment_row, cosine, sine = (
        lax.optimization_barrier(
            (rows_come[-1], buffer_grads, segment_column, segment_row, cosine, sine)
        )
    )
    segment = (segment_column, segment_row)
    me = own_shard[None].astype(jnp.int32)

    full_rows, normed_one, inverse_one = gathered_norm(me, buffer_rows, rows_come)
    first_grads, normed_one = lax.optimization_barrier((first_grads, normed_one))
    grads_begun = line_step((first_grads, first_grads), "tp", shards, 1)
    qkv = project_qkv(normed_one, full_qkv, cosine, sine)
    attended = attend(qkv, segment)
    attended, *grads_begun = lax.optimization_barrier((attended, *grads_begun))
    att_come = chain_gather(attended, "tp", shards)
    *grads_begun, last_low, last_high = lax.optimization_barrier((*grads_begun, *att_come[-1]))
    att_come[-1] = (last_low, last_high)
    grads_come = [grads_begun, line_step(grads_begun, "tp", shards, 2)]
    hidden, normed_two, inverse_two = hidden_and_norm(me, attended, att_come, full_out, full_rows)
    *grads_come[1], normed_two = lax.optimization_barrier((*grads_come[1], normed_two))
    grads_come = chain_gather(first_grads, "tp", shards, grads_come)
    gate, up, activated = mlp_up(normed_two, full_mlp)
    def features_of(rows, owner):
        return lax.dynamic_slice_in_dim(rows, owner * width, width, 1)

    *last, activated = lax.optimization_barrier((*grads_come[-1], activated))
    grads_come[-1] = tuple(last)
    full_grads, gate_grad, up_grad = mlp_down_back(
        me, first_grads, grads_come, full_mlp, gate, up
    )

    def rows_of(rows, owner):
        return lax.dynamic_slice_in_dim(rows, owner * quarter, quarter, 0)

    two_first = two_grad_pieces(
        order[:1], gate_grad, up_grad, full_mlp, normed_two, inverse_two, quarter
    )
    two_rest = two_grad_pieces(
        order[1:], gate_grad, after(up_grad, *two_first), full_mlp, normed_two, inverse_two, quarter
    )
    two_came = [
        sent_on(term, "tp", shards, step)
        for term, step in zip((*two_first, *two_rest), steps)
    ]
    grad_mlp = mlp_grads(0, [normed_two], [after(gate_grad, *two_rest)])
    grad_mlp = mlp_grads(1, [normed_two], [up_grad], grad_mlp)
    grad_mlp = mlp_grads(2, [activated], [full_grads], grad_mlp)
    *two_came, grad_mlp = lax.optimization_barrier((*two_came, grad_mlp))
    sum_mlp = lax.psum_scatter(grad_mlp, "fsdp", scatter_dimension=1, tiled=True)
    back_low = added(
        rows_of(full_grads, own_shard).astype(f32) + two_rest[-1].astype(f32), two_came
    ).astype(bf16)
    back_come = [line_step((back_low, back_low), "tp", shards, 1)]
    own_out = lax.dynamic_slice_in_dim(full_out, own_shard * local_width, local_width, 0)

    def att_piece(block):
        return times_transposed(block, own_out).astype(bf16)

    def merged(step):
        low, high = back_come[step - 1]
        if 2 * step < shards:
            return low, high
        both = jnp.where(own_shard >= step, low, high)
        return both, both

    att_pieces = [att_piece(back_low)]
    terms = mlp_pieces(around, after(activated, grad_mlp, back_low), full_mlp, width)
    mlp_come = []
    for step in range(1, shards):
        back_come[-1], mlp_come, terms = lax.optimization_barrier(
            (back_come[-1], mlp_come, terms)
        )
        if step < shards - 1:
            back_come.append(line_step(back_come[-1], "tp", shards, step + 1))
            att_pieces += [att_piece(block) for block in merged(step)]
        low, high = terms[shards - step], terms[step]
        if mlp_come:
            low, high = (
                (term.astype(f32) + came.astype(f32)).astype(bf16)
                for term, came in zip((low, high), mlp_come)
            )
        up = [(i, i + 1) for i in range(step)]
        down = [(i, i - 1) for i in range(shards - 1, shards - 1 - step, -1)]
        mlp_come = [lax.ppermute(low, "tp", up), lax.ppermute(high, "tp", down)]
    att_pieces += [att_piece(block) for block in merged(shards - 1)]
    qkv_grad = attend_back(
        me,
        qkv,
        [att_pieces[0], *att_pieces[1::2], *att_pieces[2::2]],
        segment,
        cosine,
        sine,
    )
    one_terms = one_grad_pieces(place, qkv_grad, full_qkv, normed_one, inverse_one)
    one_came = [sent_on(term, "tp", shards, step) for term, step in zip(one_terms, steps)]
    full_hidden_grad = jnp.concatenate(
        line_whole(after(back_low, *one_terms[:3]), back_come, "tp", shards), axis=0
    )
    *mlp_come, late_grad, _ = lax.optimization_barrier(
        (*mlp_come, tuple(qkv_grad), tuple(one_terms[:3]))
    )
    grad_att = att_grads(
        normed_one, late_grad, attended, full_hidden_grad, groups
    )
    sum_mlp, grad_att = lax.optimization_barrier((sum_mlp, grad_att))
    sum_att = lax.psum_scatter(grad_att, "fsdp", scatter_dimension=0, tiled=False)

    sum_att = sum_att.astype(f32)
    out_part = sum_att[:, 3 * local_width :]
    out_pieces = model // out_part.shape[1]
    out_height = shard_rows // out_pieces
    sum_out = jnp.concatenate(
        [out_part[i * out_height : (i + 1) * out_height] for i in range(out_pieces)], axis=1
    )
    sum_gate, sum_up, sum_down = sum_mlp.astype(f32)
    back_here = added(one_terms[-1].astype(f32), one_came)
    input_here = features_of(full_hidden_grad, own_shard).astype(f32) + back_here
    output_here = hidden + added(terms[0].astype(f32), mlp_come)
    here = jnp.concatenate([output_here.astype(bf16), input_here.astype(bf16)], axis=1)
    sent_back = transposed_times(place_in, here).astype(bf16)
    sums = (
        sum_att[:, : local_width],
        sum_att[:, local_width : 2 * local_width],
        sum_att[:, 2 * local_width : 3 * local_width],
        sum_out,
        sum_gate,
        sum_up,
        sum_down,
    )
    came_back, *sums = lax.optimization_barrier((over_fsdp(sent_back), *sums))
    home = transposed_times(deal_out, came_back).astype(bf16)
    return (home[:, :width], home[:, width:], *sums)


def solution(mesh):
    in_specs = (
        P("fsdp", "tp"),
        P("fsdp", "tp"),
        P("fsdp", "tp"),
        P("fsdp", "tp"),
        P("fsdp", "tp"),
        P(("tp", "fsdp"), None),
        P("fsdp", "tp"),
        P("fsdp", "tp"),
        P(("tp", "fsdp"), None),
        P(),
        P(),
        P("fsdp"),
    )
    out_specs = (
        P("fsdp", "tp"),
        P("fsdp", "tp"),
        P("fsdp", "tp"),
        P("fsdp", "tp"),
        P("fsdp", "tp"),
        P(("tp", "fsdp"), None),
        P("fsdp", "tp"),
        P("fsdp", "tp"),
        P(("tp", "fsdp"), None),
    )
    return jax.shard_map(
        on_device, mesh=mesh, in_specs=in_specs, out_specs=out_specs, check_vma=False
    )
```

```python
import jax
import jax.numpy as jnp
from jax import lax
from jax.experimental import pallas as pl
from jax.experimental.pallas import tpu as pltpu
from jax.sharding import PartitionSpec as P

HEAD_DIM = 128
GROUP_CAP = 1024
SEQ_SLOTS = 4

norm_eps = 1e-05
rope_base = 10000.0
bf16 = jnp.bfloat16
f32 = jnp.float32


def matmul(left, right):
    return jnp.dot(left, right, preferred_element_type=f32)


def times_transposed(left, right):
    return lax.dot_general(
        left, right, (((1,), (1,)), ((), ())), preferred_element_type=f32
    )


def transposed_times(left, right):
    return lax.dot_general(
        left, right, (((0,), (0,)), ((), ())), preferred_element_type=f32
    )


def norm_parts(values_in):
    row_mean = jnp.mean(values_in, axis=-1, keepdims=True)
    centered = values_in - row_mean
    variance = jnp.mean(centered * centered, axis=-1, keepdims=True)
    inverse = lax.rsqrt(variance + norm_eps)
    return centered * inverse, inverse


def rope_tables(position, head_dim):
    half_dim = head_dim // 2
    frequency = rope_base ** (-(jnp.arange(half_dim, dtype=f32) * 2.0) / head_dim)
    angles = position.astype(f32)[:, None] * frequency[None, :]
    cosine, sine = jnp.cos(angles), jnp.sin(angles)
    return (
        jnp.concatenate([cosine, cosine], axis=1),
        jnp.concatenate([-sine, sine], axis=1),
    )


def segments(lengths):
    row_index = jnp.arange(GROUP_CAP, dtype=jnp.int32)
    slot_ids = jnp.arange(SEQ_SLOTS, dtype=jnp.int32)
    ends = jnp.sum(
        jnp.where(slot_ids[:, None] <= slot_ids[None, :], lengths[:, None], 0), axis=0
    )
    passed = row_index[:, None] >= ends[None, :]
    segment = jnp.sum(passed.astype(jnp.int32), axis=1)
    begin_row = jnp.max(jnp.where(passed, ends[None, :], 0), axis=1)
    return (segment, row_index - begin_row)


MIB = 1024 * 1024
BLOCK = 256
WIDE = 512


def params(mib=58):
    return pltpu.CompilerParams(vmem_limit_bytes=mib * MIB)


def cost(flops, read, transcendentals=0):
    return pl.CostEstimate(
        flops=int(flops), bytes_accessed=int(read), transcendentals=int(transcendentals)
    )


def half_turn(values_in):
    return pltpu.roll(values_in, HEAD_DIM // 2, 1)


def pick(me, owner, own, low, high):
    piece = own
    for step, (lower, higher) in enumerate(zip(low, high), start=1):
        piece = jnp.where(me == owner + step, lower, piece)
        piece = jnp.where(me == owner - step, higher, piece)
    return piece


def flat(own, arrived):
    return [own, *[low for low, _ in arrived], *[high for _, high in arrived]]


def picked(me, owner, refs):
    steps = len(refs) // 2
    blocks = [ref[...] for ref in refs]
    return pick(me, owner, blocks[0], blocks[1 : 1 + steps], blocks[1 + steps :])


def norm_kernel(me_ref, *refs):
    *come_refs, rows_ref, normed_ref, inverse_ref = refs
    size = len(come_refs) // 2 + 1
    rows = jnp.concatenate([picked(me_ref[0], j, come_refs) for j in range(size)], axis=1)
    rows_ref[...] = rows
    unit, inverse_ref[...] = norm_parts(rows.astype(f32))
    normed_ref[...] = unit.astype(bf16)


def gathered_norm(me, own, arrived):
    count, width = own.shape
    operands = flat(own, arrived)
    model = width * (len(operands) // 2 + 1)
    here = lambda i, me: (i, 0)
    out = jax.ShapeDtypeStruct((count, model), bf16)
    return pl.pallas_call(
        norm_kernel,
        grid_spec=pltpu.PrefetchScalarGridSpec(
            num_scalar_prefetch=1,
            grid=(count // BLOCK,),
            in_specs=[pl.BlockSpec((BLOCK, width), here)] * len(operands),
            out_specs=[
                pl.BlockSpec((BLOCK, model), here),
                pl.BlockSpec((BLOCK, model), here),
                pl.BlockSpec((BLOCK, 1), here),
            ],
        ),
        out_shape=[out, out, jax.ShapeDtypeStruct((count, 1), f32)],
        compiler_params=params(),
        cost_estimate=cost(20 * count * model, 8 * count * model),
        name="gathered_norm",
    )(me, *operands)


def qkv_kernel(rows_ref, wq_ref, wk_ref, wv_ref, cos_ref, sin_ref, *out_refs):
    weight = jnp.concatenate([wq_ref[...], wk_ref[...], wv_ref[...]], axis=1)
    for first in range(0, rows_ref.shape[0], BLOCK):
        rows = pl.ds(first, BLOCK)
        pre = matmul(rows_ref[rows, :], weight)
        for part in range(3):
            piece = pre[:, part * HEAD_DIM : (part + 1) * HEAD_DIM]
            if part < 2:
                piece = piece * cos_ref[rows, :] + half_turn(piece) * sin_ref[rows, :]
            out_refs[part][rows, :] = piece.astype(bf16)


def head_specs(model, heads):
    return [
        pl.BlockSpec((model, HEAD_DIM), lambda h, part=part: (0, part * heads + h))
        for part in range(3)
    ]


def project_qkv(rows, weight, cosine, sine):
    count, model = rows.shape
    columns = weight.shape[1]
    heads = columns // (3 * HEAD_DIM)
    whole = lambda h: (0, 0)
    return pl.pallas_call(
        qkv_kernel,
        grid=(heads,),
        in_specs=[
            pl.BlockSpec((count, model), whole),
            *head_specs(model, heads),
            pl.BlockSpec((count, HEAD_DIM), whole),
            pl.BlockSpec((count, HEAD_DIM), whole),
        ],
        out_specs=[pl.BlockSpec((count, HEAD_DIM), lambda h: (0, h))] * 3,
        out_shape=[jax.ShapeDtypeStruct((count, heads * HEAD_DIM), bf16)] * 3,
        compiler_params=params(),
        cost_estimate=cost(2 * count * model * columns, 2 * model * (count + columns)),
        name="qkv",
    )(rows, weight, weight, weight, cosine, sine)


def masked_softmax(q_rows, k_rows, seg_column, seg_row, row_first):
    scores = times_transposed(q_rows, k_rows) * HEAD_DIM ** (-0.5)
    row = lax.broadcasted_iota(jnp.int32, scores.shape, 0) + row_first
    column = lax.broadcasted_iota(jnp.int32, scores.shape, 1)
    allowed = (seg_column == seg_row) & (column <= row)
    scores = jnp.where(allowed, scores, -1e30)
    exponent = jnp.exp(scores - jnp.max(scores, axis=-1, keepdims=True))
    return exponent * (1.0 / jnp.sum(exponent, axis=-1, keepdims=True))


PAIR = 2 * HEAD_DIM


def attend_kernel(q_ref, k_ref, v_ref, column_ref, row_ref, out_ref):
    block = pl.program_id(1)
    for index in range(k_ref.shape[0] // BLOCK):

        @pl.when(block == index)
        def _(index=index):
            seen = (index + 1) * BLOCK
            for first in range(0, PAIR, HEAD_DIM):
                head = slice(first, first + HEAD_DIM)
                prob = masked_softmax(
                    q_ref[:, head],
                    k_ref[:seen, head],
                    column_ref[...],
                    row_ref[:, :seen],
                    index * BLOCK,
                )
                out_ref[:, head] = matmul(prob.astype(bf16), v_ref[:seen, head]).astype(bf16)


def attend(qkv, segment):
    count, local = qkv[0].shape
    column = lambda h, i: (0, h)
    return pl.pallas_call(
        attend_kernel,
        grid=(local // PAIR, count // BLOCK),
        in_specs=[
            pl.BlockSpec((BLOCK, PAIR), lambda h, i: (i, h)),
            pl.BlockSpec((count, PAIR), column),
            pl.BlockSpec((count, PAIR), column),
            pl.BlockSpec((BLOCK, 1), lambda h, i: (i, 0)),
            pl.BlockSpec((1, count), lambda h, i: (0, 0)),
        ],
        out_specs=pl.BlockSpec((BLOCK, PAIR), lambda h, i: (i, h)),
        out_shape=jax.ShapeDtypeStruct((count, local), bf16),
        compiler_params=params(),
        cost_estimate=cost(4 * count * count * local, 8 * count * local, count * count * 4),
        name="attend",
    )(*qkv, *segment)


def attend_back_kernel(
    me_ref, q_ref, k_ref, v_ref, column_ref, row_ref, cos_ref, sin_ref, *refs
):
    *grad_refs, dq_ref, dk_ref, dv_ref, total = refs
    block = pl.program_id(1)
    scale = HEAD_DIM ** (-0.5)
    blocks = k_ref.shape[0] // BLOCK

    @pl.when(block == 0)
    def _():
        total[...] = jnp.zeros_like(total)

    for index in range(blocks):

        @pl.when(block == index)
        def _(index=index):
            seen = (index + 1) * BLOCK
            grads = picked(me_ref[0], index, grad_refs)
            for first in range(0, PAIR, HEAD_DIM):
                head = slice(first, first + HEAD_DIM)
                q_rows, k_rows, grad = q_ref[:, head], k_ref[:seen, head], grads[:, head]
                prob = masked_softmax(
                    q_rows, k_rows, column_ref[...], row_ref[:, :seen], index * BLOCK
                )
                prob_grad = times_transposed(grad, v_ref[:seen, head])
                delta = jnp.sum(prob_grad * prob, axis=-1, keepdims=True)
                score_grad = (prob * (prob_grad - delta)).astype(bf16)
                total[0, index * BLOCK : seen, head] = matmul(score_grad, k_rows) * scale
                total[1, :seen, head] += transposed_times(score_grad, q_rows) * scale
                total[2, :seen, head] += transposed_times(prob.astype(bf16), grad)

    @pl.when(block == blocks - 1)
    def _():
        for part, out_ref in enumerate((dq_ref, dk_ref, dv_ref)):
            for first in range(0, PAIR, HEAD_DIM):
                head = slice(first, first + HEAD_DIM)
                piece = total[part, :, head]
                if part < 2:
                    piece = piece * cos_ref[...] - half_turn(piece) * sin_ref[...]
                out_ref[:, head] = piece.astype(bf16)


def attend_back(me, qkv, grads, segment, cosine, sine):
    count, local = qkv[0].shape
    whole = lambda h, i, me: (0, 0)
    column = lambda h, i, me: (0, h)
    return pl.pallas_call(
        attend_back_kernel,
        grid_spec=pltpu.PrefetchScalarGridSpec(
            num_scalar_prefetch=1,
            grid=(local // PAIR, count // BLOCK),
            in_specs=[
                pl.BlockSpec((BLOCK, PAIR), lambda h, i, me: (i, h)),
                pl.BlockSpec((count, PAIR), column),
                pl.BlockSpec((count, PAIR), column),
                pl.BlockSpec((BLOCK, 1), lambda h, i, me: (i, 0)),
                pl.BlockSpec((1, count), whole),
                pl.BlockSpec((count, HEAD_DIM), whole),
                pl.BlockSpec((count, HEAD_DIM), whole),
                *[pl.BlockSpec((BLOCK, PAIR), column)] * len(grads),
            ],
            out_specs=[pl.BlockSpec((count, PAIR), column)] * 3,
            scratch_shapes=[pltpu.VMEM((3, count, PAIR), f32)],
        ),
        out_shape=[jax.ShapeDtypeStruct((count, local), bf16)] * 3,
        compiler_params=params(32),
        cost_estimate=cost(1000, 1000),
        name="attend_back",
    )(me, *qkv, *segment, cosine, sine, *grads)


def hidden_kernel(me_ref, weight_ref, rows_ref, *refs):
    *come_refs, hidden_ref, normed_ref, inverse_ref = refs
    size = len(come_refs) // 2 + 1
    attended = jnp.concatenate([picked(me_ref[0], j, come_refs) for j in range(size)], axis=1)
    hidden = rows_ref[...].astype(f32) + matmul(attended, weight_ref[...])
    width = hidden_ref.shape[1]
    own = hidden[:, :width]
    for piece in range(1, size):
        own = jnp.where(me_ref[0] == piece, hidden[:, piece * width : (piece + 1) * width], own)
    hidden_ref[...] = own
    unit, inverse_ref[...] = norm_parts(hidden)
    normed_ref[...] = unit.astype(bf16)


def hidden_and_norm(me, own, arrived, weight, rows):
    count, model = rows.shape
    operands = flat(own, arrived)
    here = lambda i, me: (i, 0)
    return pl.pallas_call(
        hidden_kernel,
        grid_spec=pltpu.PrefetchScalarGridSpec(
            num_scalar_prefetch=1,
            grid=(count // BLOCK,),
            in_specs=[
                pl.BlockSpec((model, model), lambda i, me: (0, 0), pipeline_mode=pl.Buffered(1)),
                pl.BlockSpec((BLOCK, model), here),
                *[pl.BlockSpec((BLOCK, own.shape[1]), here)] * len(operands),
            ],
            out_specs=[
                pl.BlockSpec((BLOCK, own.shape[1]), here),
                pl.BlockSpec((BLOCK, model), here),
                pl.BlockSpec((BLOCK, 1), here),
            ],
        ),
        out_shape=[
            jax.ShapeDtypeStruct(own.shape, f32),
            jax.ShapeDtypeStruct((count, model), bf16),
            jax.ShapeDtypeStruct((count, 1), f32),
        ],
        compiler_params=params(),
        cost_estimate=cost(2 * count * model * model, 2 * model * model + 10 * count * model),
        name="hidden",
    )(me, weight, rows, *operands)


def up_kernel(rows_ref, gate_ref, up_ref, gate_out, up_out, act_ref):
    for first in range(0, rows_ref.shape[0], BLOCK):
        rows = pl.ds(first, BLOCK)
        gate = matmul(rows_ref[rows, :], gate_ref[0])
        up = matmul(rows_ref[rows, :], up_ref[0])
        sigmoid = 1.0 / (1.0 + jnp.exp(-gate))
        silu = gate * sigmoid
        gate_out[rows, :] = (up * (sigmoid + silu * (1.0 - sigmoid))).astype(bf16)
        up_out[rows, :] = silu.astype(bf16)
        act_ref[rows, :] = (silu * up).astype(bf16)


def mlp_up(rows, weights):
    count, model = rows.shape
    hidden_units = weights.shape[2]
    out = jax.ShapeDtypeStruct((count, hidden_units), bf16)
    return pl.pallas_call(
        up_kernel,
        grid=(hidden_units // WIDE,),
        in_specs=[
            pl.BlockSpec((count, model), lambda j: (0, 0)),
            pl.BlockSpec((1, model, WIDE), lambda j: (0, 0, j)),
            pl.BlockSpec((1, model, WIDE), lambda j: (1, 0, j)),
        ],
        out_specs=[pl.BlockSpec((count, WIDE), lambda j: (0, j))] * 3,
        out_shape=[out] * 3,
        compiler_params=params(),
        cost_estimate=cost(
            4 * count * model * hidden_units,
            4 * model * hidden_units + 2 * count * model + 10 * count * hidden_units,
            count * hidden_units,
        ),
        name="mlp_up",
    )(rows, weights, weights)


def down_back_kernel(me_ref, down_ref, gate_in, up_in, *refs):
    *come_refs, grad_ref, dgate_ref, dup_ref = refs
    size = len(come_refs) // 2 + 1
    width = come_refs[0].shape[1]

    @pl.when(pl.program_id(0) == 0)
    def _():
        for owner in range(size):
            grad_ref[:, owner * width : (owner + 1) * width] = picked(
                me_ref[0], owner, come_refs
            )

    for first in range(0, grad_ref.shape[0], BLOCK):
        rows = pl.ds(first, BLOCK)
        down = times_transposed(grad_ref[rows, :], down_ref[0])
        dgate_ref[rows, :] = (down * gate_in[rows, :].astype(f32)).astype(bf16)
        dup_ref[rows, :] = (down * up_in[rows, :].astype(f32)).astype(bf16)


def mlp_down_back(me, own, arrived, weights, gate, up):
    operands = flat(own, arrived)
    count, width = own.shape
    model = width * (len(operands) // 2 + 1)
    hidden_units = weights.shape[2]
    part = pl.BlockSpec((count, WIDE), lambda j, me: (0, j))
    whole = lambda j, me: (0, 0)
    out = jax.ShapeDtypeStruct((count, hidden_units), bf16)
    return pl.pallas_call(
        down_back_kernel,
        grid_spec=pltpu.PrefetchScalarGridSpec(
            num_scalar_prefetch=1,
            grid=(hidden_units // WIDE,),
            in_specs=[
                pl.BlockSpec((1, WIDE, model), lambda j, me: (2, j, 0)),
                part,
                part,
                *[pl.BlockSpec((count, width), whole, pipeline_mode=pl.Buffered(1))]
                * len(operands),
            ],
            out_specs=[pl.BlockSpec((count, model), whole), part, part],
        ),
        out_shape=[jax.ShapeDtypeStruct((count, model), bf16), out, out],
        compiler_params=params(),
        cost_estimate=cost(
            2 * count * model * hidden_units,
            2 * model * hidden_units + 2 * count * model + 12 * count * hidden_units,
            count * hidden_units,
        ),
        name="mlp_down_back",
    )(me, weights, gate, up, *operands)


def mlp_piece_kernel(order_ref, act_ref, down_ref, *out_refs):
    for piece, out_ref in enumerate(out_refs):

        @pl.when(pl.program_id(0) == piece)
        def _(out_ref=out_ref):
            for first in range(0, act_ref.shape[0], BLOCK):
                rows = pl.ds(first, BLOCK)
                out_ref[rows, :] = matmul(act_ref[rows, :], down_ref[0]).astype(bf16)


def mlp_pieces(order, act, weights, width):
    count, hidden_units = act.shape
    pieces = order.shape[0]
    whole = lambda g, order: (0, 0)
    return pl.pallas_call(
        mlp_piece_kernel,
        grid_spec=pltpu.PrefetchScalarGridSpec(
            num_scalar_prefetch=1,
            grid=(pieces,),
            in_specs=[
                pl.BlockSpec((count, hidden_units), whole, pipeline_mode=pl.Buffered(1)),
                pl.BlockSpec((1, hidden_units, width), lambda g, order: (2, 0, order[g])),
            ],
            out_specs=[pl.BlockSpec((count, width), whole)] * pieces,
        ),
        out_shape=[jax.ShapeDtypeStruct((count, width), bf16)] * pieces,
        compiler_params=params(32),
        cost_estimate=cost(
            2 * pieces * count * width * hidden_units, 2 * pieces * width * hidden_units
        ),
        name="mlp_piece",
    )(order, act, weights)


def norm_back(unit_rows, inverse, grad_in):
    unit_rows = unit_rows.astype(f32)
    return inverse * (
        grad_in
        - jnp.mean(grad_in, axis=-1, keepdims=True)
        - unit_rows * jnp.mean(grad_in * unit_rows, axis=-1, keepdims=True)
    )


def put_at(place, value, refs):
    for index, ref in enumerate(refs):

        @pl.when(place == index)
        def _(ref=ref):
            ref[...] = value


def two_grad_kernel(order_ref, *refs):
    pieces = (len(refs) - 3) // 5
    row_refs = refs[: 4 * pieces]
    gate_ref, up_ref = refs[4 * pieces : 4 * pieces + 2]
    out_refs, total = refs[4 * pieces + 2 : -1], refs[-1]
    step = pl.program_id(0)
    columns = pl.ds(pl.multiple_of(step * WIDE, WIDE), WIDE)
    for piece in range(pieces):
        total[piece, :, columns] = times_transposed(
            row_refs[4 * piece][...], gate_ref[0]
        ) + times_transposed(row_refs[4 * piece + 1][...], up_ref[0])

    @pl.when(step == pl.num_programs(0) - 1)
    def _():
        for piece in range(pieces):
            out_refs[piece][...] = norm_back(
                row_refs[4 * piece + 2][...], row_refs[4 * piece + 3][...], total[piece]
            ).astype(bf16)


def two_grad_pieces(order, dgate, dup, weights, normed, inverse, quarter):
    pieces = order.shape[0]
    hidden_units = dgate.shape[1]
    model = weights.shape[1]
    rows = []
    for p in range(pieces):
        here = lambda j, order, p=p: (order[p], 0)
        rows += [pl.BlockSpec((quarter, hidden_units), here)] * 2
        rows += [pl.BlockSpec((quarter, model), here, pipeline_mode=pl.Buffered(1))]
        rows += [pl.BlockSpec((quarter, 1), here, pipeline_mode=pl.Buffered(1))]
    return pl.pallas_call(
        two_grad_kernel,
        grid_spec=pltpu.PrefetchScalarGridSpec(
            num_scalar_prefetch=1,
            grid=(model // WIDE,),
            in_specs=[
                *rows,
                pl.BlockSpec((1, WIDE, hidden_units), lambda j, order: (0, j, 0)),
                pl.BlockSpec((1, WIDE, hidden_units), lambda j, order: (1, j, 0)),
            ],
            out_specs=[pl.BlockSpec((quarter, model), lambda j, order: (0, 0))] * pieces,
            scratch_shapes=[pltpu.VMEM((pieces, quarter, model), f32)],
        ),
        out_shape=[jax.ShapeDtypeStruct((quarter, model), bf16)] * pieces,
        compiler_params=params(),
        cost_estimate=cost(
            4 * pieces * quarter * model * hidden_units, 4 * model * hidden_units
        ),
        name="two_grad",
    )(order, *([dgate, dup, normed, inverse] * pieces), weights, weights)


def one_grad_kernel(place_ref, dq_ref, dk_ref, dv_ref, weight_ref, unit_ref, inv_ref, *out_refs):
    columns = jnp.concatenate([dq_ref[...], dk_ref[...], dv_ref[...]], axis=1)
    grad = norm_back(
        unit_ref[...], inv_ref[...], times_transposed(columns, weight_ref[...])
    ).astype(bf16)
    width = out_refs[0].shape[1]
    for piece in range(len(out_refs)):
        put_at(place_ref[piece], grad[:, piece * width : (piece + 1) * width], out_refs)


def one_grad_pieces(place, grads, weight, rows, inverse):
    count, local = grads[0].shape
    columns = 3 * local
    pieces = place.shape[0]
    model = rows.shape[1]
    here = lambda i, place: (i, 0)
    return pl.pallas_call(
        one_grad_kernel,
        grid_spec=pltpu.PrefetchScalarGridSpec(
            num_scalar_prefetch=1,
            grid=(count // BLOCK,),
            in_specs=[
                *[pl.BlockSpec((BLOCK, local), here)] * 3,
                pl.BlockSpec(
                    (model, columns), lambda i, place: (0, 0), pipeline_mode=pl.Buffered(1)
                ),
                pl.BlockSpec((BLOCK, model), here),
                pl.BlockSpec((BLOCK, 1), here),
            ],
            out_specs=[pl.BlockSpec((BLOCK, model // pieces), here)] * pieces,
        ),
        out_shape=[jax.ShapeDtypeStruct((count, model // pieces), bf16)] * pieces,
        compiler_params=params(32),
        cost_estimate=cost(
            2 * count * model * columns, 2 * columns * model + 6 * count * columns
        ),
        name="one_grad",
    )(place, *grads, weight, rows, inverse)


def att_grads_kernel(normed_ref, dq_ref, dk_ref, dv_ref, att_ref, hidden_ref, out_ref):
    owner = pl.program_id(0)
    columns = 3 * dq_ref.shape[1]
    grads = jnp.concatenate([dq_ref[...], dk_ref[...], dv_ref[...]], axis=1)
    out_ref[0, :, :columns] = transposed_times(normed_ref[...], grads).astype(bf16)
    model = hidden_ref.shape[1]
    rest = model - columns
    pieces = model // rest
    height = out_ref.shape[1] // pieces
    per_tile = HEAD_DIM // height
    product = transposed_times(att_ref[...], hidden_ref[...]).astype(bf16)
    for place in range(per_tile):

        @pl.when(lax.rem(owner, per_tile) == place)
        def _(place=place):
            for piece in range(pieces):
                out_ref[0, piece * height : (piece + 1) * height, columns:] = product[
                    place * height : (place + 1) * height, piece * rest : (piece + 1) * rest
                ]


def att_grads(normed, qkv_grad, attended, hidden_grad, groups):
    count, model = normed.shape
    local = attended.shape[1]
    columns = 3 * local
    tall = model // groups
    per_tile = HEAD_DIM // (local // groups)
    once = pl.Buffered(1)
    whole = lambda i: (0, 0)
    if tall % HEAD_DIM == 0:
        normed_spec = pl.BlockSpec((count, tall), lambda i: (0, i))
        operand = normed
    else:
        normed_spec = pl.BlockSpec((None, count, tall), lambda i: (i, 0, 0))
        operand = normed.reshape(count, groups, tall).swapaxes(0, 1)
    return pl.pallas_call(
        att_grads_kernel,
        grid=(groups,),
        in_specs=[
            normed_spec,
            *[pl.BlockSpec((count, local), whole, pipeline_mode=once)] * 3,
            pl.BlockSpec((count, HEAD_DIM), lambda i: (0, i // per_tile)),
            pl.BlockSpec((count, model), whole, pipeline_mode=once),
        ],
        out_specs=pl.BlockSpec((1, tall, model), lambda i: (i, 0, 0)),
        out_shape=jax.ShapeDtypeStruct((groups, tall, model), bf16),
        compiler_params=params(32),
        cost_estimate=cost(1000, 1000),
        name="att_grads",
    )(operand, *qkv_grad, attended, hidden_grad)


def mlp_grads_kernel(*refs):
    *operands, out_ref = refs
    count = len(operands) // 2
    total = transposed_times(operands[0][...], operands[count][...])
    for part in range(1, count):
        total += transposed_times(operands[part][...], operands[count + part][...])
    out_ref[0] = total.astype(bf16)


def mlp_grads(which, left, right, before=None):
    rows = left[0].shape[0]
    model, hidden_units = left[0].shape[1], right[0].shape[1]
    once = pl.Buffered(1)
    specs = [pl.BlockSpec((rows, BLOCK), lambda i: (0, i)) for _ in left]
    specs += [
        pl.BlockSpec((rows, hidden_units), lambda i: (0, 0), pipeline_mode=once) for _ in right
    ]
    operands = [*left, *right]
    body = mlp_grads_kernel
    aliases = {}
    if before is not None:
        aliases = {len(operands): 0}
        specs.append(pl.BlockSpec(memory_space=pl.ANY))
        operands.append(before)
        body = lambda *refs: mlp_grads_kernel(*refs[:-2], refs[-1])
    count = rows * len(left)
    return pl.pallas_call(
        body,
        grid=(model // BLOCK,),
        in_specs=specs,
        out_specs=pl.BlockSpec((1, BLOCK, hidden_units), lambda i: (which, i, 0)),
        out_shape=jax.ShapeDtypeStruct((3, model, hidden_units), bf16),
        input_output_aliases=aliases,
        compiler_params=params(32),
        cost_estimate=cost(
            2 * count * model * hidden_units, 2 * model * hidden_units + 4 * count * model
        ),
        name="mlp_grads",
    )(*operands)


def after(value, *others):
    return lax.optimization_barrier((value, *others))[0]


def line_step(block, axis, size, step):
    from_low, from_high = block
    up = [(i, i + 1) for i in range(step - 1, size - 1)]
    down = [(i, i - 1) for i in range(size - step, 0, -1)]
    return lax.ppermute(from_low, axis, up), lax.ppermute(from_high, axis, down)


def chain_gather(block, axis, size, begun=None):
    arrived = list(begun or [])
    for step in range(len(arrived) + 1, size):
        arrived.append(line_step(arrived[-1] if arrived else (block, block), axis, size, step))
    return arrived


def line_whole(own, arrived, axis, size):
    me = lax.axis_index(axis)
    low, high = [pair[0] for pair in arrived], [pair[1] for pair in arrived]
    return [pick(me, owner, own, low, high) for owner in range(size)]


def far_first(size):
    return sorted(range(1, size), key=lambda step: -min(step, size - step))


def sent_on(term, axis, size, step):
    return lax.ppermute(term, axis, [(i, (i + step) % size) for i in range(size)])


def added(own, came):
    for piece in came:
        own = own + piece.astype(f32)
    return own


def on_device(
    tokens,
    cotangent,
    w_query,
    w_key,
    w_value,
    w_out,
    w_gate,
    w_up,
    w_down,
    seq_lengths,
    deal,
    row_dest,
):
    groups = lax.axis_size("fsdp")
    shards = lax.axis_size("tp")
    own_group = lax.axis_index("fsdp")
    own_shard = lax.axis_index("tp")
    capacity = GROUP_CAP
    per_pair = capacity // groups
    quarter = capacity // shards
    head_dim = HEAD_DIM
    given, width = tokens.shape
    model = width * shards
    local_width = w_query.shape[1]
    shard_rows = w_query.shape[0]

    steps = far_first(shards)
    order = jnp.stack([lax.rem(own_shard + step, shards) for step in (*steps, 0)])
    around = jnp.stack([lax.rem(own_shard + step, shards) for step in range(shards)])
    place_of = [0] * shards
    for index, step in enumerate((*steps, 0)):
        place_of[step] = index
    place = jnp.stack(
        [
            sum(
                jnp.where(lax.rem(own_shard + step, shards) == j, place_of[step], 0)
                for step in range(shards)
            )
            for j in range(shards)
        ]
    )

    target = row_dest // capacity
    within = row_dest - target * capacity
    given_index = jnp.arange(given, dtype=jnp.int32)
    earlier = (target[:, None] == target[None, :]) & (
        given_index[None, :] < given_index[:, None]
    )
    slot_of = target * per_pair + jnp.sum(earlier.astype(jnp.int32), axis=1)
    slots = jnp.arange(capacity, dtype=jnp.int32)
    deal_hit = slots[:, None] == slot_of[None, :]
    deal_out = deal_hit.astype(bf16)
    place_high, place_low = (within + 1) // 32, (within + 1) % 32
    lane = jnp.arange(HEAD_DIM, dtype=jnp.int32)[None, :]
    place_columns = jnp.where(
        lane == 0, place_high[:, None], jnp.where(lane == 1, place_low[:, None], 0)
    ).astype(bf16)

    def over_fsdp(rows):
        return lax.all_to_all(rows, "fsdp", split_axis=0, concat_axis=0, tiled=True)

    sent_rows = matmul(deal_out, jnp.concatenate([tokens, place_columns], axis=1)).astype(bf16)
    sent_grads = matmul(deal_out, cotangent).astype(bf16)

    qkv_shard = jnp.concatenate([w_query, w_key, w_value], axis=1)
    full_qkv = lax.all_gather(qkv_shard, "fsdp", axis=0, tiled=True)
    out_came = [sent_on(w_out, "tp", shards, step) for step in range(1, shards)]
    came_rows = over_fsdp(sent_rows)
    mlp_shard = jnp.stack([w_gate, w_up, w_down])
    *out_came, came_rows, sent_grads, mlp_shard = lax.optimization_barrier(
        (*out_came, came_rows, sent_grads, mlp_shard)
    )
    came_place = came_rows[:, width : width + 2].astype(jnp.int32)
    recv_place = came_place[:, 0] * 32 + came_place[:, 1] - 1
    place_in = (slots[:, None] == recv_place[None, :]).astype(bf16)
    out_came = [w_out] + out_came
    out_rows = []
    for owner in range(shards):
        piece = w_out
        for step in range(1, shards):
            piece = jnp.where(own_shard == (owner + step) % shards, out_came[step], piece)
        out_rows.append(piece)
    out_rows = jnp.stack(out_rows)
    full_out = lax.all_gather(out_rows, "fsdp", axis=1, tiled=True).reshape(model, model)

    full_mlp = lax.all_gather(mlp_shard, "fsdp", axis=1, tiled=True)
    buffer_rows = matmul(place_in, came_rows[:, :width]).astype(bf16)
    buffer_grads = matmul(place_in, over_fsdp(after(sent_grads, buffer_rows))).astype(bf16)
    rows_come = chain_gather(buffer_rows, "tp", shards)
    list_index = jnp.sum(jnp.where(deal == own_group, jnp.arange(groups, dtype=jnp.int32), 0))
    lengths = lax.dynamic_index_in_dim(seq_lengths, list_index, 0, keepdims=False)
    segment, position = segments(lengths)
    cosine, sine = rope_tables(position, head_dim)
    segment_column, segment_row = segment[:, None], segment[None, :]
    rows_come[-1], first_grads, segment_column, segment_row, cosine, sine = (
        lax.optimization_barrier(
            (rows_come[-1], buffer_grads, segment_column, segment_row, cosine, sine)
        )
    )
    segment = (segment_column, segment_row)
    me = own_shard[None].astype(jnp.int32)

    full_rows, normed_one, inverse_one = gathered_norm(me, buffer_rows, rows_come)
    first_grads, normed_one = lax.optimization_barrier((first_grads, normed_one))
    grads_begun = line_step((first_grads, first_grads), "tp", shards, 1)
    qkv = project_qkv(normed_one, full_qkv, cosine, sine)
    attended = attend(qkv, segment)
    attended, *grads_begun = lax.optimization_barrier((attended, *grads_begun))
    att_come = chain_gather(attended, "tp", shards)
    *grads_begun, last_low, last_high = lax.optimization_barrier((*grads_begun, *att_come[-1]))
    att_come[-1] = (last_low, last_high)
    grads_come = [grads_begun, line_step(grads_begun, "tp", shards, 2)]
    hidden, normed_two, inverse_two = hidden_and_norm(me, attended, att_come, full_out, full_rows)
    *grads_come[1], normed_two = lax.optimization_barrier((*grads_come[1], normed_two))
    grads_come = chain_gather(first_grads, "tp", shards, grads_come)
    gate, up, activated = mlp_up(normed_two, full_mlp)
    def features_of(rows, owner):
        return lax.dynamic_slice_in_dim(rows, owner * width, width, 1)

    *last, activated = lax.optimization_barrier((*grads_come[-1], activated))
    grads_come[-1] = tuple(last)
    full_grads, gate_grad, up_grad = mlp_down_back(
        me, first_grads, grads_come, full_mlp, gate, up
    )

    def rows_of(rows, owner):
        return lax.dynamic_slice_in_dim(rows, owner * quarter, quarter, 0)

    two_first = two_grad_pieces(
        order[:1], gate_grad, up_grad, full_mlp, normed_two, inverse_two, quarter
    )
    two_rest = two_grad_pieces(
        order[1:], gate_grad, after(up_grad, *two_first), full_mlp, normed_two, inverse_two, quarter
    )
    two_came = [
        sent_on(term, "tp", shards, step)
        for term, step in zip((*two_first, *two_rest), steps)
    ]
    grad_mlp = mlp_grads(0, [normed_two], [after(gate_grad, *two_rest)])
    grad_mlp = mlp_grads(1, [normed_two], [up_grad], grad_mlp)
    grad_mlp = mlp_grads(2, [activated], [full_grads], grad_mlp)
    *two_came, grad_mlp = lax.optimization_barrier((*two_came, grad_mlp))
    sum_mlp = lax.psum_scatter(grad_mlp, "fsdp", scatter_dimension=1, tiled=True)
    back_low = added(
        rows_of(full_grads, own_shard).astype(f32) + two_rest[-1].astype(f32), two_came
    ).astype(bf16)
    back_come = [line_step((back_low, back_low), "tp", shards, 1)]
    own_out = lax.dynamic_slice_in_dim(full_out, own_shard * local_width, local_width, 0)

    def att_piece(block):
        return times_transposed(block, own_out).astype(bf16)

    def merged(step):
        low, high = back_come[step - 1]
        if 2 * step < shards:
            return low, high
        both = jnp.where(own_shard >= step, low, high)
        return both, both

    att_pieces = [att_piece(back_low)]
    terms = mlp_pieces(around, after(activated, grad_mlp, back_low), full_mlp, width)
    mlp_come = []
    for step in range(1, shards):
        back_come[-1], mlp_come, terms = lax.optimization_barrier(
            (back_come[-1], mlp_come, terms)
        )
        if step < shards - 1:
            back_come.append(line_step(back_come[-1], "tp", shards, step + 1))
            att_pieces += [att_piece(block) for block in merged(step)]
        low, high = terms[shards - step], terms[step]
        if mlp_come:
            low, high = (
                (term.astype(f32) + came.astype(f32)).astype(bf16)
                for term, came in zip((low, high), mlp_come)
            )
        up = [(i, i + 1) for i in range(step)]
        down = [(i, i - 1) for i in range(shards - 1, shards - 1 - step, -1)]
        mlp_come = [lax.ppermute(low, "tp", up), lax.ppermute(high, "tp", down)]
    att_pieces += [att_piece(block) for block in merged(shards - 1)]
    qkv_grad = attend_back(
        me,
        qkv,
        [att_pieces[0], *att_pieces[1::2], *att_pieces[2::2]],
        segment,
        cosine,
        sine,
    )
    one_terms = one_grad_pieces(place, qkv_grad, full_qkv, normed_one, inverse_one)
    one_came = [sent_on(term, "tp", shards, step) for term, step in zip(one_terms, steps)]
    full_hidden_grad = jnp.concatenate(
        line_whole(after(back_low, *one_terms[:3]), back_come, "tp", shards), axis=0
    )
    *mlp_come, late_grad, _ = lax.optimization_barrier(
        (*mlp_come, tuple(qkv_grad), tuple(one_terms[:3]))
    )
    grad_att = att_grads(
        normed_one, late_grad, attended, full_hidden_grad, groups
    )
    sum_mlp, grad_att = lax.optimization_barrier((sum_mlp, grad_att))
    sum_att = lax.psum_scatter(grad_att, "fsdp", scatter_dimension=0, tiled=False)

    sum_att = sum_att.astype(f32)
    out_part = sum_att[:, 3 * local_width :]
    out_pieces = model // out_part.shape[1]
    out_height = shard_rows // out_pieces
    sum_out = jnp.concatenate(
        [out_part[i * out_height : (i + 1) * out_height] for i in range(out_pieces)], axis=1
    )
    sum_gate, sum_up, sum_down = sum_mlp.astype(f32)
    back_here = added(one_terms[-1].astype(f32), one_came)
    input_here = features_of(full_hidden_grad, own_shard).astype(f32) + back_here
    output_here = hidden + added(terms[0].astype(f32), mlp_come)
    here = jnp.concatenate([output_here.astype(bf16), input_here.astype(bf16)], axis=1)
    sent_back = transposed_times(place_in, here).astype(bf16)
    sums = (
        sum_att[:, : local_width],
        sum_att[:, local_width : 2 * local_width],
        sum_att[:, 2 * local_width : 3 * local_width],
        sum_out,
        sum_gate,
        sum_up,
        sum_down,
    )
    came_back, *sums = lax.optimization_barrier((over_fsdp(sent_back), *sums))
    home = transposed_times(deal_out, came_back).astype(bf16)
    return (home[:, :width], home[:, width:], *sums)


def solution(mesh):
    in_specs = (
        P("fsdp", "tp"),
        P("fsdp", "tp"),
        P("fsdp", "tp"),
        P("fsdp", "tp"),
        P("fsdp", "tp"),
        P(("tp", "fsdp"), None),
        P("fsdp", "tp"),
        P("fsdp", "tp"),
        P(("tp", "fsdp"), None),
        P(),
        P(),
        P("fsdp"),
    )
    out_specs = (
        P("fsdp", "tp"),
        P("fsdp", "tp"),
        P("fsdp", "tp"),
        P("fsdp", "tp"),
        P("fsdp", "tp"),
        P(("tp", "fsdp"), None),
        P("fsdp", "tp"),
        P("fsdp", "tp"),
        P(("tp", "fsdp"), None),
    )
    return jax.shard_map(
        on_device, mesh=mesh, in_specs=in_specs, out_specs=out_specs, check_vma=False
    )
```

```python
import jax
import jax.numpy as jnp
from jax import lax
from jax.experimental import pallas as pl
from jax.experimental.pallas import tpu as pltpu
from jax.sharding import PartitionSpec as P

HEAD_DIM = 128
GROUP_CAP = 1024
SEQ_SLOTS = 4

norm_eps = 1e-05
rope_base = 10000.0
bf16 = jnp.bfloat16
f32 = jnp.float32


def matmul(left, right):
    return jnp.dot(left, right, preferred_element_type=f32)


def times_transposed(left, right):
    return lax.dot_general(
        left, right, (((1,), (1,)), ((), ())), preferred_element_type=f32
    )


def transposed_times(left, right):
    return lax.dot_general(
        left, right, (((0,), (0,)), ((), ())), preferred_element_type=f32
    )


def norm_parts(values_in):
    row_mean = jnp.mean(values_in, axis=-1, keepdims=True)
    centered = values_in - row_mean
    variance = jnp.mean(centered * centered, axis=-1, keepdims=True)
    inverse = lax.rsqrt(variance + norm_eps)
    return centered * inverse, inverse


def rope_tables(position, head_dim):
    half_dim = head_dim // 2
    frequency = rope_base ** (-(jnp.arange(half_dim, dtype=f32) * 2.0) / head_dim)
    angles = position.astype(f32)[:, None] * frequency[None, :]
    cosine, sine = jnp.cos(angles), jnp.sin(angles)
    return (
        jnp.concatenate([cosine, cosine], axis=1),
        jnp.concatenate([-sine, sine], axis=1),
    )


def segments(lengths):
    row_index = jnp.arange(GROUP_CAP, dtype=jnp.int32)
    slot_ids = jnp.arange(SEQ_SLOTS, dtype=jnp.int32)
    ends = jnp.sum(
        jnp.where(slot_ids[:, None] <= slot_ids[None, :], lengths[:, None], 0), axis=0
    )
    passed = row_index[:, None] >= ends[None, :]
    segment = jnp.sum(passed.astype(jnp.int32), axis=1)
    begin_row = jnp.max(jnp.where(passed, ends[None, :], 0), axis=1)
    return (segment, row_index - begin_row)


MIB = 1024 * 1024
BLOCK = 256
WIDE = 512


def params(mib=58):
    return pltpu.CompilerParams(vmem_limit_bytes=mib * MIB)


def cost(flops, read, transcendentals=0):
    return pl.CostEstimate(
        flops=int(flops), bytes_accessed=int(read), transcendentals=int(transcendentals)
    )


def half_turn(values_in):
    return pltpu.roll(values_in, HEAD_DIM // 2, 1)


def pick(me, owner, own, low, high):
    piece = own
    for step, (lower, higher) in enumerate(zip(low, high), start=1):
        piece = jnp.where(me == owner + step, lower, piece)
        piece = jnp.where(me == owner - step, higher, piece)
    return piece


def flat(own, arrived):
    return [own, *[low for low, _ in arrived], *[high for _, high in arrived]]


def picked(me, owner, refs):
    steps = len(refs) // 2
    blocks = [ref[...] for ref in refs]
    return pick(me, owner, blocks[0], blocks[1 : 1 + steps], blocks[1 + steps :])


def norm_kernel(me_ref, *refs):
    *come_refs, rows_ref, normed_ref, inverse_ref = refs
    size = len(come_refs) // 2 + 1
    rows = jnp.concatenate([picked(me_ref[0], j, come_refs) for j in range(size)], axis=1)
    rows_ref[...] = rows
    unit, inverse_ref[...] = norm_parts(rows.astype(f32))
    normed_ref[...] = unit.astype(bf16)


def gathered_norm(me, own, arrived):
    count, width = own.shape
    operands = flat(own, arrived)
    model = width * (len(operands) // 2 + 1)
    here = lambda i, me: (i, 0)
    out = jax.ShapeDtypeStruct((count, model), bf16)
    return pl.pallas_call(
        norm_kernel,
        grid_spec=pltpu.PrefetchScalarGridSpec(
            num_scalar_prefetch=1,
            grid=(count // BLOCK,),
            in_specs=[pl.BlockSpec((BLOCK, width), here)] * len(operands),
            out_specs=[
                pl.BlockSpec((BLOCK, model), here),
                pl.BlockSpec((BLOCK, model), here),
                pl.BlockSpec((BLOCK, 1), here),
            ],
        ),
        out_shape=[out, out, jax.ShapeDtypeStruct((count, 1), f32)],
        compiler_params=params(),
        cost_estimate=cost(20 * count * model, 8 * count * model),
        name="gathered_norm",
    )(me, *operands)


def qkv_kernel(rows_ref, wq_ref, wk_ref, wv_ref, cos_ref, sin_ref, *out_refs):
    weight = jnp.concatenate([wq_ref[...], wk_ref[...], wv_ref[...]], axis=1)
    for first in range(0, rows_ref.shape[0], BLOCK):
        rows = pl.ds(first, BLOCK)
        pre = matmul(rows_ref[rows, :], weight)
        for part in range(3):
            piece = pre[:, part * HEAD_DIM : (part + 1) * HEAD_DIM]
            if part < 2:
                piece = piece * cos_ref[rows, :] + half_turn(piece) * sin_ref[rows, :]
            out_refs[part][rows, :] = piece.astype(bf16)


def head_specs(model, heads):
    return [
        pl.BlockSpec((model, HEAD_DIM), lambda h, part=part: (0, part * heads + h))
        for part in range(3)
    ]


def project_qkv(rows, weight, cosine, sine):
    count, model = rows.shape
    columns = weight.shape[1]
    heads = columns // (3 * HEAD_DIM)
    whole = lambda h: (0, 0)
    return pl.pallas_call(
        qkv_kernel,
        grid=(heads,),
        in_specs=[
            pl.BlockSpec((count, model), whole),
            *head_specs(model, heads),
            pl.BlockSpec((count, HEAD_DIM), whole),
            pl.BlockSpec((count, HEAD_DIM), whole),
        ],
        out_specs=[pl.BlockSpec((count, HEAD_DIM), lambda h: (0, h))] * 3,
        out_shape=[jax.ShapeDtypeStruct((count, heads * HEAD_DIM), bf16)] * 3,
        compiler_params=params(),
        cost_estimate=cost(2 * count * model * columns, 2 * model * (count + columns)),
        name="qkv",
    )(rows, weight, weight, weight, cosine, sine)


def masked_softmax(q_rows, k_rows, seg_column, seg_row, row_first):
    scores = times_transposed(q_rows, k_rows) * HEAD_DIM ** (-0.5)
    row = lax.broadcasted_iota(jnp.int32, scores.shape, 0) + row_first
    column = lax.broadcasted_iota(jnp.int32, scores.shape, 1)
    allowed = (seg_column == seg_row) & (column <= row)
    scores = jnp.where(allowed, scores, -1e30)
    exponent = jnp.exp(scores - jnp.max(scores, axis=-1, keepdims=True))
    return exponent * (1.0 / jnp.sum(exponent, axis=-1, keepdims=True))


PAIR = 2 * HEAD_DIM


def attend_kernel(q_ref, k_ref, v_ref, column_ref, row_ref, out_ref):
    block = pl.program_id(1)
    for index in range(k_ref.shape[0] // BLOCK):

        @pl.when(block == index)
        def _(index=index):
            seen = (index + 1) * BLOCK
            for first in range(0, PAIR, HEAD_DIM):
                head = slice(first, first + HEAD_DIM)
                prob = masked_softmax(
                    q_ref[:, head],
                    k_ref[:seen, head],
                    column_ref[...],
                    row_ref[:, :seen],
                    index * BLOCK,
                )
                out_ref[:, head] = matmul(prob.astype(bf16), v_ref[:seen, head]).astype(bf16)


def attend(qkv, segment):
    count, local = qkv[0].shape
    column = lambda h, i: (0, h)
    return pl.pallas_call(
        attend_kernel,
        grid=(local // PAIR, count // BLOCK),
        in_specs=[
            pl.BlockSpec((BLOCK, PAIR), lambda h, i: (i, h)),
            pl.BlockSpec((count, PAIR), column),
            pl.BlockSpec((count, PAIR), column),
            pl.BlockSpec((BLOCK, 1), lambda h, i: (i, 0)),
            pl.BlockSpec((1, count), lambda h, i: (0, 0)),
        ],
        out_specs=pl.BlockSpec((BLOCK, PAIR), lambda h, i: (i, h)),
        out_shape=jax.ShapeDtypeStruct((count, local), bf16),
        compiler_params=params(),
        cost_estimate=cost(4 * count * count * local, 8 * count * local, count * count * 4),
        name="attend",
    )(*qkv, *segment)


def attend_back_kernel(
    me_ref, q_ref, k_ref, v_ref, column_ref, row_ref, cos_ref, sin_ref, *refs
):
    *grad_refs, dq_ref, dk_ref, dv_ref, total = refs
    block = pl.program_id(1)
    scale = HEAD_DIM ** (-0.5)
    blocks = k_ref.shape[0] // BLOCK

    @pl.when(block == 0)
    def _():
        total[...] = jnp.zeros_like(total)

    for index in range(blocks):

        @pl.when(block == index)
        def _(index=index):
            seen = (index + 1) * BLOCK
            grads = picked(me_ref[0], index, grad_refs)
            for first in range(0, PAIR, HEAD_DIM):
                head = slice(first, first + HEAD_DIM)
                q_rows, k_rows, grad = q_ref[:, head], k_ref[:seen, head], grads[:, head]
                prob = masked_softmax(
                    q_rows, k_rows, column_ref[...], row_ref[:, :seen], index * BLOCK
                )
                prob_grad = times_transposed(grad, v_ref[:seen, head])
                delta = jnp.sum(prob_grad * prob, axis=-1, keepdims=True)
                score_grad = (prob * (prob_grad - delta)).astype(bf16)
                total[0, index * BLOCK : seen, head] = matmul(score_grad, k_rows) * scale
                total[1, :seen, head] += transposed_times(score_grad, q_rows) * scale
                total[2, :seen, head] += transposed_times(prob.astype(bf16), grad)

    @pl.when(block == blocks - 1)
    def _():
        for part, out_ref in enumerate((dq_ref, dk_ref, dv_ref)):
            for first in range(0, PAIR, HEAD_DIM):
                head = slice(first, first + HEAD_DIM)
                piece = total[part, :, head]
                if part < 2:
                    piece = piece * cos_ref[...] - half_turn(piece) * sin_ref[...]
                out_ref[:, head] = piece.astype(bf16)


def attend_back(me, qkv, grads, segment, cosine, sine):
    count, local = qkv[0].shape
    whole = lambda h, i, me: (0, 0)
    column = lambda h, i, me: (0, h)
    return pl.pallas_call(
        attend_back_kernel,
        grid_spec=pltpu.PrefetchScalarGridSpec(
            num_scalar_prefetch=1,
            grid=(local // PAIR, count // BLOCK),
            in_specs=[
                pl.BlockSpec((BLOCK, PAIR), lambda h, i, me: (i, h)),
                pl.BlockSpec((count, PAIR), column),
                pl.BlockSpec((count, PAIR), column),
                pl.BlockSpec((BLOCK, 1), lambda h, i, me: (i, 0)),
                pl.BlockSpec((1, count), whole),
                pl.BlockSpec((count, HEAD_DIM), whole),
                pl.BlockSpec((count, HEAD_DIM), whole),
                *[pl.BlockSpec((BLOCK, PAIR), column)] * len(grads),
            ],
            out_specs=[pl.BlockSpec((count, PAIR), column)] * 3,
            scratch_shapes=[pltpu.VMEM((3, count, PAIR), f32)],
        ),
        out_shape=[jax.ShapeDtypeStruct((count, local), bf16)] * 3,
        compiler_params=params(32),
        cost_estimate=cost(1000, 1000),
        name="attend_back",
    )(me, *qkv, *segment, cosine, sine, *grads)


def hidden_kernel(me_ref, weight_ref, rows_ref, *refs):
    *come_refs, hidden_ref, normed_ref, inverse_ref = refs
    size = len(come_refs) // 2 + 1
    attended = jnp.concatenate([picked(me_ref[0], j, come_refs) for j in range(size)], axis=1)
    hidden = rows_ref[...].astype(f32) + matmul(attended, weight_ref[...])
    width = hidden_ref.shape[1]
    own = hidden[:, :width]
    for piece in range(1, size):
        own = jnp.where(me_ref[0] == piece, hidden[:, piece * width : (piece + 1) * width], own)
    hidden_ref[...] = own
    unit, inverse_ref[...] = norm_parts(hidden)
    normed_ref[...] = unit.astype(bf16)


def hidden_and_norm(me, own, arrived, weight, rows):
    count, model = rows.shape
    operands = flat(own, arrived)
    here = lambda i, me: (i, 0)
    return pl.pallas_call(
        hidden_kernel,
        grid_spec=pltpu.PrefetchScalarGridSpec(
            num_scalar_prefetch=1,
            grid=(count // BLOCK,),
            in_specs=[
                pl.BlockSpec((model, model), lambda i, me: (0, 0), pipeline_mode=pl.Buffered(1)),
                pl.BlockSpec((BLOCK, model), here),
                *[pl.BlockSpec((BLOCK, own.shape[1]), here)] * len(operands),
            ],
            out_specs=[
                pl.BlockSpec((BLOCK, own.shape[1]), here),
                pl.BlockSpec((BLOCK, model), here),
                pl.BlockSpec((BLOCK, 1), here),
            ],
        ),
        out_shape=[
            jax.ShapeDtypeStruct(own.shape, f32),
            jax.ShapeDtypeStruct((count, model), bf16),
            jax.ShapeDtypeStruct((count, 1), f32),
        ],
        compiler_params=params(),
        cost_estimate=cost(2 * count * model * model, 2 * model * model + 10 * count * model),
        name="hidden",
    )(me, weight, rows, *operands)


def up_kernel(rows_ref, gate_ref, up_ref, gate_out, up_out, act_ref):
    for first in range(0, rows_ref.shape[0], BLOCK):
        rows = pl.ds(first, BLOCK)
        gate = matmul(rows_ref[rows, :], gate_ref[0])
        up = matmul(rows_ref[rows, :], up_ref[0])
        sigmoid = 1.0 / (1.0 + jnp.exp(-gate))
        silu = gate * sigmoid
        gate_out[rows, :] = (up * (sigmoid + silu * (1.0 - sigmoid))).astype(bf16)
        up_out[rows, :] = silu.astype(bf16)
        act_ref[rows, :] = (silu * up).astype(bf16)


def mlp_up(rows, weights):
    count, model = rows.shape
    hidden_units = weights.shape[2]
    out = jax.ShapeDtypeStruct((count, hidden_units), bf16)
    return pl.pallas_call(
        up_kernel,
        grid=(hidden_units // WIDE,),
        in_specs=[
            pl.BlockSpec((count, model), lambda j: (0, 0)),
            pl.BlockSpec((1, model, WIDE), lambda j: (0, 0, j)),
            pl.BlockSpec((1, model, WIDE), lambda j: (1, 0, j)),
        ],
        out_specs=[pl.BlockSpec((count, WIDE), lambda j: (0, j))] * 3,
        out_shape=[out] * 3,
        compiler_params=params(),
        cost_estimate=cost(
            4 * count * model * hidden_units,
            4 * model * hidden_units + 2 * count * model + 10 * count * hidden_units,
            count * hidden_units,
        ),
        name="mlp_up",
    )(rows, weights, weights)


def down_back_kernel(me_ref, down_ref, gate_in, up_in, *refs):
    *come_refs, grad_ref, dgate_ref, dup_ref = refs
    size = len(come_refs) // 2 + 1
    width = come_refs[0].shape[1]

    @pl.when(pl.program_id(0) == 0)
    def _():
        for owner in range(size):
            grad_ref[:, owner * width : (owner + 1) * width] = picked(
                me_ref[0], owner, come_refs
            )

    for first in range(0, grad_ref.shape[0], BLOCK):
        rows = pl.ds(first, BLOCK)
        down = times_transposed(grad_ref[rows, :], down_ref[0])
        dgate_ref[rows, :] = (down * gate_in[rows, :].astype(f32)).astype(bf16)
        dup_ref[rows, :] = (down * up_in[rows, :].astype(f32)).astype(bf16)


def mlp_down_back(me, own, arrived, weights, gate, up):
    operands = flat(own, arrived)
    count, width = own.shape
    model = width * (len(operands) // 2 + 1)
    hidden_units = weights.shape[2]
    part = pl.BlockSpec((count, WIDE), lambda j, me: (0, j))
    whole = lambda j, me: (0, 0)
    out = jax.ShapeDtypeStruct((count, hidden_units), bf16)
    return pl.pallas_call(
        down_back_kernel,
        grid_spec=pltpu.PrefetchScalarGridSpec(
            num_scalar_prefetch=1,
            grid=(hidden_units // WIDE,),
            in_specs=[
                pl.BlockSpec((1, WIDE, model), lambda j, me: (2, j, 0)),
                part,
                part,
                *[pl.BlockSpec((count, width), whole, pipeline_mode=pl.Buffered(1))]
                * len(operands),
            ],
            out_specs=[pl.BlockSpec((count, model), whole), part, part],
        ),
        out_shape=[jax.ShapeDtypeStruct((count, model), bf16), out, out],
        compiler_params=params(),
        cost_estimate=cost(
            2 * count * model * hidden_units,
            2 * model * hidden_units + 2 * count * model + 12 * count * hidden_units,
            count * hidden_units,
        ),
        name="mlp_down_back",
    )(me, weights, gate, up, *operands)


def mlp_piece_kernel(order_ref, act_ref, down_ref, *out_refs):
    for piece, out_ref in enumerate(out_refs):

        @pl.when(pl.program_id(0) == piece)
        def _(out_ref=out_ref):
            for first in range(0, act_ref.shape[0], BLOCK):
                rows = pl.ds(first, BLOCK)
                out_ref[rows, :] = matmul(act_ref[rows, :], down_ref[0]).astype(bf16)


def mlp_pieces(order, act, weights, width):
    count, hidden_units = act.shape
    pieces = order.shape[0]
    whole = lambda g, order: (0, 0)
    return pl.pallas_call(
        mlp_piece_kernel,
        grid_spec=pltpu.PrefetchScalarGridSpec(
            num_scalar_prefetch=1,
            grid=(pieces,),
            in_specs=[
                pl.BlockSpec((count, hidden_units), whole, pipeline_mode=pl.Buffered(1)),
                pl.BlockSpec((1, hidden_units, width), lambda g, order: (2, 0, order[g])),
            ],
            out_specs=[pl.BlockSpec((count, width), whole)] * pieces,
        ),
        out_shape=[jax.ShapeDtypeStruct((count, width), bf16)] * pieces,
        compiler_params=params(32),
        cost_estimate=cost(
            2 * pieces * count * width * hidden_units, 2 * pieces * width * hidden_units
        ),
        name="mlp_piece",
    )(order, act, weights)


def norm_back(unit_rows, inverse, grad_in):
    unit_rows = unit_rows.astype(f32)
    return inverse * (
        grad_in
        - jnp.mean(grad_in, axis=-1, keepdims=True)
        - unit_rows * jnp.mean(grad_in * unit_rows, axis=-1, keepdims=True)
    )


def first_two_kernel(at_ref, *refs):
    (down_ref, gate_ref, up_ref, gate_in, up_in, normed_ref, inverse_ref) = refs[:7]
    *come_refs, out_ref, grad_ref, dgate_ref, dup_ref, total = refs[7:]
    step, half = pl.program_id(0), pl.num_programs(0) // 2
    size = len(come_refs) // 2 + 1
    width = come_refs[0].shape[1]

    @pl.when(step == 0)
    def _():
        for owner in range(size):
            grad_ref[:, owner * width : (owner + 1) * width] = picked(
                at_ref[1], owner, come_refs
            )

    @pl.when(step < half)
    def _():
        columns = pl.ds(pl.multiple_of(step * WIDE, WIDE), WIDE)
        down = times_transposed(grad_ref[...], down_ref[0])
        dgate_ref[:, columns] = (down * gate_in[...].astype(f32)).astype(bf16)
        dup_ref[:, columns] = (down * up_in[...].astype(f32)).astype(bf16)

    @pl.when(step >= half)
    def _():
        columns = pl.ds(pl.multiple_of((step - half) * WIDE, WIDE), WIDE)
        total[:, columns] = times_transposed(dgate_ref[...], gate_ref[0]) + times_transposed(
            dup_ref[...], up_ref[0]
        )

    @pl.when(step == 2 * half - 1)
    def _():
        out_ref[...] = norm_back(normed_ref[...], inverse_ref[...], total[...]).astype(bf16)


def first_two_grad(at, own, arrived, weights, gate, up, normed, inverse, quarter):
    operands = flat(own, arrived)
    width = own.shape[1]
    hidden_units = gate.shape[1]
    model = weights.shape[1]
    half = hidden_units // WIDE
    first = lambda j: jnp.minimum(j, half - 1)
    second = lambda j: jnp.maximum(j - half, 0)
    rows = lambda j, at: (at[0], 0)
    part = pl.BlockSpec((quarter, WIDE), lambda j, at: (at[0], first(j)))
    once = pl.Buffered(1)
    return pl.pallas_call(
        first_two_kernel,
        grid_spec=pltpu.PrefetchScalarGridSpec(
            num_scalar_prefetch=1,
            grid=(2 * half,),
            in_specs=[
                pl.BlockSpec((1, WIDE, model), lambda j, at: (2, first(j), 0)),
                pl.BlockSpec((1, WIDE, hidden_units), lambda j, at: (0, second(j), 0)),
                pl.BlockSpec((1, WIDE, hidden_units), lambda j, at: (1, second(j), 0)),
                part,
                part,
                pl.BlockSpec((quarter, model), rows, pipeline_mode=once),
                pl.BlockSpec((quarter, 1), rows, pipeline_mode=once),
                *[pl.BlockSpec((quarter, width), rows, pipeline_mode=once)] * len(operands),
            ],
            out_specs=pl.BlockSpec((quarter, model), lambda j, at: (0, 0)),
            scratch_shapes=[
                pltpu.VMEM((quarter, model), bf16),
                pltpu.VMEM((quarter, hidden_units), bf16),
                pltpu.VMEM((quarter, hidden_units), bf16),
                pltpu.VMEM((quarter, model), f32),
            ],
        ),
        out_shape=jax.ShapeDtypeStruct((quarter, model), bf16),
        compiler_params=params(),
        cost_estimate=cost(6 * quarter * model * hidden_units, 6 * model * hidden_units),
        name="first_two_grad",
    )(at, weights, weights, weights, gate, up, normed, inverse, *operands)


def put_at(place, value, refs):
    for index, ref in enumerate(refs):

        @pl.when(place == index)
        def _(ref=ref):
            ref[...] = value


def two_grad_kernel(order_ref, *refs):
    pieces = (len(refs) - 3) // 5
    row_refs = refs[: 4 * pieces]
    gate_ref, up_ref = refs[4 * pieces : 4 * pieces + 2]
    out_refs, total = refs[4 * pieces + 2 : -1], refs[-1]
    step = pl.program_id(0)
    columns = pl.ds(pl.multiple_of(step * WIDE, WIDE), WIDE)
    for piece in range(pieces):
        total[piece, :, columns] = times_transposed(
            row_refs[4 * piece][...], gate_ref[0]
        ) + times_transposed(row_refs[4 * piece + 1][...], up_ref[0])

    @pl.when(step == pl.num_programs(0) - 1)
    def _():
        for piece in range(pieces):
            out_refs[piece][...] = norm_back(
                row_refs[4 * piece + 2][...], row_refs[4 * piece + 3][...], total[piece]
            ).astype(bf16)


def two_grad_pieces(order, dgate, dup, weights, normed, inverse, quarter):
    pieces = order.shape[0]
    hidden_units = dgate.shape[1]
    model = weights.shape[1]
    rows = []
    for p in range(pieces):
        here = lambda j, order, p=p: (order[p], 0)
        rows += [pl.BlockSpec((quarter, hidden_units), here)] * 2
        rows += [pl.BlockSpec((quarter, model), here, pipeline_mode=pl.Buffered(1))]
        rows += [pl.BlockSpec((quarter, 1), here, pipeline_mode=pl.Buffered(1))]
    return pl.pallas_call(
        two_grad_kernel,
        grid_spec=pltpu.PrefetchScalarGridSpec(
            num_scalar_prefetch=1,
            grid=(model // WIDE,),
            in_specs=[
                *rows,
                pl.BlockSpec((1, WIDE, hidden_units), lambda j, order: (0, j, 0)),
                pl.BlockSpec((1, WIDE, hidden_units), lambda j, order: (1, j, 0)),
            ],
            out_specs=[pl.BlockSpec((quarter, model), lambda j, order: (0, 0))] * pieces,
            scratch_shapes=[pltpu.VMEM((pieces, quarter, model), f32)],
        ),
        out_shape=[jax.ShapeDtypeStruct((quarter, model), bf16)] * pieces,
        compiler_params=params(),
        cost_estimate=cost(
            4 * pieces * quarter * model * hidden_units, 4 * model * hidden_units
        ),
        name="two_grad",
    )(order, *([dgate, dup, normed, inverse] * pieces), weights, weights)


def one_grad_kernel(place_ref, dq_ref, dk_ref, dv_ref, weight_ref, unit_ref, inv_ref, *out_refs):
    columns = jnp.concatenate([dq_ref[...], dk_ref[...], dv_ref[...]], axis=1)
    grad = norm_back(
        unit_ref[...], inv_ref[...], times_transposed(columns, weight_ref[...])
    ).astype(bf16)
    width = out_refs[0].shape[1]
    for piece in range(len(out_refs)):
        put_at(place_ref[piece], grad[:, piece * width : (piece + 1) * width], out_refs)


def one_grad_pieces(place, grads, weight, rows, inverse):
    count, local = grads[0].shape
    columns = 3 * local
    pieces = place.shape[0]
    model = rows.shape[1]
    here = lambda i, place: (i, 0)
    return pl.pallas_call(
        one_grad_kernel,
        grid_spec=pltpu.PrefetchScalarGridSpec(
            num_scalar_prefetch=1,
            grid=(count // BLOCK,),
            in_specs=[
                *[pl.BlockSpec((BLOCK, local), here)] * 3,
                pl.BlockSpec(
                    (model, columns), lambda i, place: (0, 0), pipeline_mode=pl.Buffered(1)
                ),
                pl.BlockSpec((BLOCK, model), here),
                pl.BlockSpec((BLOCK, 1), here),
            ],
            out_specs=[pl.BlockSpec((BLOCK, model // pieces), here)] * pieces,
        ),
        out_shape=[jax.ShapeDtypeStruct((count, model // pieces), bf16)] * pieces,
        compiler_params=params(32),
        cost_estimate=cost(
            2 * count * model * columns, 2 * columns * model + 6 * count * columns
        ),
        name="one_grad",
    )(place, *grads, weight, rows, inverse)


def att_grads_kernel(normed_ref, dq_ref, dk_ref, dv_ref, att_ref, hidden_ref, out_ref):
    owner = pl.program_id(0)
    columns = 3 * dq_ref.shape[1]
    grads = jnp.concatenate([dq_ref[...], dk_ref[...], dv_ref[...]], axis=1)
    out_ref[0, :, :columns] = transposed_times(normed_ref[...], grads).astype(bf16)
    model = hidden_ref.shape[1]
    rest = model - columns
    pieces = model // rest
    height = out_ref.shape[1] // pieces
    per_tile = HEAD_DIM // height
    product = transposed_times(att_ref[...], hidden_ref[...]).astype(bf16)
    for place in range(per_tile):

        @pl.when(lax.rem(owner, per_tile) == place)
        def _(place=place):
            for piece in range(pieces):
                out_ref[0, piece * height : (piece + 1) * height, columns:] = product[
                    place * height : (place + 1) * height, piece * rest : (piece + 1) * rest
                ]


def att_grads(normed, qkv_grad, attended, hidden_grad, groups):
    count, model = normed.shape
    local = attended.shape[1]
    columns = 3 * local
    tall = model // groups
    per_tile = HEAD_DIM // (local // groups)
    once = pl.Buffered(1)
    whole = lambda i: (0, 0)
    if tall % HEAD_DIM == 0:
        normed_spec = pl.BlockSpec((count, tall), lambda i: (0, i))
        operand = normed
    else:
        normed_spec = pl.BlockSpec((None, count, tall), lambda i: (i, 0, 0))
        operand = normed.reshape(count, groups, tall).swapaxes(0, 1)
    return pl.pallas_call(
        att_grads_kernel,
        grid=(groups,),
        in_specs=[
            normed_spec,
            *[pl.BlockSpec((count, local), whole, pipeline_mode=once)] * 3,
            pl.BlockSpec((count, HEAD_DIM), lambda i: (0, i // per_tile)),
            pl.BlockSpec((count, model), whole, pipeline_mode=once),
        ],
        out_specs=pl.BlockSpec((1, tall, model), lambda i: (i, 0, 0)),
        out_shape=jax.ShapeDtypeStruct((groups, tall, model), bf16),
        compiler_params=params(32),
        cost_estimate=cost(1000, 1000),
        name="att_grads",
    )(operand, *qkv_grad, attended, hidden_grad)


def mlp_grads_kernel(*refs):
    *operands, out_ref = refs
    count = len(operands) // 2
    total = transposed_times(operands[0][...], operands[count][...])
    for part in range(1, count):
        total += transposed_times(operands[part][...], operands[count + part][...])
    out_ref[0] = total.astype(bf16)


def mlp_grads(which, left, right, before=None):
    rows = left[0].shape[0]
    model, hidden_units = left[0].shape[1], right[0].shape[1]
    once = pl.Buffered(1)
    specs = [pl.BlockSpec((rows, BLOCK), lambda i: (0, i)) for _ in left]
    specs += [
        pl.BlockSpec((rows, hidden_units), lambda i: (0, 0), pipeline_mode=once) for _ in right
    ]
    operands = [*left, *right]
    body = mlp_grads_kernel
    aliases = {}
    if before is not None:
        aliases = {len(operands): 0}
        specs.append(pl.BlockSpec(memory_space=pl.ANY))
        operands.append(before)
        body = lambda *refs: mlp_grads_kernel(*refs[:-2], refs[-1])
    count = rows * len(left)
    return pl.pallas_call(
        body,
        grid=(model // BLOCK,),
        in_specs=specs,
        out_specs=pl.BlockSpec((1, BLOCK, hidden_units), lambda i: (which, i, 0)),
        out_shape=jax.ShapeDtypeStruct((3, model, hidden_units), bf16),
        input_output_aliases=aliases,
        compiler_params=params(32),
        cost_estimate=cost(
            2 * count * model * hidden_units, 2 * model * hidden_units + 4 * count * model
        ),
        name="mlp_grads",
    )(*operands)


def after(value, *others):
    return lax.optimization_barrier((value, *others))[0]


def line_step(block, axis, size, step):
    from_low, from_high = block
    up = [(i, i + 1) for i in range(step - 1, size - 1)]
    down = [(i, i - 1) for i in range(size - step, 0, -1)]
    return lax.ppermute(from_low, axis, up), lax.ppermute(from_high, axis, down)


def chain_gather(block, axis, size, begun=None):
    arrived = list(begun or [])
    for step in range(len(arrived) + 1, size):
        arrived.append(line_step(arrived[-1] if arrived else (block, block), axis, size, step))
    return arrived


def line_whole(own, arrived, axis, size):
    me = lax.axis_index(axis)
    low, high = [pair[0] for pair in arrived], [pair[1] for pair in arrived]
    return [pick(me, owner, own, low, high) for owner in range(size)]


def far_first(size):
    return sorted(range(1, size), key=lambda step: -min(step, size - step))


def sent_on(term, axis, size, step):
    return lax.ppermute(term, axis, [(i, (i + step) % size) for i in range(size)])


def added(own, came):
    for piece in came:
        own = own + piece.astype(f32)
    return own


def on_device(
    tokens,
    cotangent,
    w_query,
    w_key,
    w_value,
    w_out,
    w_gate,
    w_up,
    w_down,
    seq_lengths,
    deal,
    row_dest,
):
    groups = lax.axis_size("fsdp")
    shards = lax.axis_size("tp")
    own_group = lax.axis_index("fsdp")
    own_shard = lax.axis_index("tp")
    capacity = GROUP_CAP
    per_pair = capacity // groups
    quarter = capacity // shards
    head_dim = HEAD_DIM
    given, width = tokens.shape
    model = width * shards
    local_width = w_query.shape[1]
    shard_rows = w_query.shape[0]

    steps = far_first(shards)
    order = jnp.stack([lax.rem(own_shard + step, shards) for step in (*steps, 0)])
    around = jnp.stack([lax.rem(own_shard + step, shards) for step in range(shards)])
    place_of = [0] * shards
    for index, step in enumerate((*steps, 0)):
        place_of[step] = index
    place = jnp.stack(
        [
            sum(
                jnp.where(lax.rem(own_shard + step, shards) == j, place_of[step], 0)
                for step in range(shards)
            )
            for j in range(shards)
        ]
    )

    target = row_dest // capacity
    within = row_dest - target * capacity
    given_index = jnp.arange(given, dtype=jnp.int32)
    earlier = (target[:, None] == target[None, :]) & (
        given_index[None, :] < given_index[:, None]
    )
    slot_of = target * per_pair + jnp.sum(earlier.astype(jnp.int32), axis=1)
    slots = jnp.arange(capacity, dtype=jnp.int32)
    deal_hit = slots[:, None] == slot_of[None, :]
    deal_out = deal_hit.astype(bf16)
    place_high, place_low = (within + 1) // 32, (within + 1) % 32
    lane = jnp.arange(HEAD_DIM, dtype=jnp.int32)[None, :]
    place_columns = jnp.where(
        lane == 0, place_high[:, None], jnp.where(lane == 1, place_low[:, None], 0)
    ).astype(bf16)

    def over_fsdp(rows):
        return lax.all_to_all(rows, "fsdp", split_axis=0, concat_axis=0, tiled=True)

    sent_rows = matmul(deal_out, jnp.concatenate([tokens, place_columns], axis=1)).astype(bf16)
    sent_grads = matmul(deal_out, cotangent).astype(bf16)

    qkv_shard = jnp.concatenate([w_query, w_key, w_value], axis=1)
    full_qkv = lax.all_gather(qkv_shard, "fsdp", axis=0, tiled=True)
    out_came = [sent_on(w_out, "tp", shards, step) for step in range(1, shards)]
    came_rows = over_fsdp(sent_rows)
    mlp_shard = jnp.stack([w_gate, w_up, w_down])
    *out_came, came_rows, sent_grads, mlp_shard = lax.optimization_barrier(
        (*out_came, came_rows, sent_grads, mlp_shard)
    )
    came_place = came_rows[:, width : width + 2].astype(jnp.int32)
    recv_place = came_place[:, 0] * 32 + came_place[:, 1] - 1
    place_in = (slots[:, None] == recv_place[None, :]).astype(bf16)
    out_came = [w_out] + out_came
    out_rows = []
    for owner in range(shards):
        piece = w_out
        for step in range(1, shards):
            piece = jnp.where(own_shard == (owner + step) % shards, out_came[step], piece)
        out_rows.append(piece)
    out_rows = jnp.stack(out_rows)
    full_out = lax.all_gather(out_rows, "fsdp", axis=1, tiled=True).reshape(model, model)

    full_mlp = lax.all_gather(mlp_shard, "fsdp", axis=1, tiled=True)
    buffer_rows = matmul(place_in, came_rows[:, :width]).astype(bf16)
    buffer_grads = matmul(place_in, over_fsdp(after(sent_grads, buffer_rows))).astype(bf16)
    rows_come = chain_gather(buffer_rows, "tp", shards)
    list_index = jnp.sum(jnp.where(deal == own_group, jnp.arange(groups, dtype=jnp.int32), 0))
    lengths = lax.dynamic_index_in_dim(seq_lengths, list_index, 0, keepdims=False)
    segment, position = segments(lengths)
    cosine, sine = rope_tables(position, head_dim)
    segment_column, segment_row = segment[:, None], segment[None, :]
    rows_come[-1], first_grads, segment_column, segment_row, cosine, sine = (
        lax.optimization_barrier(
            (rows_come[-1], buffer_grads, segment_column, segment_row, cosine, sine)
        )
    )
    segment = (segment_column, segment_row)
    me = own_shard[None].astype(jnp.int32)

    full_rows, normed_one, inverse_one = gathered_norm(me, buffer_rows, rows_come)
    first_grads, normed_one = lax.optimization_barrier((first_grads, normed_one))
    grads_begun = line_step((first_grads, first_grads), "tp", shards, 1)
    qkv = project_qkv(normed_one, full_qkv, cosine, sine)
    attended = attend(qkv, segment)
    attended, *grads_begun = lax.optimization_barrier((attended, *grads_begun))
    att_come = chain_gather(attended, "tp", shards)
    *grads_begun, last_low, last_high = lax.optimization_barrier((*grads_begun, *att_come[-1]))
    att_come[-1] = (last_low, last_high)
    grads_come = [grads_begun, line_step(grads_begun, "tp", shards, 2)]
    hidden, normed_two, inverse_two = hidden_and_norm(me, attended, att_come, full_out, full_rows)
    *grads_come[1], normed_two = lax.optimization_barrier((*grads_come[1], normed_two))
    grads_come = chain_gather(first_grads, "tp", shards, grads_come)
    gate, up, activated = mlp_up(normed_two, full_mlp)
    def features_of(rows, owner):
        return lax.dynamic_slice_in_dim(rows, owner * width, width, 1)

    *last, activated = lax.optimization_barrier((*grads_come[-1], activated))
    grads_come[-1] = tuple(last)
    two_first = first_two_grad(
        jnp.stack([order[0], own_shard]),
        first_grads,
        grads_come,
        full_mlp,
        gate,
        up,
        normed_two,
        inverse_two,
        quarter,
    )
    full_grads, gate_grad, up_grad = mlp_down_back(
        me, first_grads, grads_come, full_mlp, after(gate, two_first), up
    )

    def rows_of(rows, owner):
        return lax.dynamic_slice_in_dim(rows, owner * quarter, quarter, 0)

    two_rest = two_grad_pieces(
        order[1:], gate_grad, up_grad, full_mlp, normed_two, inverse_two, quarter
    )
    two_came = [
        sent_on(term, "tp", shards, step)
        for term, step in zip((two_first, *two_rest), steps)
    ]
    grad_mlp = mlp_grads(0, [normed_two], [after(gate_grad, *two_rest)])
    grad_mlp = mlp_grads(1, [normed_two], [up_grad], grad_mlp)
    grad_mlp = mlp_grads(2, [activated], [full_grads], grad_mlp)
    *two_came, grad_mlp = lax.optimization_barrier((*two_came, grad_mlp))
    sum_mlp = lax.psum_scatter(grad_mlp, "fsdp", scatter_dimension=1, tiled=True)
    back_low = added(
        rows_of(full_grads, own_shard).astype(f32) + two_rest[-1].astype(f32), two_came
    ).astype(bf16)
    back_come = [line_step((back_low, back_low), "tp", shards, 1)]
    own_out = lax.dynamic_slice_in_dim(full_out, own_shard * local_width, local_width, 0)

    def att_piece(block):
        return times_transposed(block, own_out).astype(bf16)

    def merged(step):
        low, high = back_come[step - 1]
        if 2 * step < shards:
            return low, high
        both = jnp.where(own_shard >= step, low, high)
        return both, both

    att_pieces = [att_piece(back_low)]
    terms = mlp_pieces(around, after(activated, grad_mlp, back_low), full_mlp, width)
    mlp_come = []
    for step in range(1, shards):
        back_come[-1], mlp_come, terms = lax.optimization_barrier(
            (back_come[-1], mlp_come, terms)
        )
        if step < shards - 1:
            back_come.append(line_step(back_come[-1], "tp", shards, step + 1))
            att_pieces += [att_piece(block) for block in merged(step)]
        low, high = terms[shards - step], terms[step]
        if mlp_come:
            low, high = (
                (term.astype(f32) + came.astype(f32)).astype(bf16)
                for term, came in zip((low, high), mlp_come)
            )
        up = [(i, i + 1) for i in range(step)]
        down = [(i, i - 1) for i in range(shards - 1, shards - 1 - step, -1)]
        mlp_come = [lax.ppermute(low, "tp", up), lax.ppermute(high, "tp", down)]
    att_pieces += [att_piece(block) for block in merged(shards - 1)]
    qkv_grad = attend_back(
        me,
        qkv,
        [att_pieces[0], *att_pieces[1::2], *att_pieces[2::2]],
        segment,
        cosine,
        sine,
    )
    one_terms = one_grad_pieces(place, qkv_grad, full_qkv, normed_one, inverse_one)
    one_came = [sent_on(term, "tp", shards, step) for term, step in zip(one_terms, steps)]
    full_hidden_grad = jnp.concatenate(
        line_whole(after(back_low, *one_terms[:3]), back_come, "tp", shards), axis=0
    )
    *mlp_come, late_grad, _ = lax.optimization_barrier(
        (*mlp_come, tuple(qkv_grad), tuple(one_terms[:3]))
    )
    grad_att = att_grads(
        normed_one, late_grad, attended, full_hidden_grad, groups
    )
    sum_mlp, grad_att = lax.optimization_barrier((sum_mlp, grad_att))
    sum_att = lax.psum_scatter(grad_att, "fsdp", scatter_dimension=0, tiled=False)

    sum_att = sum_att.astype(f32)
    out_part = sum_att[:, 3 * local_width :]
    out_pieces = model // out_part.shape[1]
    out_height = shard_rows // out_pieces
    sum_out = jnp.concatenate(
        [out_part[i * out_height : (i + 1) * out_height] for i in range(out_pieces)], axis=1
    )
    sum_gate, sum_up, sum_down = sum_mlp.astype(f32)
    back_here = added(one_terms[-1].astype(f32), one_came)
    input_here = features_of(full_hidden_grad, own_shard).astype(f32) + back_here
    output_here = hidden + added(terms[0].astype(f32), mlp_come)
    here = jnp.concatenate([output_here.astype(bf16), input_here.astype(bf16)], axis=1)
    sent_back = transposed_times(place_in, here).astype(bf16)
    sums = (
        sum_att[:, : local_width],
        sum_att[:, local_width : 2 * local_width],
        sum_att[:, 2 * local_width : 3 * local_width],
        sum_out,
        sum_gate,
        sum_up,
        sum_down,
    )
    came_back, *sums = lax.optimization_barrier((over_fsdp(sent_back), *sums))
    home = transposed_times(deal_out, came_back).astype(bf16)
    return (home[:, :width], home[:, width:], *sums)


def solution(mesh):
    in_specs = (
        P("fsdp", "tp"),
        P("fsdp", "tp"),
        P("fsdp", "tp"),
        P("fsdp", "tp"),
        P("fsdp", "tp"),
        P(("tp", "fsdp"), None),
        P("fsdp", "tp"),
        P("fsdp", "tp"),
        P(("tp", "fsdp"), None),
        P(),
        P(),
        P("fsdp"),
    )
    out_specs = (
        P("fsdp", "tp"),
        P("fsdp", "tp"),
        P("fsdp", "tp"),
        P("fsdp", "tp"),
        P("fsdp", "tp"),
        P(("tp", "fsdp"), None),
        P("fsdp", "tp"),
        P("fsdp", "tp"),
        P(("tp", "fsdp"), None),
    )
    return jax.shard_map(
        on_device, mesh=mesh, in_specs=in_specs, out_specs=out_specs, check_vma=False
    )
```

```python
import jax
import jax.numpy as jnp
from jax import lax
from jax.experimental import pallas as pl
from jax.experimental.pallas import tpu as pltpu
from jax.sharding import PartitionSpec as P

HEAD_DIM = 128
GROUP_CAP = 1024
SEQ_SLOTS = 4

norm_eps = 1e-05
rope_base = 10000.0
bf16 = jnp.bfloat16
f32 = jnp.float32


def matmul(left, right):
    return jnp.dot(left, right, preferred_element_type=f32)


def times_transposed(left, right):
    return lax.dot_general(
        left, right, (((1,), (1,)), ((), ())), preferred_element_type=f32
    )


def transposed_times(left, right):
    return lax.dot_general(
        left, right, (((0,), (0,)), ((), ())), preferred_element_type=f32
    )


def norm_parts(values_in):
    row_mean = jnp.mean(values_in, axis=-1, keepdims=True)
    centered = values_in - row_mean
    variance = jnp.mean(centered * centered, axis=-1, keepdims=True)
    inverse = lax.rsqrt(variance + norm_eps)
    return centered * inverse, inverse


def rope_tables(position, head_dim):
    half_dim = head_dim // 2
    frequency = rope_base ** (-(jnp.arange(half_dim, dtype=f32) * 2.0) / head_dim)
    angles = position.astype(f32)[:, None] * frequency[None, :]
    cosine, sine = jnp.cos(angles), jnp.sin(angles)
    return (
        jnp.concatenate([cosine, cosine], axis=1),
        jnp.concatenate([-sine, sine], axis=1),
    )


def segments(lengths):
    row_index = jnp.arange(GROUP_CAP, dtype=jnp.int32)
    slot_ids = jnp.arange(SEQ_SLOTS, dtype=jnp.int32)
    ends = jnp.sum(
        jnp.where(slot_ids[:, None] <= slot_ids[None, :], lengths[:, None], 0), axis=0
    )
    passed = row_index[:, None] >= ends[None, :]
    segment = jnp.sum(passed.astype(jnp.int32), axis=1)
    begin_row = jnp.max(jnp.where(passed, ends[None, :], 0), axis=1)
    return (segment, row_index - begin_row)


MIB = 1024 * 1024
BLOCK = 256
WIDE = 512


def params(mib=58):
    return pltpu.CompilerParams(vmem_limit_bytes=mib * MIB)


def cost(flops, read, transcendentals=0):
    return pl.CostEstimate(
        flops=int(flops), bytes_accessed=int(read), transcendentals=int(transcendentals)
    )


def half_turn(values_in):
    return pltpu.roll(values_in, HEAD_DIM // 2, 1)


def pick(me, owner, own, low, high):
    piece = own
    for step, (lower, higher) in enumerate(zip(low, high), start=1):
        piece = jnp.where(me == owner + step, lower, piece)
        piece = jnp.where(me == owner - step, higher, piece)
    return piece


def flat(own, arrived):
    return [own, *[low for low, _ in arrived], *[high for _, high in arrived]]


def picked(me, owner, refs):
    steps = len(refs) // 2
    blocks = [ref[...] for ref in refs]
    return pick(me, owner, blocks[0], blocks[1 : 1 + steps], blocks[1 + steps :])


def norm_kernel(me_ref, *refs):
    *come_refs, rows_ref, normed_ref, inverse_ref = refs
    size = len(come_refs) // 2 + 1
    rows = jnp.concatenate([picked(me_ref[0], j, come_refs) for j in range(size)], axis=1)
    rows_ref[...] = rows
    unit, inverse_ref[...] = norm_parts(rows.astype(f32))
    normed_ref[...] = unit.astype(bf16)


def gathered_norm(me, own, arrived):
    count, width = own.shape
    operands = flat(own, arrived)
    model = width * (len(operands) // 2 + 1)
    here = lambda i, me: (i, 0)
    out = jax.ShapeDtypeStruct((count, model), bf16)
    return pl.pallas_call(
        norm_kernel,
        grid_spec=pltpu.PrefetchScalarGridSpec(
            num_scalar_prefetch=1,
            grid=(count // BLOCK,),
            in_specs=[pl.BlockSpec((BLOCK, width), here)] * len(operands),
            out_specs=[
                pl.BlockSpec((BLOCK, model), here),
                pl.BlockSpec((BLOCK, model), here),
                pl.BlockSpec((BLOCK, 1), here),
            ],
        ),
        out_shape=[out, out, jax.ShapeDtypeStruct((count, 1), f32)],
        compiler_params=params(),
        cost_estimate=cost(20 * count * model, 8 * count * model),
        name="gathered_norm",
    )(me, *operands)


def qkv_kernel(rows_ref, wq_ref, wk_ref, wv_ref, cos_ref, sin_ref, *out_refs):
    weight = jnp.concatenate([wq_ref[...], wk_ref[...], wv_ref[...]], axis=1)
    for first in range(0, rows_ref.shape[0], BLOCK):
        rows = pl.ds(first, BLOCK)
        pre = matmul(rows_ref[rows, :], weight)
        for part in range(3):
            piece = pre[:, part * HEAD_DIM : (part + 1) * HEAD_DIM]
            if part < 2:
                piece = piece * cos_ref[rows, :] + half_turn(piece) * sin_ref[rows, :]
            out_refs[part][rows, :] = piece.astype(bf16)


def head_specs(model, heads):
    return [
        pl.BlockSpec((model, HEAD_DIM), lambda h, part=part: (0, part * heads + h))
        for part in range(3)
    ]


def project_qkv(rows, weight, cosine, sine):
    count, model = rows.shape
    columns = weight.shape[1]
    heads = columns // (3 * HEAD_DIM)
    whole = lambda h: (0, 0)
    return pl.pallas_call(
        qkv_kernel,
        grid=(heads,),
        in_specs=[
            pl.BlockSpec((count, model), whole),
            *head_specs(model, heads),
            pl.BlockSpec((count, HEAD_DIM), whole),
            pl.BlockSpec((count, HEAD_DIM), whole),
        ],
        out_specs=[pl.BlockSpec((count, HEAD_DIM), lambda h: (0, h))] * 3,
        out_shape=[jax.ShapeDtypeStruct((count, heads * HEAD_DIM), bf16)] * 3,
        compiler_params=params(),
        cost_estimate=cost(2 * count * model * columns, 2 * model * (count + columns)),
        name="qkv",
    )(rows, weight, weight, weight, cosine, sine)


def masked_softmax(q_rows, k_rows, seg_column, seg_row, row_first):
    scores = times_transposed(q_rows, k_rows) * HEAD_DIM ** (-0.5)
    row = lax.broadcasted_iota(jnp.int32, scores.shape, 0) + row_first
    column = lax.broadcasted_iota(jnp.int32, scores.shape, 1)
    allowed = (seg_column == seg_row) & (column <= row)
    scores = jnp.where(allowed, scores, -1e30)
    exponent = jnp.exp(scores - jnp.max(scores, axis=-1, keepdims=True))
    return exponent * (1.0 / jnp.sum(exponent, axis=-1, keepdims=True))


PAIR = 2 * HEAD_DIM


def attend_kernel(q_ref, k_ref, v_ref, column_ref, row_ref, out_ref):
    block = pl.program_id(1)
    for index in range(k_ref.shape[0] // BLOCK):

        @pl.when(block == index)
        def _(index=index):
            seen = (index + 1) * BLOCK
            for first in range(0, PAIR, HEAD_DIM):
                head = slice(first, first + HEAD_DIM)
                prob = masked_softmax(
                    q_ref[:, head],
                    k_ref[:seen, head],
                    column_ref[...],
                    row_ref[:, :seen],
                    index * BLOCK,
                )
                out_ref[:, head] = matmul(prob.astype(bf16), v_ref[:seen, head]).astype(bf16)


def attend(qkv, segment):
    count, local = qkv[0].shape
    column = lambda h, i: (0, h)
    return pl.pallas_call(
        attend_kernel,
        grid=(local // PAIR, count // BLOCK),
        in_specs=[
            pl.BlockSpec((BLOCK, PAIR), lambda h, i: (i, h)),
            pl.BlockSpec((count, PAIR), column),
            pl.BlockSpec((count, PAIR), column),
            pl.BlockSpec((BLOCK, 1), lambda h, i: (i, 0)),
            pl.BlockSpec((1, count), lambda h, i: (0, 0)),
        ],
        out_specs=pl.BlockSpec((BLOCK, PAIR), lambda h, i: (i, h)),
        out_shape=jax.ShapeDtypeStruct((count, local), bf16),
        compiler_params=params(),
        cost_estimate=cost(4 * count * count * local, 8 * count * local, count * count * 4),
        name="attend",
    )(*qkv, *segment)


def attend_back_kernel(
    me_ref, q_ref, k_ref, v_ref, column_ref, row_ref, cos_ref, sin_ref, *refs
):
    *grad_refs, dq_ref, dk_ref, dv_ref, total = refs
    block = pl.program_id(1)
    scale = HEAD_DIM ** (-0.5)
    blocks = k_ref.shape[0] // BLOCK

    @pl.when(block == 0)
    def _():
        total[...] = jnp.zeros_like(total)

    for index in range(blocks):

        @pl.when(block == index)
        def _(index=index):
            seen = (index + 1) * BLOCK
            grads = picked(me_ref[0], index, grad_refs)
            for first in range(0, PAIR, HEAD_DIM):
                head = slice(first, first + HEAD_DIM)
                q_rows, k_rows, grad = q_ref[:, head], k_ref[:seen, head], grads[:, head]
                prob = masked_softmax(
                    q_rows, k_rows, column_ref[...], row_ref[:, :seen], index * BLOCK
                )
                prob_grad = times_transposed(grad, v_ref[:seen, head])
                delta = jnp.sum(prob_grad * prob, axis=-1, keepdims=True)
                score_grad = (prob * (prob_grad - delta)).astype(bf16)
                total[0, index * BLOCK : seen, head] = matmul(score_grad, k_rows) * scale
                total[1, :seen, head] += transposed_times(score_grad, q_rows) * scale
                total[2, :seen, head] += transposed_times(prob.astype(bf16), grad)

    @pl.when(block == blocks - 1)
    def _():
        for part, out_ref in enumerate((dq_ref, dk_ref, dv_ref)):
            for first in range(0, PAIR, HEAD_DIM):
                head = slice(first, first + HEAD_DIM)
                piece = total[part, :, head]
                if part < 2:
                    piece = piece * cos_ref[...] - half_turn(piece) * sin_ref[...]
                out_ref[:, head] = piece.astype(bf16)


def attend_back(me, qkv, grads, segment, cosine, sine):
    count, local = qkv[0].shape
    whole = lambda h, i, me: (0, 0)
    column = lambda h, i, me: (0, h)
    return pl.pallas_call(
        attend_back_kernel,
        grid_spec=pltpu.PrefetchScalarGridSpec(
            num_scalar_prefetch=1,
            grid=(local // PAIR, count // BLOCK),
            in_specs=[
                pl.BlockSpec((BLOCK, PAIR), lambda h, i, me: (i, h)),
                pl.BlockSpec((count, PAIR), column),
                pl.BlockSpec((count, PAIR), column),
                pl.BlockSpec((BLOCK, 1), lambda h, i, me: (i, 0)),
                pl.BlockSpec((1, count), whole),
                pl.BlockSpec((count, HEAD_DIM), whole),
                pl.BlockSpec((count, HEAD_DIM), whole),
                *[pl.BlockSpec((BLOCK, PAIR), column)] * len(grads),
            ],
            out_specs=[pl.BlockSpec((count, PAIR), column)] * 3,
            scratch_shapes=[pltpu.VMEM((3, count, PAIR), f32)],
        ),
        out_shape=[jax.ShapeDtypeStruct((count, local), bf16)] * 3,
        compiler_params=params(32),
        cost_estimate=cost(1000, 1000),
        name="attend_back",
    )(me, *qkv, *segment, cosine, sine, *grads)


def hidden_kernel(me_ref, weight_ref, rows_ref, *refs):
    *come_refs, hidden_ref, normed_ref, inverse_ref = refs
    size = len(come_refs) // 2 + 1
    attended = jnp.concatenate([picked(me_ref[0], j, come_refs) for j in range(size)], axis=1)
    hidden = rows_ref[...].astype(f32) + matmul(attended, weight_ref[...])
    width = hidden_ref.shape[1]
    own = hidden[:, :width]
    for piece in range(1, size):
        own = jnp.where(me_ref[0] == piece, hidden[:, piece * width : (piece + 1) * width], own)
    hidden_ref[...] = own
    unit, inverse_ref[...] = norm_parts(hidden)
    normed_ref[...] = unit.astype(bf16)


def hidden_and_norm(me, own, arrived, weight, rows):
    count, model = rows.shape
    operands = flat(own, arrived)
    here = lambda i, me: (i, 0)
    return pl.pallas_call(
        hidden_kernel,
        grid_spec=pltpu.PrefetchScalarGridSpec(
            num_scalar_prefetch=1,
            grid=(count // BLOCK,),
            in_specs=[
                pl.BlockSpec((model, model), lambda i, me: (0, 0), pipeline_mode=pl.Buffered(1)),
                pl.BlockSpec((BLOCK, model), here),
                *[pl.BlockSpec((BLOCK, own.shape[1]), here)] * len(operands),
            ],
            out_specs=[
                pl.BlockSpec((BLOCK, own.shape[1]), here),
                pl.BlockSpec((BLOCK, model), here),
                pl.BlockSpec((BLOCK, 1), here),
            ],
        ),
        out_shape=[
            jax.ShapeDtypeStruct(own.shape, f32),
            jax.ShapeDtypeStruct((count, model), bf16),
            jax.ShapeDtypeStruct((count, 1), f32),
        ],
        compiler_params=params(),
        cost_estimate=cost(2 * count * model * model, 2 * model * model + 10 * count * model),
        name="hidden",
    )(me, weight, rows, *operands)


def up_kernel(rows_ref, gate_ref, up_ref, gate_out, up_out, act_ref):
    for first in range(0, rows_ref.shape[0], BLOCK):
        rows = pl.ds(first, BLOCK)
        gate = matmul(rows_ref[rows, :], gate_ref[0])
        up = matmul(rows_ref[rows, :], up_ref[0])
        sigmoid = 1.0 / (1.0 + jnp.exp(-gate))
        silu = gate * sigmoid
        gate_out[rows, :] = (up * (sigmoid + silu * (1.0 - sigmoid))).astype(bf16)
        up_out[rows, :] = silu.astype(bf16)
        act_ref[rows, :] = (silu * up).astype(bf16)


def mlp_up(rows, weights):
    count, model = rows.shape
    hidden_units = weights.shape[2]
    out = jax.ShapeDtypeStruct((count, hidden_units), bf16)
    return pl.pallas_call(
        up_kernel,
        grid=(hidden_units // WIDE,),
        in_specs=[
            pl.BlockSpec((count, model), lambda j: (0, 0)),
            pl.BlockSpec((1, model, WIDE), lambda j: (0, 0, j)),
            pl.BlockSpec((1, model, WIDE), lambda j: (1, 0, j)),
        ],
        out_specs=[pl.BlockSpec((count, WIDE), lambda j: (0, j))] * 3,
        out_shape=[out] * 3,
        compiler_params=params(),
        cost_estimate=cost(
            4 * count * model * hidden_units,
            4 * model * hidden_units + 2 * count * model + 10 * count * hidden_units,
            count * hidden_units,
        ),
        name="mlp_up",
    )(rows, weights, weights)


def down_back_kernel(me_ref, down_ref, gate_in, up_in, *refs):
    *come_refs, grad_ref, dgate_ref, dup_ref = refs
    size = len(come_refs) // 2 + 1
    width = come_refs[0].shape[1]

    @pl.when(pl.program_id(0) == 0)
    def _():
        for owner in range(size):
            grad_ref[:, owner * width : (owner + 1) * width] = picked(
                me_ref[0], owner, come_refs
            )

    for first in range(0, grad_ref.shape[0], BLOCK):
        rows = pl.ds(first, BLOCK)
        down = times_transposed(grad_ref[rows, :], down_ref[0])
        dgate_ref[rows, :] = (down * gate_in[rows, :].astype(f32)).astype(bf16)
        dup_ref[rows, :] = (down * up_in[rows, :].astype(f32)).astype(bf16)


def mlp_down_back(me, own, arrived, weights, gate, up):
    operands = flat(own, arrived)
    count, width = own.shape
    model = width * (len(operands) // 2 + 1)
    hidden_units = weights.shape[2]
    part = pl.BlockSpec((count, WIDE), lambda j, me: (0, j))
    whole = lambda j, me: (0, 0)
    out = jax.ShapeDtypeStruct((count, hidden_units), bf16)
    return pl.pallas_call(
        down_back_kernel,
        grid_spec=pltpu.PrefetchScalarGridSpec(
            num_scalar_prefetch=1,
            grid=(hidden_units // WIDE,),
            in_specs=[
                pl.BlockSpec((1, WIDE, model), lambda j, me: (2, j, 0)),
                part,
                part,
                *[pl.BlockSpec((count, width), whole, pipeline_mode=pl.Buffered(1))]
                * len(operands),
            ],
            out_specs=[pl.BlockSpec((count, model), whole), part, part],
        ),
        out_shape=[jax.ShapeDtypeStruct((count, model), bf16), out, out],
        compiler_params=params(),
        cost_estimate=cost(
            2 * count * model * hidden_units,
            2 * model * hidden_units + 2 * count * model + 12 * count * hidden_units,
            count * hidden_units,
        ),
        name="mlp_down_back",
    )(me, weights, gate, up, *operands)


def mlp_piece_kernel(order_ref, act_ref, down_ref, *out_refs):
    for piece, out_ref in enumerate(out_refs):

        @pl.when(pl.program_id(0) == piece)
        def _(out_ref=out_ref):
            for first in range(0, act_ref.shape[0], BLOCK):
                rows = pl.ds(first, BLOCK)
                out_ref[rows, :] = matmul(act_ref[rows, :], down_ref[0]).astype(bf16)


def mlp_pieces(order, act, weights, width):
    count, hidden_units = act.shape
    pieces = order.shape[0]
    whole = lambda g, order: (0, 0)
    return pl.pallas_call(
        mlp_piece_kernel,
        grid_spec=pltpu.PrefetchScalarGridSpec(
            num_scalar_prefetch=1,
            grid=(pieces,),
            in_specs=[
                pl.BlockSpec((count, hidden_units), whole, pipeline_mode=pl.Buffered(1)),
                pl.BlockSpec((1, hidden_units, width), lambda g, order: (2, 0, order[g])),
            ],
            out_specs=[pl.BlockSpec((count, width), whole)] * pieces,
        ),
        out_shape=[jax.ShapeDtypeStruct((count, width), bf16)] * pieces,
        compiler_params=params(32),
        cost_estimate=cost(
            2 * pieces * count * width * hidden_units, 2 * pieces * width * hidden_units
        ),
        name="mlp_piece",
    )(order, act, weights)


def norm_back(unit_rows, inverse, grad_in):
    unit_rows = unit_rows.astype(f32)
    return inverse * (
        grad_in
        - jnp.mean(grad_in, axis=-1, keepdims=True)
        - unit_rows * jnp.mean(grad_in * unit_rows, axis=-1, keepdims=True)
    )


def first_two_kernel(at_ref, *refs):
    (down_ref, gate_ref, up_ref, gate_in, up_in, normed_ref, inverse_ref) = refs[:7]
    *come_refs, out_ref, grad_ref, dgate_ref, dup_ref, total = refs[7:]
    step, half = pl.program_id(0), pl.num_programs(0) // 2
    size = len(come_refs) // 2 + 1
    width = come_refs[0].shape[1]

    @pl.when(step == 0)
    def _():
        for owner in range(size):
            grad_ref[:, owner * width : (owner + 1) * width] = picked(
                at_ref[1], owner, come_refs
            )

    @pl.when(step < half)
    def _():
        columns = pl.ds(pl.multiple_of(step * WIDE, WIDE), WIDE)
        down = times_transposed(grad_ref[...], down_ref[0])
        dgate_ref[:, columns] = (down * gate_in[...].astype(f32)).astype(bf16)
        dup_ref[:, columns] = (down * up_in[...].astype(f32)).astype(bf16)

    @pl.when(step >= half)
    def _():
        columns = pl.ds(pl.multiple_of((step - half) * WIDE, WIDE), WIDE)
        total[:, columns] = times_transposed(dgate_ref[...], gate_ref[0]) + times_transposed(
            dup_ref[...], up_ref[0]
        )

    @pl.when(step == 2 * half - 1)
    def _():
        out_ref[...] = norm_back(normed_ref[...], inverse_ref[...], total[...]).astype(bf16)


def first_two_grad(at, own, arrived, weights, gate, up, normed, inverse, quarter):
    operands = flat(own, arrived)
    width = own.shape[1]
    hidden_units = gate.shape[1]
    model = weights.shape[1]
    half = hidden_units // WIDE
    first = lambda j: jnp.minimum(j, half - 1)
    second = lambda j: jnp.maximum(j - half, 0)
    rows = lambda j, at: (at[0], 0)
    part = pl.BlockSpec((quarter, WIDE), lambda j, at: (at[0], first(j)))
    once = pl.Buffered(1)
    return pl.pallas_call(
        first_two_kernel,
        grid_spec=pltpu.PrefetchScalarGridSpec(
            num_scalar_prefetch=1,
            grid=(2 * half,),
            in_specs=[
                pl.BlockSpec((1, WIDE, model), lambda j, at: (2, first(j), 0)),
                pl.BlockSpec((1, WIDE, hidden_units), lambda j, at: (0, second(j), 0)),
                pl.BlockSpec((1, WIDE, hidden_units), lambda j, at: (1, second(j), 0)),
                part,
                part,
                pl.BlockSpec((quarter, model), rows, pipeline_mode=once),
                pl.BlockSpec((quarter, 1), rows, pipeline_mode=once),
                *[pl.BlockSpec((quarter, width), rows, pipeline_mode=once)] * len(operands),
            ],
            out_specs=pl.BlockSpec((quarter, model), lambda j, at: (0, 0)),
            scratch_shapes=[
                pltpu.VMEM((quarter, model), bf16),
                pltpu.VMEM((quarter, hidden_units), bf16),
                pltpu.VMEM((quarter, hidden_units), bf16),
                pltpu.VMEM((quarter, model), f32),
            ],
        ),
        out_shape=jax.ShapeDtypeStruct((quarter, model), bf16),
        compiler_params=params(),
        cost_estimate=cost(6 * quarter * model * hidden_units, 6 * model * hidden_units),
        name="first_two_grad",
    )(at, weights, weights, weights, gate, up, normed, inverse, *operands)


def put_at(place, value, refs):
    for index, ref in enumerate(refs):

        @pl.when(place == index)
        def _(ref=ref):
            ref[...] = value


def two_grad_kernel(order_ref, *refs):
    pieces = (len(refs) - 3) // 5
    row_refs = refs[: 4 * pieces]
    gate_ref, up_ref = refs[4 * pieces : 4 * pieces + 2]
    out_refs, total = refs[4 * pieces + 2 : -1], refs[-1]
    step = pl.program_id(0)
    columns = pl.ds(pl.multiple_of(step * WIDE, WIDE), WIDE)
    for piece in range(pieces):
        total[piece, :, columns] = times_transposed(
            row_refs[4 * piece][...], gate_ref[0]
        ) + times_transposed(row_refs[4 * piece + 1][...], up_ref[0])

    @pl.when(step == pl.num_programs(0) - 1)
    def _():
        for piece in range(pieces):
            out_refs[piece][...] = norm_back(
                row_refs[4 * piece + 2][...], row_refs[4 * piece + 3][...], total[piece]
            ).astype(bf16)


def two_grad_pieces(order, dgate, dup, weights, normed, inverse, quarter):
    pieces = order.shape[0]
    hidden_units = dgate.shape[1]
    model = weights.shape[1]
    rows = []
    for p in range(pieces):
        here = lambda j, order, p=p: (order[p], 0)
        rows += [pl.BlockSpec((quarter, hidden_units), here)] * 2
        rows += [pl.BlockSpec((quarter, model), here, pipeline_mode=pl.Buffered(1))]
        rows += [pl.BlockSpec((quarter, 1), here, pipeline_mode=pl.Buffered(1))]
    return pl.pallas_call(
        two_grad_kernel,
        grid_spec=pltpu.PrefetchScalarGridSpec(
            num_scalar_prefetch=1,
            grid=(model // WIDE,),
            in_specs=[
                *rows,
                pl.BlockSpec((1, WIDE, hidden_units), lambda j, order: (0, j, 0)),
                pl.BlockSpec((1, WIDE, hidden_units), lambda j, order: (1, j, 0)),
            ],
            out_specs=[pl.BlockSpec((quarter, model), lambda j, order: (0, 0))] * pieces,
            scratch_shapes=[pltpu.VMEM((pieces, quarter, model), f32)],
        ),
        out_shape=[jax.ShapeDtypeStruct((quarter, model), bf16)] * pieces,
        compiler_params=params(),
        cost_estimate=cost(
            4 * pieces * quarter * model * hidden_units, 4 * model * hidden_units
        ),
        name="two_grad",
    )(order, *([dgate, dup, normed, inverse] * pieces), weights, weights)


def one_grad_kernel(place_ref, dq_ref, dk_ref, dv_ref, weight_ref, unit_ref, inv_ref, *out_refs):
    columns = jnp.concatenate([dq_ref[...], dk_ref[...], dv_ref[...]], axis=1)
    grad = norm_back(
        unit_ref[...], inv_ref[...], times_transposed(columns, weight_ref[...])
    ).astype(bf16)
    width = out_refs[0].shape[1]
    for piece in range(len(out_refs)):
        put_at(place_ref[piece], grad[:, piece * width : (piece + 1) * width], out_refs)


def one_grad_pieces(place, grads, weight, rows, inverse):
    count, local = grads[0].shape
    columns = 3 * local
    pieces = place.shape[0]
    model = rows.shape[1]
    here = lambda i, place: (i, 0)
    return pl.pallas_call(
        one_grad_kernel,
        grid_spec=pltpu.PrefetchScalarGridSpec(
            num_scalar_prefetch=1,
            grid=(count // BLOCK,),
            in_specs=[
                *[pl.BlockSpec((BLOCK, local), here)] * 3,
                pl.BlockSpec(
                    (model, columns), lambda i, place: (0, 0), pipeline_mode=pl.Buffered(1)
                ),
                pl.BlockSpec((BLOCK, model), here),
                pl.BlockSpec((BLOCK, 1), here),
            ],
            out_specs=[pl.BlockSpec((BLOCK, model // pieces), here)] * pieces,
        ),
        out_shape=[jax.ShapeDtypeStruct((count, model // pieces), bf16)] * pieces,
        compiler_params=params(32),
        cost_estimate=cost(
            2 * count * model * columns, 2 * columns * model + 6 * count * columns
        ),
        name="one_grad",
    )(place, *grads, weight, rows, inverse)


def att_grads_kernel(normed_ref, dq_ref, dk_ref, dv_ref, att_ref, hidden_ref, out_ref):
    owner = pl.program_id(0)
    columns = 3 * dq_ref.shape[1]
    grads = jnp.concatenate([dq_ref[...], dk_ref[...], dv_ref[...]], axis=1)
    out_ref[0, :, :columns] = transposed_times(normed_ref[...], grads).astype(bf16)
    model = hidden_ref.shape[1]
    rest = model - columns
    pieces = model // rest
    height = out_ref.shape[1] // pieces
    per_tile = HEAD_DIM // height
    product = transposed_times(att_ref[...], hidden_ref[...]).astype(bf16)
    for place in range(per_tile):

        @pl.when(lax.rem(owner, per_tile) == place)
        def _(place=place):
            for piece in range(pieces):
                out_ref[0, piece * height : (piece + 1) * height, columns:] = product[
                    place * height : (place + 1) * height, piece * rest : (piece + 1) * rest
                ]


def att_grads(normed, qkv_grad, attended, hidden_grad, groups):
    count, model = normed.shape
    local = attended.shape[1]
    columns = 3 * local
    tall = model // groups
    per_tile = HEAD_DIM // (local // groups)
    once = pl.Buffered(1)
    whole = lambda i: (0, 0)
    if tall % HEAD_DIM == 0:
        normed_spec = pl.BlockSpec((count, tall), lambda i: (0, i))
        operand = normed
    else:
        normed_spec = pl.BlockSpec((None, count, tall), lambda i: (i, 0, 0))
        operand = normed.reshape(count, groups, tall).swapaxes(0, 1)
    return pl.pallas_call(
        att_grads_kernel,
        grid=(groups,),
        in_specs=[
            normed_spec,
            *[pl.BlockSpec((count, local), whole, pipeline_mode=once)] * 3,
            pl.BlockSpec((count, HEAD_DIM), lambda i: (0, i // per_tile)),
            pl.BlockSpec((count, model), whole, pipeline_mode=once),
        ],
        out_specs=pl.BlockSpec((1, tall, model), lambda i: (i, 0, 0)),
        out_shape=jax.ShapeDtypeStruct((groups, tall, model), bf16),
        compiler_params=params(32),
        cost_estimate=cost(1000, 1000),
        name="att_grads",
    )(operand, *qkv_grad, attended, hidden_grad)


def mlp_grads_kernel(*refs):
    *operands, out_ref = refs
    count = len(operands) // 2
    total = transposed_times(operands[0][...], operands[count][...])
    for part in range(1, count):
        total += transposed_times(operands[part][...], operands[count + part][...])
    out_ref[0] = total.astype(bf16)


def mlp_grads(which, left, right, before=None):
    rows = left[0].shape[0]
    model, hidden_units = left[0].shape[1], right[0].shape[1]
    once = pl.Buffered(1)
    specs = [pl.BlockSpec((rows, BLOCK), lambda i: (0, i)) for _ in left]
    specs += [
        pl.BlockSpec((rows, hidden_units), lambda i: (0, 0), pipeline_mode=once) for _ in right
    ]
    operands = [*left, *right]
    body = mlp_grads_kernel
    aliases = {}
    if before is not None:
        aliases = {len(operands): 0}
        specs.append(pl.BlockSpec(memory_space=pl.ANY))
        operands.append(before)
        body = lambda *refs: mlp_grads_kernel(*refs[:-2], refs[-1])
    count = rows * len(left)
    return pl.pallas_call(
        body,
        grid=(model // BLOCK,),
        in_specs=specs,
        out_specs=pl.BlockSpec((1, BLOCK, hidden_units), lambda i: (which, i, 0)),
        out_shape=jax.ShapeDtypeStruct((3, model, hidden_units), bf16),
        input_output_aliases=aliases,
        compiler_params=params(32),
        cost_estimate=cost(
            2 * count * model * hidden_units, 2 * model * hidden_units + 4 * count * model
        ),
        name="mlp_grads",
    )(*operands)


def after(value, *others):
    return lax.optimization_barrier((value, *others))[0]


def line_step(block, axis, size, step):
    from_low, from_high = block
    up = [(i, i + 1) for i in range(step - 1, size - 1)]
    down = [(i, i - 1) for i in range(size - step, 0, -1)]
    return lax.ppermute(from_low, axis, up), lax.ppermute(from_high, axis, down)


def chain_gather(block, axis, size, begun=None):
    arrived = list(begun or [])
    for step in range(len(arrived) + 1, size):
        arrived.append(line_step(arrived[-1] if arrived else (block, block), axis, size, step))
    return arrived


def line_whole(own, arrived, axis, size):
    me = lax.axis_index(axis)
    low, high = [pair[0] for pair in arrived], [pair[1] for pair in arrived]
    return [pick(me, owner, own, low, high) for owner in range(size)]


def far_first(size):
    return sorted(range(1, size), key=lambda step: -min(step, size - step))


def sent_on(term, axis, size, step):
    return lax.ppermute(term, axis, [(i, (i + step) % size) for i in range(size)])


def added(own, came):
    for piece in came:
        own = own + piece.astype(f32)
    return own


def on_device(
    tokens,
    cotangent,
    w_query,
    w_key,
    w_value,
    w_out,
    w_gate,
    w_up,
    w_down,
    seq_lengths,
    deal,
    row_dest,
):
    groups = lax.axis_size("fsdp")
    shards = lax.axis_size("tp")
    own_group = lax.axis_index("fsdp")
    own_shard = lax.axis_index("tp")
    capacity = GROUP_CAP
    per_pair = capacity // groups
    quarter = capacity // shards
    head_dim = HEAD_DIM
    given, width = tokens.shape
    model = width * shards
    local_width = w_query.shape[1]
    shard_rows = w_query.shape[0]

    steps = far_first(shards)
    order = jnp.stack([lax.rem(own_shard + step, shards) for step in (*steps, 0)])
    around = jnp.stack([lax.rem(own_shard + step, shards) for step in range(shards)])
    place_of = [0] * shards
    for index, step in enumerate((*steps, 0)):
        place_of[step] = index
    place = jnp.stack(
        [
            sum(
                jnp.where(lax.rem(own_shard + step, shards) == j, place_of[step], 0)
                for step in range(shards)
            )
            for j in range(shards)
        ]
    )

    target = row_dest // capacity
    within = row_dest - target * capacity
    given_index = jnp.arange(given, dtype=jnp.int32)
    earlier = (target[:, None] == target[None, :]) & (
        given_index[None, :] < given_index[:, None]
    )
    slot_of = target * per_pair + jnp.sum(earlier.astype(jnp.int32), axis=1)
    slots = jnp.arange(capacity, dtype=jnp.int32)
    deal_hit = slots[:, None] == slot_of[None, :]
    deal_out = deal_hit.astype(bf16)
    place_high, place_low = (within + 1) // 32, (within + 1) % 32
    lane = jnp.arange(HEAD_DIM, dtype=jnp.int32)[None, :]
    place_columns = jnp.where(
        lane == 0, place_high[:, None], jnp.where(lane == 1, place_low[:, None], 0)
    ).astype(bf16)

    def over_fsdp(rows):
        return lax.all_to_all(rows, "fsdp", split_axis=0, concat_axis=0, tiled=True)

    sent_rows = matmul(deal_out, jnp.concatenate([tokens, place_columns], axis=1)).astype(bf16)
    sent_grads = matmul(deal_out, cotangent).astype(bf16)

    qkv_shard = jnp.concatenate([w_query, w_key, w_value], axis=1)
    full_qkv = lax.all_gather(qkv_shard, "fsdp", axis=0, tiled=True)
    out_came = [sent_on(w_out, "tp", shards, step) for step in range(1, shards)]
    came_rows = over_fsdp(sent_rows)
    mlp_shard = jnp.stack([w_gate, w_up, w_down])
    *out_came, came_rows, sent_grads, mlp_shard = lax.optimization_barrier(
        (*out_came, came_rows, sent_grads, mlp_shard)
    )
    came_place = came_rows[:, width : width + 2].astype(jnp.int32)
    recv_place = came_place[:, 0] * 32 + came_place[:, 1] - 1
    place_in = (slots[:, None] == recv_place[None, :]).astype(bf16)
    out_came = [w_out] + out_came
    out_rows = []
    for owner in range(shards):
        piece = w_out
        for step in range(1, shards):
            piece = jnp.where(own_shard == (owner + step) % shards, out_came[step], piece)
        out_rows.append(piece)
    out_rows = jnp.stack(out_rows)
    full_out = lax.all_gather(out_rows, "fsdp", axis=1, tiled=True).reshape(model, model)

    full_mlp = lax.all_gather(mlp_shard, "fsdp", axis=1, tiled=True)
    buffer_rows = matmul(place_in, came_rows[:, :width]).astype(bf16)
    buffer_grads = matmul(place_in, over_fsdp(after(sent_grads, buffer_rows))).astype(bf16)
    rows_come = chain_gather(buffer_rows, "tp", shards)
    list_index = jnp.sum(jnp.where(deal == own_group, jnp.arange(groups, dtype=jnp.int32), 0))
    lengths = lax.dynamic_index_in_dim(seq_lengths, list_index, 0, keepdims=False)
    segment, position = segments(lengths)
    cosine, sine = rope_tables(position, head_dim)
    segment_column, segment_row = segment[:, None], segment[None, :]
    rows_come[-1], first_grads, segment_column, segment_row, cosine, sine = (
        lax.optimization_barrier(
            (rows_come[-1], buffer_grads, segment_column, segment_row, cosine, sine)
        )
    )
    segment = (segment_column, segment_row)
    me = own_shard[None].astype(jnp.int32)

    full_rows, normed_one, inverse_one = gathered_norm(me, buffer_rows, rows_come)
    first_grads, normed_one = lax.optimization_barrier((first_grads, normed_one))
    grads_begun = line_step((first_grads, first_grads), "tp", shards, 1)
    qkv = project_qkv(normed_one, full_qkv, cosine, sine)
    attended = attend(qkv, segment)
    attended, *grads_begun = lax.optimization_barrier((attended, *grads_begun))
    att_come = chain_gather(attended, "tp", shards)
    *grads_begun, last_low, last_high = lax.optimization_barrier((*grads_begun, *att_come[-1]))
    att_come[-1] = (last_low, last_high)
    grads_come = [grads_begun, line_step(grads_begun, "tp", shards, 2)]
    hidden, normed_two, inverse_two = hidden_and_norm(me, attended, att_come, full_out, full_rows)
    *grads_come[1], normed_two = lax.optimization_barrier((*grads_come[1], normed_two))
    grads_come = chain_gather(first_grads, "tp", shards, grads_come)
    gate, up, activated = mlp_up(normed_two, full_mlp)
    def features_of(rows, owner):
        return lax.dynamic_slice_in_dim(rows, owner * width, width, 1)

    *last, activated = lax.optimization_barrier((*grads_come[-1], activated))
    grads_come[-1] = tuple(last)
    two_first = first_two_grad(
        jnp.stack([order[0], own_shard]),
        first_grads,
        grads_come,
        full_mlp,
        gate,
        up,
        normed_two,
        inverse_two,
        quarter,
    )
    full_grads, gate_grad, up_grad = mlp_down_back(
        me, first_grads, grads_come, full_mlp, after(gate, two_first), up
    )

    def rows_of(rows, owner):
        return lax.dynamic_slice_in_dim(rows, owner * quarter, quarter, 0)

    two_rest = two_grad_pieces(
        order[1:], gate_grad, up_grad, full_mlp, normed_two, inverse_two, quarter
    )
    two_came = [
        sent_on(term, "tp", shards, step)
        for term, step in zip((two_first, *two_rest), steps)
    ]
    grad_mlp = mlp_grads(0, [normed_two], [after(gate_grad, *two_rest)])
    grad_mlp = mlp_grads(1, [normed_two], [up_grad], grad_mlp)
    grad_mlp = mlp_grads(2, [activated], [full_grads], grad_mlp)
    *two_came, grad_mlp = lax.optimization_barrier((*two_came, grad_mlp))
    sum_mlp = lax.psum_scatter(grad_mlp, "fsdp", scatter_dimension=1, tiled=True)
    back_low = added(
        rows_of(full_grads, own_shard).astype(f32) + two_rest[-1].astype(f32), two_came
    ).astype(bf16)
    back_come = [line_step((back_low, back_low), "tp", shards, 1)]
    own_out = lax.dynamic_slice_in_dim(full_out, own_shard * local_width, local_width, 0)

    def att_piece(block):
        return times_transposed(block, own_out).astype(bf16)

    def merged(step):
        low, high = back_come[step - 1]
        if 2 * step < shards:
            return low, high
        both = jnp.where(own_shard >= step, low, high)
        return both, both

    att_pieces = [att_piece(back_low)]
    terms = mlp_pieces(around, after(activated, grad_mlp, back_low), full_mlp, width)
    mlp_come = []
    for step in range(1, shards):
        back_come[-1], mlp_come, terms = lax.optimization_barrier(
            (back_come[-1], mlp_come, terms)
        )
        if step < shards - 1:
            back_come.append(line_step(back_come[-1], "tp", shards, step + 1))
            att_pieces += [att_piece(block) for block in merged(step)]
        low, high = terms[shards - step], terms[step]
        if mlp_come:
            low, high = (
                (term.astype(f32) + came.astype(f32)).astype(bf16)
                for term, came in zip((low, high), mlp_come)
            )
        up = [(i, i + 1) for i in range(step)]
        down = [(i, i - 1) for i in range(shards - 1, shards - 1 - step, -1)]
        mlp_come = [lax.ppermute(low, "tp", up), lax.ppermute(high, "tp", down)]
    att_pieces += [att_piece(block) for block in merged(shards - 1)]
    qkv_grad = attend_back(
        me,
        qkv,
        [att_pieces[0], *att_pieces[1::2], *att_pieces[2::2]],
        segment,
        cosine,
        sine,
    )
    one_terms = one_grad_pieces(place, qkv_grad, full_qkv, normed_one, inverse_one)
    one_came = [
        sent_on(term, "tp", shards, step) for term, step in list(zip(one_terms, steps))[::-1]
    ]
    full_hidden_grad = jnp.concatenate(
        line_whole(after(back_low, *one_terms[:3]), back_come, "tp", shards), axis=0
    )
    *mlp_come, late_grad, _ = lax.optimization_barrier(
        (*mlp_come, tuple(qkv_grad), tuple(one_terms[:3]))
    )
    grad_att = att_grads(
        normed_one, late_grad, attended, full_hidden_grad, groups
    )
    sum_mlp, grad_att = lax.optimization_barrier((sum_mlp, grad_att))
    sum_att = lax.psum_scatter(grad_att, "fsdp", scatter_dimension=0, tiled=False)

    sum_att = sum_att.astype(f32)
    out_part = sum_att[:, 3 * local_width :]
    out_pieces = model // out_part.shape[1]
    out_height = shard_rows // out_pieces
    sum_out = jnp.concatenate(
        [out_part[i * out_height : (i + 1) * out_height] for i in range(out_pieces)], axis=1
    )
    sum_gate, sum_up, sum_down = sum_mlp.astype(f32)
    back_here = added(one_terms[-1].astype(f32), one_came)
    input_here = features_of(full_hidden_grad, own_shard).astype(f32) + back_here
    output_here = (hidden + added(terms[0].astype(f32), mlp_come)).astype(bf16)
    out_came = over_fsdp(
        transposed_times(place_in, after(output_here, grad_att)).astype(bf16)
    )
    output = transposed_times(deal_out, out_came).astype(bf16)
    sent_back = transposed_times(place_in, input_here.astype(bf16)).astype(bf16)
    sums = (
        sum_att[:, : local_width],
        sum_att[:, local_width : 2 * local_width],
        sum_att[:, 2 * local_width : 3 * local_width],
        sum_out,
        sum_gate,
        sum_up,
        sum_down,
    )
    came_back, *sums = lax.optimization_barrier((over_fsdp(sent_back), *sums))
    input_grad = transposed_times(deal_out, came_back).astype(bf16)
    return (output, input_grad, *sums)


def solution(mesh):
    in_specs = (
        P("fsdp", "tp"),
        P("fsdp", "tp"),
        P("fsdp", "tp"),
        P("fsdp", "tp"),
        P("fsdp", "tp"),
        P(("tp", "fsdp"), None),
        P("fsdp", "tp"),
        P("fsdp", "tp"),
        P(("tp", "fsdp"), None),
        P(),
        P(),
        P("fsdp"),
    )
    out_specs = (
        P("fsdp", "tp"),
        P("fsdp", "tp"),
        P("fsdp", "tp"),
        P("fsdp", "tp"),
        P("fsdp", "tp"),
        P(("tp", "fsdp"), None),
        P("fsdp", "tp"),
        P("fsdp", "tp"),
        P(("tp", "fsdp"), None),
    )
    return jax.shard_map(
        on_device, mesh=mesh, in_specs=in_specs, out_specs=out_specs, check_vma=False
    )
```

```python
import jax
import jax.numpy as jnp
from jax import lax
from jax.experimental import pallas as pl
from jax.experimental.pallas import tpu as pltpu
from jax.sharding import PartitionSpec as P

HEAD_DIM = 128
GROUP_CAP = 1024
SEQ_SLOTS = 4

norm_eps = 1e-05
rope_base = 10000.0
bf16 = jnp.bfloat16
f32 = jnp.float32


def matmul(left, right):
    return jnp.dot(left, right, preferred_element_type=f32)


def times_transposed(left, right):
    return lax.dot_general(
        left, right, (((1,), (1,)), ((), ())), preferred_element_type=f32
    )


def transposed_times(left, right):
    return lax.dot_general(
        left, right, (((0,), (0,)), ((), ())), preferred_element_type=f32
    )


def norm_parts(values_in):
    row_mean = jnp.mean(values_in, axis=-1, keepdims=True)
    centered = values_in - row_mean
    variance = jnp.mean(centered * centered, axis=-1, keepdims=True)
    inverse = lax.rsqrt(variance + norm_eps)
    return centered * inverse, inverse


def rope_tables(position, head_dim):
    half_dim = head_dim // 2
    frequency = rope_base ** (-(jnp.arange(half_dim, dtype=f32) * 2.0) / head_dim)
    angles = position.astype(f32)[:, None] * frequency[None, :]
    cosine, sine = jnp.cos(angles), jnp.sin(angles)
    return (
        jnp.concatenate([cosine, cosine], axis=1),
        jnp.concatenate([-sine, sine], axis=1),
    )


def segments(lengths):
    row_index = jnp.arange(GROUP_CAP, dtype=jnp.int32)
    slot_ids = jnp.arange(SEQ_SLOTS, dtype=jnp.int32)
    ends = jnp.sum(
        jnp.where(slot_ids[:, None] <= slot_ids[None, :], lengths[:, None], 0), axis=0
    )
    passed = row_index[:, None] >= ends[None, :]
    segment = jnp.sum(passed.astype(jnp.int32), axis=1)
    begin_row = jnp.max(jnp.where(passed, ends[None, :], 0), axis=1)
    return (segment, row_index - begin_row)


MIB = 1024 * 1024
BLOCK = 256
WIDE = 512


def params(mib=58):
    return pltpu.CompilerParams(vmem_limit_bytes=mib * MIB)


def cost(flops, read, transcendentals=0):
    return pl.CostEstimate(
        flops=int(flops), bytes_accessed=int(read), transcendentals=int(transcendentals)
    )


def half_turn(values_in):
    return pltpu.roll(values_in, HEAD_DIM // 2, 1)


def pick(me, owner, own, low, high):
    piece = own
    for step, (lower, higher) in enumerate(zip(low, high), start=1):
        piece = jnp.where(me == owner + step, lower, piece)
        piece = jnp.where(me == owner - step, higher, piece)
    return piece


def flat(own, arrived):
    return [own, *[low for low, _ in arrived], *[high for _, high in arrived]]


def picked(me, owner, refs):
    steps = len(refs) // 2
    blocks = [ref[...] for ref in refs]
    return pick(me, owner, blocks[0], blocks[1 : 1 + steps], blocks[1 + steps :])


def norm_kernel(me_ref, *refs):
    *come_refs, rows_ref, normed_ref, inverse_ref = refs
    size = len(come_refs) // 2 + 1
    rows = jnp.concatenate([picked(me_ref[0], j, come_refs) for j in range(size)], axis=1)
    rows_ref[...] = rows
    unit, inverse_ref[...] = norm_parts(rows.astype(f32))
    normed_ref[...] = unit.astype(bf16)


def gathered_norm(me, own, arrived):
    count, width = own.shape
    operands = flat(own, arrived)
    model = width * (len(operands) // 2 + 1)
    here = lambda i, me: (i, 0)
    out = jax.ShapeDtypeStruct((count, model), bf16)
    return pl.pallas_call(
        norm_kernel,
        grid_spec=pltpu.PrefetchScalarGridSpec(
            num_scalar_prefetch=1,
            grid=(count // BLOCK,),
            in_specs=[pl.BlockSpec((BLOCK, width), here)] * len(operands),
            out_specs=[
                pl.BlockSpec((BLOCK, model), here),
                pl.BlockSpec((BLOCK, model), here),
                pl.BlockSpec((BLOCK, 1), here),
            ],
        ),
        out_shape=[out, out, jax.ShapeDtypeStruct((count, 1), f32)],
        compiler_params=params(),
        cost_estimate=cost(20 * count * model, 8 * count * model),
        name="gathered_norm",
    )(me, *operands)


def qkv_kernel(rows_ref, wq_ref, wk_ref, wv_ref, cos_ref, sin_ref, *out_refs):
    weight = jnp.concatenate([wq_ref[...], wk_ref[...], wv_ref[...]], axis=1)
    for first in range(0, rows_ref.shape[0], BLOCK):
        rows = pl.ds(first, BLOCK)
        pre = matmul(rows_ref[rows, :], weight)
        for part in range(3):
            piece = pre[:, part * HEAD_DIM : (part + 1) * HEAD_DIM]
            if part < 2:
                piece = piece * cos_ref[rows, :] + half_turn(piece) * sin_ref[rows, :]
            out_refs[part][rows, :] = piece.astype(bf16)


def head_specs(model, heads):
    return [
        pl.BlockSpec((model, HEAD_DIM), lambda h, part=part: (0, part * heads + h))
        for part in range(3)
    ]


def project_qkv(rows, weight, cosine, sine):
    count, model = rows.shape
    columns = weight.shape[1]
    heads = columns // (3 * HEAD_DIM)
    whole = lambda h: (0, 0)
    return pl.pallas_call(
        qkv_kernel,
        grid=(heads,),
        in_specs=[
            pl.BlockSpec((count, model), whole),
            *head_specs(model, heads),
            pl.BlockSpec((count, HEAD_DIM), whole),
            pl.BlockSpec((count, HEAD_DIM), whole),
        ],
        out_specs=[pl.BlockSpec((count, HEAD_DIM), lambda h: (0, h))] * 3,
        out_shape=[jax.ShapeDtypeStruct((count, heads * HEAD_DIM), bf16)] * 3,
        compiler_params=params(),
        cost_estimate=cost(2 * count * model * columns, 2 * model * (count + columns)),
        name="qkv",
    )(rows, weight, weight, weight, cosine, sine)


def masked_softmax(q_rows, k_rows, seg_column, seg_row, row_first):
    scores = times_transposed(q_rows, k_rows) * HEAD_DIM ** (-0.5)
    row = lax.broadcasted_iota(jnp.int32, scores.shape, 0) + row_first
    column = lax.broadcasted_iota(jnp.int32, scores.shape, 1)
    allowed = (seg_column == seg_row) & (column <= row)
    scores = jnp.where(allowed, scores, -1e30)
    exponent = jnp.exp(scores - jnp.max(scores, axis=-1, keepdims=True))
    return exponent * (1.0 / jnp.sum(exponent, axis=-1, keepdims=True))


PAIR = 2 * HEAD_DIM


def attend_kernel(q_ref, k_ref, v_ref, column_ref, row_ref, out_ref):
    block = pl.program_id(1)
    for index in range(k_ref.shape[0] // BLOCK):

        @pl.when(block == index)
        def _(index=index):
            seen = (index + 1) * BLOCK
            for first in range(0, PAIR, HEAD_DIM):
                head = slice(first, first + HEAD_DIM)
                prob = masked_softmax(
                    q_ref[:, head],
                    k_ref[:seen, head],
                    column_ref[...],
                    row_ref[:, :seen],
                    index * BLOCK,
                )
                out_ref[:, head] = matmul(prob.astype(bf16), v_ref[:seen, head]).astype(bf16)


def attend(qkv, segment):
    count, local = qkv[0].shape
    column = lambda h, i: (0, h)
    return pl.pallas_call(
        attend_kernel,
        grid=(local // PAIR, count // BLOCK),
        in_specs=[
            pl.BlockSpec((BLOCK, PAIR), lambda h, i: (i, h)),
            pl.BlockSpec((count, PAIR), column),
            pl.BlockSpec((count, PAIR), column),
            pl.BlockSpec((BLOCK, 1), lambda h, i: (i, 0)),
            pl.BlockSpec((1, count), lambda h, i: (0, 0)),
        ],
        out_specs=pl.BlockSpec((BLOCK, PAIR), lambda h, i: (i, h)),
        out_shape=jax.ShapeDtypeStruct((count, local), bf16),
        compiler_params=params(),
        cost_estimate=cost(4 * count * count * local, 8 * count * local, count * count * 4),
        name="attend",
    )(*qkv, *segment)


def attend_back_kernel(
    me_ref, q_ref, k_ref, v_ref, column_ref, row_ref, cos_ref, sin_ref, *refs
):
    *grad_refs, dq_ref, dk_ref, dv_ref, total = refs
    block = pl.program_id(1)
    scale = HEAD_DIM ** (-0.5)
    blocks = k_ref.shape[0] // BLOCK

    @pl.when(block == 0)
    def _():
        total[...] = jnp.zeros_like(total)

    for index in range(blocks):

        @pl.when(block == index)
        def _(index=index):
            seen = (index + 1) * BLOCK
            grads = picked(me_ref[0], index, grad_refs)
            for first in range(0, PAIR, HEAD_DIM):
                head = slice(first, first + HEAD_DIM)
                q_rows, k_rows, grad = q_ref[:, head], k_ref[:seen, head], grads[:, head]
                prob = masked_softmax(
                    q_rows, k_rows, column_ref[...], row_ref[:, :seen], index * BLOCK
                )
                prob_grad = times_transposed(grad, v_ref[:seen, head])
                delta = jnp.sum(prob_grad * prob, axis=-1, keepdims=True)
                score_grad = (prob * (prob_grad - delta)).astype(bf16)
                total[0, index * BLOCK : seen, head] = matmul(score_grad, k_rows) * scale
                total[1, :seen, head] += transposed_times(score_grad, q_rows) * scale
                total[2, :seen, head] += transposed_times(prob.astype(bf16), grad)

    @pl.when(block == blocks - 1)
    def _():
        for part, out_ref in enumerate((dq_ref, dk_ref, dv_ref)):
            for first in range(0, PAIR, HEAD_DIM):
                head = slice(first, first + HEAD_DIM)
                piece = total[part, :, head]
                if part < 2:
                    piece = piece * cos_ref[...] - half_turn(piece) * sin_ref[...]
                out_ref[:, head] = piece.astype(bf16)


def attend_back(me, qkv, grads, segment, cosine, sine):
    count, local = qkv[0].shape
    whole = lambda h, i, me: (0, 0)
    column = lambda h, i, me: (0, h)
    return pl.pallas_call(
        attend_back_kernel,
        grid_spec=pltpu.PrefetchScalarGridSpec(
            num_scalar_prefetch=1,
            grid=(local // PAIR, count // BLOCK),
            in_specs=[
                pl.BlockSpec((BLOCK, PAIR), lambda h, i, me: (i, h)),
                pl.BlockSpec((count, PAIR), column),
                pl.BlockSpec((count, PAIR), column),
                pl.BlockSpec((BLOCK, 1), lambda h, i, me: (i, 0)),
                pl.BlockSpec((1, count), whole),
                pl.BlockSpec((count, HEAD_DIM), whole),
                pl.BlockSpec((count, HEAD_DIM), whole),
                *[pl.BlockSpec((BLOCK, PAIR), column)] * len(grads),
            ],
            out_specs=[pl.BlockSpec((count, PAIR), column)] * 3,
            scratch_shapes=[pltpu.VMEM((3, count, PAIR), f32)],
        ),
        out_shape=[jax.ShapeDtypeStruct((count, local), bf16)] * 3,
        compiler_params=params(32),
        cost_estimate=cost(1000, 1000),
        name="attend_back",
    )(me, *qkv, *segment, cosine, sine, *grads)


def hidden_kernel(me_ref, weight_ref, rows_ref, *refs):
    *come_refs, hidden_ref, normed_ref, inverse_ref = refs
    size = len(come_refs) // 2 + 1
    attended = jnp.concatenate([picked(me_ref[0], j, come_refs) for j in range(size)], axis=1)
    hidden = rows_ref[...].astype(f32) + matmul(attended, weight_ref[...])
    width = hidden_ref.shape[1]
    own = hidden[:, :width]
    for piece in range(1, size):
        own = jnp.where(me_ref[0] == piece, hidden[:, piece * width : (piece + 1) * width], own)
    hidden_ref[...] = own
    unit, inverse_ref[...] = norm_parts(hidden)
    normed_ref[...] = unit.astype(bf16)


def hidden_and_norm(me, own, arrived, weight, rows):
    count, model = rows.shape
    operands = flat(own, arrived)
    here = lambda i, me: (i, 0)
    return pl.pallas_call(
        hidden_kernel,
        grid_spec=pltpu.PrefetchScalarGridSpec(
            num_scalar_prefetch=1,
            grid=(count // BLOCK,),
            in_specs=[
                pl.BlockSpec((model, model), lambda i, me: (0, 0), pipeline_mode=pl.Buffered(1)),
                pl.BlockSpec((BLOCK, model), here),
                *[pl.BlockSpec((BLOCK, own.shape[1]), here)] * len(operands),
            ],
            out_specs=[
                pl.BlockSpec((BLOCK, own.shape[1]), here),
                pl.BlockSpec((BLOCK, model), here),
                pl.BlockSpec((BLOCK, 1), here),
            ],
        ),
        out_shape=[
            jax.ShapeDtypeStruct(own.shape, f32),
            jax.ShapeDtypeStruct((count, model), bf16),
            jax.ShapeDtypeStruct((count, 1), f32),
        ],
        compiler_params=params(),
        cost_estimate=cost(2 * count * model * model, 2 * model * model + 10 * count * model),
        name="hidden",
    )(me, weight, rows, *operands)


def up_kernel(rows_ref, gate_ref, up_ref, gate_out, up_out, act_ref):
    for first in range(0, rows_ref.shape[0], BLOCK):
        rows = pl.ds(first, BLOCK)
        gate = matmul(rows_ref[rows, :], gate_ref[0])
        up = matmul(rows_ref[rows, :], up_ref[0])
        sigmoid = 1.0 / (1.0 + jnp.exp(-gate))
        silu = gate * sigmoid
        gate_out[rows, :] = (up * (sigmoid + silu * (1.0 - sigmoid))).astype(bf16)
        up_out[rows, :] = silu.astype(bf16)
        act_ref[rows, :] = (silu * up).astype(bf16)


def mlp_up(rows, weights):
    count, model = rows.shape
    hidden_units = weights.shape[2]
    out = jax.ShapeDtypeStruct((count, hidden_units), bf16)
    return pl.pallas_call(
        up_kernel,
        grid=(hidden_units // WIDE,),
        in_specs=[
            pl.BlockSpec((count, model), lambda j: (0, 0)),
            pl.BlockSpec((1, model, WIDE), lambda j: (0, 0, j)),
            pl.BlockSpec((1, model, WIDE), lambda j: (1, 0, j)),
        ],
        out_specs=[pl.BlockSpec((count, WIDE), lambda j: (0, j))] * 3,
        out_shape=[out] * 3,
        compiler_params=params(),
        cost_estimate=cost(
            4 * count * model * hidden_units,
            4 * model * hidden_units + 2 * count * model + 10 * count * hidden_units,
            count * hidden_units,
        ),
        name="mlp_up",
    )(rows, weights, weights)


def down_back_kernel(me_ref, down_ref, gate_in, up_in, *refs):
    *come_refs, grad_ref, dgate_ref, dup_ref = refs
    size = len(come_refs) // 2 + 1
    width = come_refs[0].shape[1]

    @pl.when(pl.program_id(0) == 0)
    def _():
        for owner in range(size):
            grad_ref[:, owner * width : (owner + 1) * width] = picked(
                me_ref[0], owner, come_refs
            )

    for first in range(0, grad_ref.shape[0], BLOCK):
        rows = pl.ds(first, BLOCK)
        down = times_transposed(grad_ref[rows, :], down_ref[0])
        dgate_ref[rows, :] = (down * gate_in[rows, :].astype(f32)).astype(bf16)
        dup_ref[rows, :] = (down * up_in[rows, :].astype(f32)).astype(bf16)


def mlp_down_back(me, own, arrived, weights, gate, up):
    operands = flat(own, arrived)
    count, width = own.shape
    model = width * (len(operands) // 2 + 1)
    hidden_units = weights.shape[2]
    part = pl.BlockSpec((count, WIDE), lambda j, me: (0, j))
    whole = lambda j, me: (0, 0)
    out = jax.ShapeDtypeStruct((count, hidden_units), bf16)
    return pl.pallas_call(
        down_back_kernel,
        grid_spec=pltpu.PrefetchScalarGridSpec(
            num_scalar_prefetch=1,
            grid=(hidden_units // WIDE,),
            in_specs=[
                pl.BlockSpec((1, WIDE, model), lambda j, me: (2, j, 0)),
                part,
                part,
                *[pl.BlockSpec((count, width), whole, pipeline_mode=pl.Buffered(1))]
                * len(operands),
            ],
            out_specs=[pl.BlockSpec((count, model), whole), part, part],
        ),
        out_shape=[jax.ShapeDtypeStruct((count, model), bf16), out, out],
        compiler_params=params(),
        cost_estimate=cost(
            2 * count * model * hidden_units,
            2 * model * hidden_units + 2 * count * model + 12 * count * hidden_units,
            count * hidden_units,
        ),
        name="mlp_down_back",
    )(me, weights, gate, up, *operands)


def mlp_piece_kernel(order_ref, act_ref, down_ref, *out_refs):
    for piece, out_ref in enumerate(out_refs):

        @pl.when(pl.program_id(0) == piece)
        def _(out_ref=out_ref):
            for first in range(0, act_ref.shape[0], BLOCK):
                rows = pl.ds(first, BLOCK)
                out_ref[rows, :] = matmul(act_ref[rows, :], down_ref[0]).astype(bf16)


def mlp_pieces(order, act, weights, width):
    count, hidden_units = act.shape
    pieces = order.shape[0]
    whole = lambda g, order: (0, 0)
    return pl.pallas_call(
        mlp_piece_kernel,
        grid_spec=pltpu.PrefetchScalarGridSpec(
            num_scalar_prefetch=1,
            grid=(pieces,),
            in_specs=[
                pl.BlockSpec((count, hidden_units), whole, pipeline_mode=pl.Buffered(1)),
                pl.BlockSpec((1, hidden_units, width), lambda g, order: (2, 0, order[g])),
            ],
            out_specs=[pl.BlockSpec((count, width), whole)] * pieces,
        ),
        out_shape=[jax.ShapeDtypeStruct((count, width), bf16)] * pieces,
        compiler_params=params(32),
        cost_estimate=cost(
            2 * pieces * count * width * hidden_units, 2 * pieces * width * hidden_units
        ),
        name="mlp_piece",
    )(order, act, weights)


def norm_back(unit_rows, inverse, grad_in):
    unit_rows = unit_rows.astype(f32)
    return inverse * (
        grad_in
        - jnp.mean(grad_in, axis=-1, keepdims=True)
        - unit_rows * jnp.mean(grad_in * unit_rows, axis=-1, keepdims=True)
    )


def first_two_kernel(at_ref, *refs):
    (down_ref, gate_ref, up_ref, gate_in, up_in, normed_ref, inverse_ref) = refs[:7]
    *come_refs, out_ref, grad_ref, dgate_ref, dup_ref, total = refs[7:]
    step, half = pl.program_id(0), pl.num_programs(0) // 2
    size = len(come_refs) // 2 + 1
    width = come_refs[0].shape[1]

    @pl.when(step == 0)
    def _():
        for owner in range(size):
            grad_ref[:, owner * width : (owner + 1) * width] = picked(
                at_ref[1], owner, come_refs
            )

    @pl.when(step < half)
    def _():
        columns = pl.ds(pl.multiple_of(step * WIDE, WIDE), WIDE)
        down = times_transposed(grad_ref[...], down_ref[0])
        dgate_ref[:, columns] = (down * gate_in[...].astype(f32)).astype(bf16)
        dup_ref[:, columns] = (down * up_in[...].astype(f32)).astype(bf16)

    @pl.when(step >= half)
    def _():
        columns = pl.ds(pl.multiple_of((step - half) * WIDE, WIDE), WIDE)
        total[:, columns] = times_transposed(dgate_ref[...], gate_ref[0]) + times_transposed(
            dup_ref[...], up_ref[0]
        )

    @pl.when(step == 2 * half - 1)
    def _():
        out_ref[...] = norm_back(normed_ref[...], inverse_ref[...], total[...]).astype(bf16)


def first_two_grad(at, own, arrived, weights, gate, up, normed, inverse, quarter):
    operands = flat(own, arrived)
    width = own.shape[1]
    hidden_units = gate.shape[1]
    model = weights.shape[1]
    half = hidden_units // WIDE
    first = lambda j: jnp.minimum(j, half - 1)
    second = lambda j: jnp.maximum(j - half, 0)
    rows = lambda j, at: (at[0], 0)
    part = pl.BlockSpec((quarter, WIDE), lambda j, at: (at[0], first(j)))
    once = pl.Buffered(1)
    return pl.pallas_call(
        first_two_kernel,
        grid_spec=pltpu.PrefetchScalarGridSpec(
            num_scalar_prefetch=1,
            grid=(2 * half,),
            in_specs=[
                pl.BlockSpec((1, WIDE, model), lambda j, at: (2, first(j), 0)),
                pl.BlockSpec((1, WIDE, hidden_units), lambda j, at: (0, second(j), 0)),
                pl.BlockSpec((1, WIDE, hidden_units), lambda j, at: (1, second(j), 0)),
                part,
                part,
                pl.BlockSpec((quarter, model), rows, pipeline_mode=once),
                pl.BlockSpec((quarter, 1), rows, pipeline_mode=once),
                *[pl.BlockSpec((quarter, width), rows, pipeline_mode=once)] * len(operands),
            ],
            out_specs=pl.BlockSpec((quarter, model), lambda j, at: (0, 0)),
            scratch_shapes=[
                pltpu.VMEM((quarter, model), bf16),
                pltpu.VMEM((quarter, hidden_units), bf16),
                pltpu.VMEM((quarter, hidden_units), bf16),
                pltpu.VMEM((quarter, model), f32),
            ],
        ),
        out_shape=jax.ShapeDtypeStruct((quarter, model), bf16),
        compiler_params=params(),
        cost_estimate=cost(6 * quarter * model * hidden_units, 6 * model * hidden_units),
        name="first_two_grad",
    )(at, weights, weights, weights, gate, up, normed, inverse, *operands)


def put_at(place, value, refs):
    for index, ref in enumerate(refs):

        @pl.when(place == index)
        def _(ref=ref):
            ref[...] = value


def two_grad_kernel(order_ref, *refs):
    pieces = (len(refs) - 3) // 5
    row_refs = refs[: 4 * pieces]
    gate_ref, up_ref = refs[4 * pieces : 4 * pieces + 2]
    out_refs, total = refs[4 * pieces + 2 : -1], refs[-1]
    step = pl.program_id(0)
    columns = pl.ds(pl.multiple_of(step * WIDE, WIDE), WIDE)
    for piece in range(pieces):
        total[piece, :, columns] = times_transposed(
            row_refs[4 * piece][...], gate_ref[0]
        ) + times_transposed(row_refs[4 * piece + 1][...], up_ref[0])

    @pl.when(step == pl.num_programs(0) - 1)
    def _():
        for piece in range(pieces):
            out_refs[piece][...] = norm_back(
                row_refs[4 * piece + 2][...], row_refs[4 * piece + 3][...], total[piece]
            ).astype(bf16)


def two_grad_pieces(order, dgate, dup, weights, normed, inverse, quarter):
    pieces = order.shape[0]
    hidden_units = dgate.shape[1]
    model = weights.shape[1]
    rows = []
    for p in range(pieces):
        here = lambda j, order, p=p: (order[p], 0)
        rows += [pl.BlockSpec((quarter, hidden_units), here)] * 2
        rows += [pl.BlockSpec((quarter, model), here, pipeline_mode=pl.Buffered(1))]
        rows += [pl.BlockSpec((quarter, 1), here, pipeline_mode=pl.Buffered(1))]
    return pl.pallas_call(
        two_grad_kernel,
        grid_spec=pltpu.PrefetchScalarGridSpec(
            num_scalar_prefetch=1,
            grid=(model // WIDE,),
            in_specs=[
                *rows,
                pl.BlockSpec((1, WIDE, hidden_units), lambda j, order: (0, j, 0)),
                pl.BlockSpec((1, WIDE, hidden_units), lambda j, order: (1, j, 0)),
            ],
            out_specs=[pl.BlockSpec((quarter, model), lambda j, order: (0, 0))] * pieces,
            scratch_shapes=[pltpu.VMEM((pieces, quarter, model), f32)],
        ),
        out_shape=[jax.ShapeDtypeStruct((quarter, model), bf16)] * pieces,
        compiler_params=params(),
        cost_estimate=cost(
            4 * pieces * quarter * model * hidden_units, 4 * model * hidden_units
        ),
        name="two_grad",
    )(order, *([dgate, dup, normed, inverse] * pieces), weights, weights)


def one_grad_kernel(place_ref, dq_ref, dk_ref, dv_ref, weight_ref, unit_ref, inv_ref, *out_refs):
    columns = jnp.concatenate([dq_ref[...], dk_ref[...], dv_ref[...]], axis=1)
    grad = norm_back(
        unit_ref[...], inv_ref[...], times_transposed(columns, weight_ref[...])
    ).astype(bf16)
    width = out_refs[0].shape[1]
    for piece in range(len(out_refs)):
        put_at(place_ref[piece], grad[:, piece * width : (piece + 1) * width], out_refs)


def one_grad_pieces(place, grads, weight, rows, inverse):
    count, local = grads[0].shape
    columns = 3 * local
    pieces = place.shape[0]
    model = rows.shape[1]
    here = lambda i, place: (i, 0)
    return pl.pallas_call(
        one_grad_kernel,
        grid_spec=pltpu.PrefetchScalarGridSpec(
            num_scalar_prefetch=1,
            grid=(count // BLOCK,),
            in_specs=[
                *[pl.BlockSpec((BLOCK, local), here)] * 3,
                pl.BlockSpec(
                    (model, columns), lambda i, place: (0, 0), pipeline_mode=pl.Buffered(1)
                ),
                pl.BlockSpec((BLOCK, model), here),
                pl.BlockSpec((BLOCK, 1), here),
            ],
            out_specs=[pl.BlockSpec((BLOCK, model // pieces), here)] * pieces,
        ),
        out_shape=[jax.ShapeDtypeStruct((count, model // pieces), bf16)] * pieces,
        compiler_params=params(32),
        cost_estimate=cost(
            2 * count * model * columns, 2 * columns * model + 6 * count * columns
        ),
        name="one_grad",
    )(place, *grads, weight, rows, inverse)


def att_grads_kernel(normed_ref, dq_ref, dk_ref, dv_ref, att_ref, hidden_ref, out_ref):
    owner = pl.program_id(0)
    columns = 3 * dq_ref.shape[1]
    grads = jnp.concatenate([dq_ref[...], dk_ref[...], dv_ref[...]], axis=1)
    out_ref[0, :, :columns] = transposed_times(normed_ref[...], grads).astype(bf16)
    model = hidden_ref.shape[1]
    rest = model - columns
    pieces = model // rest
    height = out_ref.shape[1] // pieces
    per_tile = HEAD_DIM // height
    product = transposed_times(att_ref[...], hidden_ref[...]).astype(bf16)
    for place in range(per_tile):

        @pl.when(lax.rem(owner, per_tile) == place)
        def _(place=place):
            for piece in range(pieces):
                out_ref[0, piece * height : (piece + 1) * height, columns:] = product[
                    place * height : (place + 1) * height, piece * rest : (piece + 1) * rest
                ]


def att_grads(normed, qkv_grad, attended, hidden_grad, groups):
    count, model = normed.shape
    local = attended.shape[1]
    columns = 3 * local
    tall = model // groups
    per_tile = HEAD_DIM // (local // groups)
    once = pl.Buffered(1)
    whole = lambda i: (0, 0)
    if tall % HEAD_DIM == 0:
        normed_spec = pl.BlockSpec((count, tall), lambda i: (0, i))
        operand = normed
    else:
        normed_spec = pl.BlockSpec((None, count, tall), lambda i: (i, 0, 0))
        operand = normed.reshape(count, groups, tall).swapaxes(0, 1)
    return pl.pallas_call(
        att_grads_kernel,
        grid=(groups,),
        in_specs=[
            normed_spec,
            *[pl.BlockSpec((count, local), whole, pipeline_mode=once)] * 3,
            pl.BlockSpec((count, HEAD_DIM), lambda i: (0, i // per_tile)),
            pl.BlockSpec((count, model), whole, pipeline_mode=once),
        ],
        out_specs=pl.BlockSpec((1, tall, model), lambda i: (i, 0, 0)),
        out_shape=jax.ShapeDtypeStruct((groups, tall, model), bf16),
        compiler_params=params(),
        cost_estimate=cost(1000, 1000),
        name="att_grads",
    )(operand, *qkv_grad, attended, hidden_grad)


def mlp_grads_kernel(*refs):
    *operands, out_ref = refs
    count = len(operands) // 2
    total = transposed_times(operands[0][...], operands[count][...])
    for part in range(1, count):
        total += transposed_times(operands[part][...], operands[count + part][...])
    out_ref[0] = total.astype(bf16)


def mlp_grads(which, left, right, before=None):
    rows = left[0].shape[0]
    model, hidden_units = left[0].shape[1], right[0].shape[1]
    once = pl.Buffered(1)
    specs = [pl.BlockSpec((rows, BLOCK), lambda i: (0, i)) for _ in left]
    specs += [
        pl.BlockSpec((rows, hidden_units), lambda i: (0, 0), pipeline_mode=once) for _ in right
    ]
    operands = [*left, *right]
    body = mlp_grads_kernel
    aliases = {}
    if before is not None:
        aliases = {len(operands): 0}
        specs.append(pl.BlockSpec(memory_space=pl.ANY))
        operands.append(before)
        body = lambda *refs: mlp_grads_kernel(*refs[:-2], refs[-1])
    count = rows * len(left)
    return pl.pallas_call(
        body,
        grid=(model // BLOCK,),
        in_specs=specs,
        out_specs=pl.BlockSpec((1, BLOCK, hidden_units), lambda i: (which, i, 0)),
        out_shape=jax.ShapeDtypeStruct((3, model, hidden_units), bf16),
        input_output_aliases=aliases,
        compiler_params=params(32),
        cost_estimate=cost(
            2 * count * model * hidden_units, 2 * model * hidden_units + 4 * count * model
        ),
        name="mlp_grads",
    )(*operands)


def after(value, *others):
    return lax.optimization_barrier((value, *others))[0]


def line_step(block, axis, size, step):
    from_low, from_high = block
    up = [(i, i + 1) for i in range(step - 1, size - 1)]
    down = [(i, i - 1) for i in range(size - step, 0, -1)]
    return lax.ppermute(from_low, axis, up), lax.ppermute(from_high, axis, down)


def chain_gather(block, axis, size, begun=None):
    arrived = list(begun or [])
    for step in range(len(arrived) + 1, size):
        arrived.append(line_step(arrived[-1] if arrived else (block, block), axis, size, step))
    return arrived


def line_whole(own, arrived, axis, size):
    me = lax.axis_index(axis)
    low, high = [pair[0] for pair in arrived], [pair[1] for pair in arrived]
    return [pick(me, owner, own, low, high) for owner in range(size)]


def far_first(size):
    return sorted(range(1, size), key=lambda step: -min(step, size - step))


def sent_on(term, axis, size, step):
    return lax.ppermute(term, axis, [(i, (i + step) % size) for i in range(size)])


def added(own, came):
    for piece in came:
        own = own + piece.astype(f32)
    return own


def on_device(
    tokens,
    cotangent,
    w_query,
    w_key,
    w_value,
    w_out,
    w_gate,
    w_up,
    w_down,
    seq_lengths,
    deal,
    row_dest,
):
    groups = lax.axis_size("fsdp")
    shards = lax.axis_size("tp")
    own_group = lax.axis_index("fsdp")
    own_shard = lax.axis_index("tp")
    capacity = GROUP_CAP
    per_pair = capacity // groups
    quarter = capacity // shards
    head_dim = HEAD_DIM
    given, width = tokens.shape
    model = width * shards
    local_width = w_query.shape[1]
    shard_rows = w_query.shape[0]

    steps = far_first(shards)
    order = jnp.stack([lax.rem(own_shard + step, shards) for step in (*steps, 0)])
    around = jnp.stack([lax.rem(own_shard + step, shards) for step in range(shards)])
    place_of = [0] * shards
    for index, step in enumerate((*steps, 0)):
        place_of[step] = index
    place = jnp.stack(
        [
            sum(
                jnp.where(lax.rem(own_shard + step, shards) == j, place_of[step], 0)
                for step in range(shards)
            )
            for j in range(shards)
        ]
    )

    target = row_dest // capacity
    within = row_dest - target * capacity
    given_index = jnp.arange(given, dtype=jnp.int32)
    earlier = (target[:, None] == target[None, :]) & (
        given_index[None, :] < given_index[:, None]
    )
    slot_of = target * per_pair + jnp.sum(earlier.astype(jnp.int32), axis=1)
    slots = jnp.arange(capacity, dtype=jnp.int32)
    deal_hit = slots[:, None] == slot_of[None, :]
    deal_out = deal_hit.astype(bf16)
    place_high, place_low = (within + 1) // 32, (within + 1) % 32
    lane = jnp.arange(HEAD_DIM, dtype=jnp.int32)[None, :]
    place_columns = jnp.where(
        lane == 0, place_high[:, None], jnp.where(lane == 1, place_low[:, None], 0)
    ).astype(bf16)

    def over_fsdp(rows):
        return lax.all_to_all(rows, "fsdp", split_axis=0, concat_axis=0, tiled=True)

    sent_rows = matmul(deal_out, jnp.concatenate([tokens, place_columns], axis=1)).astype(bf16)
    sent_grads = matmul(deal_out, cotangent).astype(bf16)

    qkv_shard = jnp.concatenate([w_query, w_key, w_value], axis=1)
    full_qkv = lax.all_gather(qkv_shard, "fsdp", axis=0, tiled=True)
    out_came = [sent_on(w_out, "tp", shards, step) for step in range(1, shards)]
    came_rows = over_fsdp(sent_rows)
    mlp_shard = jnp.stack([w_gate, w_up, w_down])
    *out_came, came_rows, sent_grads, mlp_shard = lax.optimization_barrier(
        (*out_came, came_rows, sent_grads, mlp_shard)
    )
    came_place = came_rows[:, width : width + 2].astype(jnp.int32)
    recv_place = came_place[:, 0] * 32 + came_place[:, 1] - 1
    place_in = (slots[:, None] == recv_place[None, :]).astype(bf16)
    out_came = [w_out] + out_came
    out_rows = []
    for owner in range(shards):
        piece = w_out
        for step in range(1, shards):
            piece = jnp.where(own_shard == (owner + step) % shards, out_came[step], piece)
        out_rows.append(piece)
    out_rows = jnp.stack(out_rows)
    full_out = lax.all_gather(out_rows, "fsdp", axis=1, tiled=True).reshape(model, model)

    full_mlp = lax.all_gather(mlp_shard, "fsdp", axis=1, tiled=True)
    buffer_rows = matmul(place_in, came_rows[:, :width]).astype(bf16)
    buffer_grads = matmul(place_in, over_fsdp(after(sent_grads, buffer_rows))).astype(bf16)
    rows_come = chain_gather(buffer_rows, "tp", shards)
    list_index = jnp.sum(jnp.where(deal == own_group, jnp.arange(groups, dtype=jnp.int32), 0))
    lengths = lax.dynamic_index_in_dim(seq_lengths, list_index, 0, keepdims=False)
    segment, position = segments(lengths)
    cosine, sine = rope_tables(position, head_dim)
    segment_column, segment_row = segment[:, None], segment[None, :]
    rows_come[-1], first_grads, segment_column, segment_row, cosine, sine = (
        lax.optimization_barrier(
            (rows_come[-1], buffer_grads, segment_column, segment_row, cosine, sine)
        )
    )
    segment = (segment_column, segment_row)
    me = own_shard[None].astype(jnp.int32)

    full_rows, normed_one, inverse_one = gathered_norm(me, buffer_rows, rows_come)
    first_grads, normed_one = lax.optimization_barrier((first_grads, normed_one))
    grads_begun = line_step((first_grads, first_grads), "tp", shards, 1)
    qkv = project_qkv(normed_one, full_qkv, cosine, sine)
    attended = attend(qkv, segment)
    attended, *grads_begun = lax.optimization_barrier((attended, *grads_begun))
    att_come = chain_gather(attended, "tp", shards)
    *grads_begun, last_low, last_high = lax.optimization_barrier((*grads_begun, *att_come[-1]))
    att_come[-1] = (last_low, last_high)
    grads_come = [grads_begun, line_step(grads_begun, "tp", shards, 2)]
    hidden, normed_two, inverse_two = hidden_and_norm(me, attended, att_come, full_out, full_rows)
    *grads_come[1], normed_two = lax.optimization_barrier((*grads_come[1], normed_two))
    grads_come = chain_gather(first_grads, "tp", shards, grads_come)
    gate, up, activated = mlp_up(normed_two, full_mlp)
    def features_of(rows, owner):
        return lax.dynamic_slice_in_dim(rows, owner * width, width, 1)

    *last, activated = lax.optimization_barrier((*grads_come[-1], activated))
    grads_come[-1] = tuple(last)
    two_first = first_two_grad(
        jnp.stack([order[0], own_shard]),
        first_grads,
        grads_come,
        full_mlp,
        gate,
        up,
        normed_two,
        inverse_two,
        quarter,
    )
    full_grads, gate_grad, up_grad = mlp_down_back(
        me, first_grads, grads_come, full_mlp, after(gate, two_first), up
    )

    def rows_of(rows, owner):
        return lax.dynamic_slice_in_dim(rows, owner * quarter, quarter, 0)

    two_rest = two_grad_pieces(
        order[1:], gate_grad, up_grad, full_mlp, normed_two, inverse_two, quarter
    )
    two_came = [
        sent_on(term, "tp", shards, step)
        for term, step in zip((two_first, *two_rest), steps)
    ]
    grad_mlp = mlp_grads(0, [normed_two], [after(gate_grad, *two_rest)])
    grad_mlp = mlp_grads(1, [normed_two], [up_grad], grad_mlp)
    grad_mlp = mlp_grads(2, [activated], [full_grads], grad_mlp)
    *two_came, grad_mlp = lax.optimization_barrier((*two_came, grad_mlp))
    sum_mlp = lax.psum_scatter(grad_mlp, "fsdp", scatter_dimension=1, tiled=True)
    back_low = added(
        rows_of(full_grads, own_shard).astype(f32) + two_rest[-1].astype(f32), two_came
    ).astype(bf16)
    back_come = [line_step((back_low, back_low), "tp", shards, 1)]
    own_out = lax.dynamic_slice_in_dim(full_out, own_shard * local_width, local_width, 0)

    def att_piece(block):
        return times_transposed(block, own_out).astype(bf16)

    def merged(step):
        low, high = back_come[step - 1]
        if 2 * step < shards:
            return low, high
        both = jnp.where(own_shard >= step, low, high)
        return both, both

    att_pieces = [att_piece(back_low)]
    terms = mlp_pieces(around, after(activated, grad_mlp, back_low), full_mlp, width)
    mlp_come = []
    for step in range(1, shards):
        back_come[-1], mlp_come, terms = lax.optimization_barrier(
            (back_come[-1], mlp_come, terms)
        )
        if step < shards - 1:
            back_come.append(line_step(back_come[-1], "tp", shards, step + 1))
            att_pieces += [att_piece(block) for block in merged(step)]
        low, high = terms[shards - step], terms[step]
        if mlp_come:
            low, high = (
                (term.astype(f32) + came.astype(f32)).astype(bf16)
                for term, came in zip((low, high), mlp_come)
            )
        up = [(i, i + 1) for i in range(step)]
        down = [(i, i - 1) for i in range(shards - 1, shards - 1 - step, -1)]
        mlp_come = [lax.ppermute(low, "tp", up), lax.ppermute(high, "tp", down)]
    att_pieces += [att_piece(block) for block in merged(shards - 1)]
    qkv_grad = attend_back(
        me,
        qkv,
        [att_pieces[0], *att_pieces[1::2], *att_pieces[2::2]],
        segment,
        cosine,
        sine,
    )
    one_terms = one_grad_pieces(place, qkv_grad, full_qkv, normed_one, inverse_one)
    one_came = [
        sent_on(term, "tp", shards, step) for term, step in list(zip(one_terms, steps))[::-1]
    ]
    full_hidden_grad = jnp.concatenate(
        line_whole(after(back_low, *one_terms[:3]), back_come, "tp", shards), axis=0
    )
    *mlp_come, late_grad, _ = lax.optimization_barrier(
        (*mlp_come, tuple(qkv_grad), tuple(one_terms[:3]))
    )
    grad_att = att_grads(
        normed_one, late_grad, attended, full_hidden_grad, groups
    )
    sum_mlp, grad_att = lax.optimization_barrier((sum_mlp, grad_att))
    sum_att = lax.psum_scatter(grad_att, "fsdp", scatter_dimension=0, tiled=False)

    sum_att = sum_att.astype(f32)
    out_part = sum_att[:, 3 * local_width :]
    out_pieces = model // out_part.shape[1]
    out_height = shard_rows // out_pieces
    sum_out = jnp.concatenate(
        [out_part[i * out_height : (i + 1) * out_height] for i in range(out_pieces)], axis=1
    )
    sum_gate, sum_up, sum_down = sum_mlp.astype(f32)
    back_here = added(one_terms[-1].astype(f32), one_came)
    input_here = features_of(full_hidden_grad, own_shard).astype(f32) + back_here
    output_here = (hidden + added(terms[0].astype(f32), mlp_come)).astype(bf16)
    out_came = over_fsdp(
        transposed_times(place_in, after(output_here, grad_att)).astype(bf16)
    )
    output = transposed_times(deal_out, out_came).astype(bf16)
    sent_back = transposed_times(place_in, input_here.astype(bf16)).astype(bf16)
    sums = (
        sum_att[:, : local_width],
        sum_att[:, local_width : 2 * local_width],
        sum_att[:, 2 * local_width : 3 * local_width],
        sum_out,
        sum_gate,
        sum_up,
        sum_down,
    )
    came_back, *sums = lax.optimization_barrier((over_fsdp(sent_back), *sums))
    input_grad = transposed_times(deal_out, came_back).astype(bf16)
    return (output, input_grad, *sums)


def solution(mesh):
    in_specs = (
        P("fsdp", "tp"),
        P("fsdp", "tp"),
        P("fsdp", "tp"),
        P("fsdp", "tp"),
        P("fsdp", "tp"),
        P(("tp", "fsdp"), None),
        P("fsdp", "tp"),
        P("fsdp", "tp"),
        P(("tp", "fsdp"), None),
        P(),
        P(),
        P("fsdp"),
    )
    out_specs = (
        P("fsdp", "tp"),
        P("fsdp", "tp"),
        P("fsdp", "tp"),
        P("fsdp", "tp"),
        P("fsdp", "tp"),
        P(("tp", "fsdp"), None),
        P("fsdp", "tp"),
        P("fsdp", "tp"),
        P(("tp", "fsdp"), None),
    )
    return jax.shard_map(
        on_device, mesh=mesh, in_specs=in_specs, out_specs=out_specs, check_vma=False
    )
```

```python
import jax
import jax.numpy as jnp
from jax import lax
from jax.experimental import pallas as pl
from jax.experimental.pallas import tpu as pltpu
from jax.sharding import PartitionSpec as P

HEAD_DIM = 128
GROUP_CAP = 1024
SEQ_SLOTS = 4

norm_eps = 1e-05
rope_base = 10000.0
bf16 = jnp.bfloat16
f32 = jnp.float32


def matmul(left, right):
    return jnp.dot(left, right, preferred_element_type=f32)


def times_transposed(left, right):
    return lax.dot_general(
        left, right, (((1,), (1,)), ((), ())), preferred_element_type=f32
    )


def transposed_times(left, right):
    return lax.dot_general(
        left, right, (((0,), (0,)), ((), ())), preferred_element_type=f32
    )


def norm_parts(values_in):
    row_mean = jnp.mean(values_in, axis=-1, keepdims=True)
    centered = values_in - row_mean
    variance = jnp.mean(centered * centered, axis=-1, keepdims=True)
    inverse = lax.rsqrt(variance + norm_eps)
    return centered * inverse, inverse


def rope_tables(position, head_dim):
    half_dim = head_dim // 2
    frequency = rope_base ** (-(jnp.arange(half_dim, dtype=f32) * 2.0) / head_dim)
    angles = position.astype(f32)[:, None] * frequency[None, :]
    cosine, sine = jnp.cos(angles), jnp.sin(angles)
    return (
        jnp.concatenate([cosine, cosine], axis=1),
        jnp.concatenate([-sine, sine], axis=1),
    )


def segments(lengths):
    row_index = jnp.arange(GROUP_CAP, dtype=jnp.int32)
    slot_ids = jnp.arange(SEQ_SLOTS, dtype=jnp.int32)
    ends = jnp.sum(
        jnp.where(slot_ids[:, None] <= slot_ids[None, :], lengths[:, None], 0), axis=0
    )
    passed = row_index[:, None] >= ends[None, :]
    segment = jnp.sum(passed.astype(jnp.int32), axis=1)
    begin_row = jnp.max(jnp.where(passed, ends[None, :], 0), axis=1)
    return (segment, row_index - begin_row)


MIB = 1024 * 1024
BLOCK = 256
WIDE = 512


def params(mib=58):
    return pltpu.CompilerParams(vmem_limit_bytes=mib * MIB)


def cost(flops, read, transcendentals=0):
    return pl.CostEstimate(
        flops=int(flops), bytes_accessed=int(read), transcendentals=int(transcendentals)
    )


def half_turn(values_in):
    return pltpu.roll(values_in, HEAD_DIM // 2, 1)


def pick(me, owner, own, low, high):
    piece = own
    for step, (lower, higher) in enumerate(zip(low, high), start=1):
        piece = jnp.where(me == owner + step, lower, piece)
        piece = jnp.where(me == owner - step, higher, piece)
    return piece


def flat(own, arrived):
    return [own, *[low for low, _ in arrived], *[high for _, high in arrived]]


def picked(me, owner, refs):
    steps = len(refs) // 2
    blocks = [ref[...] for ref in refs]
    return pick(me, owner, blocks[0], blocks[1 : 1 + steps], blocks[1 + steps :])


def norm_kernel(me_ref, *refs):
    *come_refs, rows_ref, normed_ref, inverse_ref = refs
    size = len(come_refs) // 2 + 1
    rows = jnp.concatenate([picked(me_ref[0], j, come_refs) for j in range(size)], axis=1)
    rows_ref[...] = rows
    unit, inverse_ref[...] = norm_parts(rows.astype(f32))
    normed_ref[...] = unit.astype(bf16)


def gathered_norm(me, own, arrived):
    count, width = own.shape
    operands = flat(own, arrived)
    model = width * (len(operands) // 2 + 1)
    here = lambda i, me: (i, 0)
    out = jax.ShapeDtypeStruct((count, model), bf16)
    return pl.pallas_call(
        norm_kernel,
        grid_spec=pltpu.PrefetchScalarGridSpec(
            num_scalar_prefetch=1,
            grid=(count // BLOCK,),
            in_specs=[pl.BlockSpec((BLOCK, width), here)] * len(operands),
            out_specs=[
                pl.BlockSpec((BLOCK, model), here),
                pl.BlockSpec((BLOCK, model), here),
                pl.BlockSpec((BLOCK, 1), here),
            ],
        ),
        out_shape=[out, out, jax.ShapeDtypeStruct((count, 1), f32)],
        compiler_params=params(),
        cost_estimate=cost(20 * count * model, 8 * count * model),
        name="gathered_norm",
    )(me, *operands)


def qkv_kernel(rows_ref, wq_ref, wk_ref, wv_ref, cos_ref, sin_ref, *out_refs):
    weight = jnp.concatenate([wq_ref[...], wk_ref[...], wv_ref[...]], axis=1)
    for first in range(0, rows_ref.shape[0], BLOCK):
        rows = pl.ds(first, BLOCK)
        pre = matmul(rows_ref[rows, :], weight)
        for part in range(3):
            piece = pre[:, part * HEAD_DIM : (part + 1) * HEAD_DIM]
            if part < 2:
                piece = piece * cos_ref[rows, :] + half_turn(piece) * sin_ref[rows, :]
            out_refs[part][rows, :] = piece.astype(bf16)


def head_specs(model, heads):
    return [
        pl.BlockSpec((model, HEAD_DIM), lambda h, part=part: (0, part * heads + h))
        for part in range(3)
    ]


def project_qkv(rows, weight, cosine, sine):
    count, model = rows.shape
    columns = weight.shape[1]
    heads = columns // (3 * HEAD_DIM)
    whole = lambda h: (0, 0)
    return pl.pallas_call(
        qkv_kernel,
        grid=(heads,),
        in_specs=[
            pl.BlockSpec((count, model), whole),
            *head_specs(model, heads),
            pl.BlockSpec((count, HEAD_DIM), whole),
            pl.BlockSpec((count, HEAD_DIM), whole),
        ],
        out_specs=[pl.BlockSpec((count, HEAD_DIM), lambda h: (0, h))] * 3,
        out_shape=[jax.ShapeDtypeStruct((count, heads * HEAD_DIM), bf16)] * 3,
        compiler_params=params(),
        cost_estimate=cost(2 * count * model * columns, 2 * model * (count + columns)),
        name="qkv",
    )(rows, weight, weight, weight, cosine, sine)


def masked_softmax(q_rows, k_rows, seg_column, seg_row, row_first):
    scores = times_transposed(q_rows, k_rows) * HEAD_DIM ** (-0.5)
    row = lax.broadcasted_iota(jnp.int32, scores.shape, 0) + row_first
    column = lax.broadcasted_iota(jnp.int32, scores.shape, 1)
    allowed = (seg_column == seg_row) & (column <= row)
    scores = jnp.where(allowed, scores, -1e30)
    exponent = jnp.exp(scores - jnp.max(scores, axis=-1, keepdims=True))
    return exponent * (1.0 / jnp.sum(exponent, axis=-1, keepdims=True))


PAIR = 4 * HEAD_DIM


def attend_kernel(q_ref, k_ref, v_ref, column_ref, row_ref, out_ref):
    block = pl.program_id(1)
    for index in range(k_ref.shape[0] // BLOCK):

        @pl.when(block == index)
        def _(index=index):
            seen = (index + 1) * BLOCK
            for first in range(0, PAIR, HEAD_DIM):
                head = slice(first, first + HEAD_DIM)
                prob = masked_softmax(
                    q_ref[:, head],
                    k_ref[:seen, head],
                    column_ref[...],
                    row_ref[:, :seen],
                    index * BLOCK,
                )
                out_ref[:, head] = matmul(prob.astype(bf16), v_ref[:seen, head]).astype(bf16)


def attend(qkv, segment):
    count, local = qkv[0].shape
    column = lambda h, i: (0, h)
    return pl.pallas_call(
        attend_kernel,
        grid=(local // PAIR, count // BLOCK),
        in_specs=[
            pl.BlockSpec((BLOCK, PAIR), lambda h, i: (i, h)),
            pl.BlockSpec((count, PAIR), column),
            pl.BlockSpec((count, PAIR), column),
            pl.BlockSpec((BLOCK, 1), lambda h, i: (i, 0)),
            pl.BlockSpec((1, count), lambda h, i: (0, 0)),
        ],
        out_specs=pl.BlockSpec((BLOCK, PAIR), lambda h, i: (i, h)),
        out_shape=jax.ShapeDtypeStruct((count, local), bf16),
        compiler_params=params(),
        cost_estimate=cost(4 * count * count * local, 8 * count * local, count * count * 4),
        name="attend",
    )(*qkv, *segment)


def attend_back_kernel(
    me_ref, q_ref, k_ref, v_ref, column_ref, row_ref, cos_ref, sin_ref, *refs
):
    *grad_refs, dq_ref, dk_ref, dv_ref, total = refs
    block = pl.program_id(1)
    scale = HEAD_DIM ** (-0.5)
    blocks = k_ref.shape[0] // BLOCK

    @pl.when(block == 0)
    def _():
        total[...] = jnp.zeros_like(total)

    for index in range(blocks):

        @pl.when(block == index)
        def _(index=index):
            seen = (index + 1) * BLOCK
            grads = picked(me_ref[0], index, grad_refs)
            for first in range(0, PAIR, HEAD_DIM):
                head = slice(first, first + HEAD_DIM)
                q_rows, k_rows, grad = q_ref[:, head], k_ref[:seen, head], grads[:, head]
                prob = masked_softmax(
                    q_rows, k_rows, column_ref[...], row_ref[:, :seen], index * BLOCK
                )
                prob_grad = times_transposed(grad, v_ref[:seen, head])
                delta = jnp.sum(prob_grad * prob, axis=-1, keepdims=True)
                score_grad = (prob * (prob_grad - delta)).astype(bf16)
                total[0, index * BLOCK : seen, head] = matmul(score_grad, k_rows) * scale
                total[1, :seen, head] += transposed_times(score_grad, q_rows) * scale
                total[2, :seen, head] += transposed_times(prob.astype(bf16), grad)

    @pl.when(block == blocks - 1)
    def _():
        for part, out_ref in enumerate((dq_ref, dk_ref, dv_ref)):
            for first in range(0, PAIR, HEAD_DIM):
                head = slice(first, first + HEAD_DIM)
                piece = total[part, :, head]
                if part < 2:
                    piece = piece * cos_ref[...] - half_turn(piece) * sin_ref[...]
                out_ref[:, head] = piece.astype(bf16)


def attend_back(me, qkv, grads, segment, cosine, sine):
    count, local = qkv[0].shape
    whole = lambda h, i, me: (0, 0)
    column = lambda h, i, me: (0, h)
    return pl.pallas_call(
        attend_back_kernel,
        grid_spec=pltpu.PrefetchScalarGridSpec(
            num_scalar_prefetch=1,
            grid=(local // PAIR, count // BLOCK),
            in_specs=[
                pl.BlockSpec((BLOCK, PAIR), lambda h, i, me: (i, h)),
                pl.BlockSpec((count, PAIR), column),
                pl.BlockSpec((count, PAIR), column),
                pl.BlockSpec((BLOCK, 1), lambda h, i, me: (i, 0)),
                pl.BlockSpec((1, count), whole),
                pl.BlockSpec((count, HEAD_DIM), whole),
                pl.BlockSpec((count, HEAD_DIM), whole),
                *[pl.BlockSpec((BLOCK, PAIR), column)] * len(grads),
            ],
            out_specs=[pl.BlockSpec((count, PAIR), column)] * 3,
            scratch_shapes=[pltpu.VMEM((3, count, PAIR), f32)],
        ),
        out_shape=[jax.ShapeDtypeStruct((count, local), bf16)] * 3,
        compiler_params=params(32),
        cost_estimate=cost(1000, 1000),
        name="attend_back",
    )(me, *qkv, *segment, cosine, sine, *grads)


def hidden_kernel(me_ref, weight_ref, rows_ref, *refs):
    *come_refs, hidden_ref, normed_ref, inverse_ref = refs
    size = len(come_refs) // 2 + 1
    attended = jnp.concatenate([picked(me_ref[0], j, come_refs) for j in range(size)], axis=1)
    hidden = rows_ref[...].astype(f32) + matmul(attended, weight_ref[...])
    width = hidden_ref.shape[1]
    own = hidden[:, :width]
    for piece in range(1, size):
        own = jnp.where(me_ref[0] == piece, hidden[:, piece * width : (piece + 1) * width], own)
    hidden_ref[...] = own
    unit, inverse_ref[...] = norm_parts(hidden)
    normed_ref[...] = unit.astype(bf16)


def hidden_and_norm(me, own, arrived, weight, rows):
    count, model = rows.shape
    operands = flat(own, arrived)
    here = lambda i, me: (i, 0)
    return pl.pallas_call(
        hidden_kernel,
        grid_spec=pltpu.PrefetchScalarGridSpec(
            num_scalar_prefetch=1,
            grid=(count // BLOCK,),
            in_specs=[
                pl.BlockSpec((model, model), lambda i, me: (0, 0), pipeline_mode=pl.Buffered(1)),
                pl.BlockSpec((BLOCK, model), here),
                *[pl.BlockSpec((BLOCK, own.shape[1]), here)] * len(operands),
            ],
            out_specs=[
                pl.BlockSpec((BLOCK, own.shape[1]), here),
                pl.BlockSpec((BLOCK, model), here),
                pl.BlockSpec((BLOCK, 1), here),
            ],
        ),
        out_shape=[
            jax.ShapeDtypeStruct(own.shape, f32),
            jax.ShapeDtypeStruct((count, model), bf16),
            jax.ShapeDtypeStruct((count, 1), f32),
        ],
        compiler_params=params(),
        cost_estimate=cost(2 * count * model * model, 2 * model * model + 10 * count * model),
        name="hidden",
    )(me, weight, rows, *operands)


def up_kernel(rows_ref, gate_ref, up_ref, gate_out, up_out, act_ref):
    for first in range(0, rows_ref.shape[0], BLOCK):
        rows = pl.ds(first, BLOCK)
        gate = matmul(rows_ref[rows, :], gate_ref[0])
        up = matmul(rows_ref[rows, :], up_ref[0])
        sigmoid = 1.0 / (1.0 + jnp.exp(-gate))
        silu = gate * sigmoid
        gate_out[rows, :] = (up * (sigmoid + silu * (1.0 - sigmoid))).astype(bf16)
        up_out[rows, :] = silu.astype(bf16)
        act_ref[rows, :] = (silu * up).astype(bf16)


def mlp_up(rows, weights):
    count, model = rows.shape
    hidden_units = weights.shape[2]
    out = jax.ShapeDtypeStruct((count, hidden_units), bf16)
    return pl.pallas_call(
        up_kernel,
        grid=(hidden_units // WIDE,),
        in_specs=[
            pl.BlockSpec((count, model), lambda j: (0, 0)),
            pl.BlockSpec((1, model, WIDE), lambda j: (0, 0, j)),
            pl.BlockSpec((1, model, WIDE), lambda j: (1, 0, j)),
        ],
        out_specs=[pl.BlockSpec((count, WIDE), lambda j: (0, j))] * 3,
        out_shape=[out] * 3,
        compiler_params=params(),
        cost_estimate=cost(
            4 * count * model * hidden_units,
            4 * model * hidden_units + 2 * count * model + 10 * count * hidden_units,
            count * hidden_units,
        ),
        name="mlp_up",
    )(rows, weights, weights)


def down_back_kernel(me_ref, down_ref, gate_in, up_in, *refs):
    *come_refs, grad_ref, dgate_ref, dup_ref = refs
    size = len(come_refs) // 2 + 1
    width = come_refs[0].shape[1]

    @pl.when(pl.program_id(0) == 0)
    def _():
        for owner in range(size):
            grad_ref[:, owner * width : (owner + 1) * width] = picked(
                me_ref[0], owner, come_refs
            )

    for first in range(0, grad_ref.shape[0], BLOCK):
        rows = pl.ds(first, BLOCK)
        down = times_transposed(grad_ref[rows, :], down_ref[0])
        dgate_ref[rows, :] = (down * gate_in[rows, :].astype(f32)).astype(bf16)
        dup_ref[rows, :] = (down * up_in[rows, :].astype(f32)).astype(bf16)


def mlp_down_back(me, own, arrived, weights, gate, up):
    operands = flat(own, arrived)
    count, width = own.shape
    model = width * (len(operands) // 2 + 1)
    hidden_units = weights.shape[2]
    part = pl.BlockSpec((count, WIDE), lambda j, me: (0, j))
    whole = lambda j, me: (0, 0)
    out = jax.ShapeDtypeStruct((count, hidden_units), bf16)
    return pl.pallas_call(
        down_back_kernel,
        grid_spec=pltpu.PrefetchScalarGridSpec(
            num_scalar_prefetch=1,
            grid=(hidden_units // WIDE,),
            in_specs=[
                pl.BlockSpec((1, WIDE, model), lambda j, me: (2, j, 0)),
                part,
                part,
                *[pl.BlockSpec((count, width), whole, pipeline_mode=pl.Buffered(1))]
                * len(operands),
            ],
            out_specs=[pl.BlockSpec((count, model), whole), part, part],
        ),
        out_shape=[jax.ShapeDtypeStruct((count, model), bf16), out, out],
        compiler_params=params(),
        cost_estimate=cost(
            2 * count * model * hidden_units,
            2 * model * hidden_units + 2 * count * model + 12 * count * hidden_units,
            count * hidden_units,
        ),
        name="mlp_down_back",
    )(me, weights, gate, up, *operands)


def mlp_piece_kernel(order_ref, act_ref, down_ref, *out_refs):
    for piece, out_ref in enumerate(out_refs):

        @pl.when(pl.program_id(0) == piece)
        def _(out_ref=out_ref):
            for first in range(0, act_ref.shape[0], BLOCK):
                rows = pl.ds(first, BLOCK)
                out_ref[rows, :] = matmul(act_ref[rows, :], down_ref[0]).astype(bf16)


def mlp_pieces(order, act, weights, width):
    count, hidden_units = act.shape
    pieces = order.shape[0]
    whole = lambda g, order: (0, 0)
    return pl.pallas_call(
        mlp_piece_kernel,
        grid_spec=pltpu.PrefetchScalarGridSpec(
            num_scalar_prefetch=1,
            grid=(pieces,),
            in_specs=[
                pl.BlockSpec((count, hidden_units), whole, pipeline_mode=pl.Buffered(1)),
                pl.BlockSpec((1, hidden_units, width), lambda g, order: (2, 0, order[g])),
            ],
            out_specs=[pl.BlockSpec((count, width), whole)] * pieces,
        ),
        out_shape=[jax.ShapeDtypeStruct((count, width), bf16)] * pieces,
        compiler_params=params(32),
        cost_estimate=cost(
            2 * pieces * count * width * hidden_units, 2 * pieces * width * hidden_units
        ),
        name="mlp_piece",
    )(order, act, weights)


def norm_back(unit_rows, inverse, grad_in):
    unit_rows = unit_rows.astype(f32)
    return inverse * (
        grad_in
        - jnp.mean(grad_in, axis=-1, keepdims=True)
        - unit_rows * jnp.mean(grad_in * unit_rows, axis=-1, keepdims=True)
    )


def first_two_kernel(at_ref, *refs):
    (down_ref, gate_ref, up_ref, gate_in, up_in, normed_ref, inverse_ref) = refs[:7]
    *come_refs, out_ref, grad_ref, dgate_ref, dup_ref, total = refs[7:]
    step, half = pl.program_id(0), pl.num_programs(0) // 2
    size = len(come_refs) // 2 + 1
    width = come_refs[0].shape[1]

    @pl.when(step == 0)
    def _():
        for owner in range(size):
            grad_ref[:, owner * width : (owner + 1) * width] = picked(
                at_ref[1], owner, come_refs
            )

    @pl.when(step < half)
    def _():
        columns = pl.ds(pl.multiple_of(step * WIDE, WIDE), WIDE)
        down = times_transposed(grad_ref[...], down_ref[0])
        dgate_ref[:, columns] = (down * gate_in[...].astype(f32)).astype(bf16)
        dup_ref[:, columns] = (down * up_in[...].astype(f32)).astype(bf16)

    @pl.when(step >= half)
    def _():
        columns = pl.ds(pl.multiple_of((step - half) * WIDE, WIDE), WIDE)
        total[:, columns] = times_transposed(dgate_ref[...], gate_ref[0]) + times_transposed(
            dup_ref[...], up_ref[0]
        )

    @pl.when(step == 2 * half - 1)
    def _():
        out_ref[...] = norm_back(normed_ref[...], inverse_ref[...], total[...]).astype(bf16)


def first_two_grad(at, own, arrived, weights, gate, up, normed, inverse, quarter):
    operands = flat(own, arrived)
    width = own.shape[1]
    hidden_units = gate.shape[1]
    model = weights.shape[1]
    half = hidden_units // WIDE
    first = lambda j: jnp.minimum(j, half - 1)
    second = lambda j: jnp.maximum(j - half, 0)
    rows = lambda j, at: (at[0], 0)
    part = pl.BlockSpec((quarter, WIDE), lambda j, at: (at[0], first(j)))
    once = pl.Buffered(1)
    return pl.pallas_call(
        first_two_kernel,
        grid_spec=pltpu.PrefetchScalarGridSpec(
            num_scalar_prefetch=1,
            grid=(2 * half,),
            in_specs=[
                pl.BlockSpec((1, WIDE, model), lambda j, at: (2, first(j), 0)),
                pl.BlockSpec((1, WIDE, hidden_units), lambda j, at: (0, second(j), 0)),
                pl.BlockSpec((1, WIDE, hidden_units), lambda j, at: (1, second(j), 0)),
                part,
                part,
                pl.BlockSpec((quarter, model), rows, pipeline_mode=once),
                pl.BlockSpec((quarter, 1), rows, pipeline_mode=once),
                *[pl.BlockSpec((quarter, width), rows, pipeline_mode=once)] * len(operands),
            ],
            out_specs=pl.BlockSpec((quarter, model), lambda j, at: (0, 0)),
            scratch_shapes=[
                pltpu.VMEM((quarter, model), bf16),
                pltpu.VMEM((quarter, hidden_units), bf16),
                pltpu.VMEM((quarter, hidden_units), bf16),
                pltpu.VMEM((quarter, model), f32),
            ],
        ),
        out_shape=jax.ShapeDtypeStruct((quarter, model), bf16),
        compiler_params=params(),
        cost_estimate=cost(6 * quarter * model * hidden_units, 6 * model * hidden_units),
        name="first_two_grad",
    )(at, weights, weights, weights, gate, up, normed, inverse, *operands)


def put_at(place, value, refs):
    for index, ref in enumerate(refs):

        @pl.when(place == index)
        def _(ref=ref):
            ref[...] = value


def two_grad_kernel(order_ref, *refs):
    pieces = (len(refs) - 3) // 5
    row_refs = refs[: 4 * pieces]
    gate_ref, up_ref = refs[4 * pieces : 4 * pieces + 2]
    out_refs, total = refs[4 * pieces + 2 : -1], refs[-1]
    step = pl.program_id(0)
    columns = pl.ds(pl.multiple_of(step * WIDE, WIDE), WIDE)
    for piece in range(pieces):
        total[piece, :, columns] = times_transposed(
            row_refs[4 * piece][...], gate_ref[0]
        ) + times_transposed(row_refs[4 * piece + 1][...], up_ref[0])

    @pl.when(step == pl.num_programs(0) - 1)
    def _():
        for piece in range(pieces):
            out_refs[piece][...] = norm_back(
                row_refs[4 * piece + 2][...], row_refs[4 * piece + 3][...], total[piece]
            ).astype(bf16)


def two_grad_pieces(order, dgate, dup, weights, normed, inverse, quarter):
    pieces = order.shape[0]
    hidden_units = dgate.shape[1]
    model = weights.shape[1]
    rows = []
    for p in range(pieces):
        here = lambda j, order, p=p: (order[p], 0)
        rows += [pl.BlockSpec((quarter, hidden_units), here)] * 2
        rows += [pl.BlockSpec((quarter, model), here, pipeline_mode=pl.Buffered(1))]
        rows += [pl.BlockSpec((quarter, 1), here, pipeline_mode=pl.Buffered(1))]
    return pl.pallas_call(
        two_grad_kernel,
        grid_spec=pltpu.PrefetchScalarGridSpec(
            num_scalar_prefetch=1,
            grid=(model // WIDE,),
            in_specs=[
                *rows,
                pl.BlockSpec((1, WIDE, hidden_units), lambda j, order: (0, j, 0)),
                pl.BlockSpec((1, WIDE, hidden_units), lambda j, order: (1, j, 0)),
            ],
            out_specs=[pl.BlockSpec((quarter, model), lambda j, order: (0, 0))] * pieces,
            scratch_shapes=[pltpu.VMEM((pieces, quarter, model), f32)],
        ),
        out_shape=[jax.ShapeDtypeStruct((quarter, model), bf16)] * pieces,
        compiler_params=params(),
        cost_estimate=cost(
            4 * pieces * quarter * model * hidden_units, 4 * model * hidden_units
        ),
        name="two_grad",
    )(order, *([dgate, dup, normed, inverse] * pieces), weights, weights)


def one_grad_kernel(place_ref, dq_ref, dk_ref, dv_ref, weight_ref, unit_ref, inv_ref, *out_refs):
    columns = jnp.concatenate([dq_ref[...], dk_ref[...], dv_ref[...]], axis=1)
    grad = norm_back(
        unit_ref[...], inv_ref[...], times_transposed(columns, weight_ref[...])
    ).astype(bf16)
    width = out_refs[0].shape[1]
    for piece in range(len(out_refs)):
        put_at(place_ref[piece], grad[:, piece * width : (piece + 1) * width], out_refs)


def one_grad_pieces(place, grads, weight, rows, inverse):
    count, local = grads[0].shape
    columns = 3 * local
    pieces = place.shape[0]
    model = rows.shape[1]
    here = lambda i, place: (i, 0)
    return pl.pallas_call(
        one_grad_kernel,
        grid_spec=pltpu.PrefetchScalarGridSpec(
            num_scalar_prefetch=1,
            grid=(count // BLOCK,),
            in_specs=[
                *[pl.BlockSpec((BLOCK, local), here)] * 3,
                pl.BlockSpec(
                    (model, columns), lambda i, place: (0, 0), pipeline_mode=pl.Buffered(1)
                ),
                pl.BlockSpec((BLOCK, model), here),
                pl.BlockSpec((BLOCK, 1), here),
            ],
            out_specs=[pl.BlockSpec((BLOCK, model // pieces), here)] * pieces,
        ),
        out_shape=[jax.ShapeDtypeStruct((count, model // pieces), bf16)] * pieces,
        compiler_params=params(32),
        cost_estimate=cost(
            2 * count * model * columns, 2 * columns * model + 6 * count * columns
        ),
        name="one_grad",
    )(place, *grads, weight, rows, inverse)


def att_grads_kernel(normed_ref, dq_ref, dk_ref, dv_ref, att_ref, hidden_ref, out_ref):
    owner = pl.program_id(0)
    columns = 3 * dq_ref.shape[1]
    grads = jnp.concatenate([dq_ref[...], dk_ref[...], dv_ref[...]], axis=1)
    out_ref[0, :, :columns] = transposed_times(normed_ref[...], grads).astype(bf16)
    model = hidden_ref.shape[1]
    rest = model - columns
    pieces = model // rest
    height = out_ref.shape[1] // pieces
    per_tile = HEAD_DIM // height
    product = transposed_times(att_ref[...], hidden_ref[...]).astype(bf16)
    for place in range(per_tile):

        @pl.when(lax.rem(owner, per_tile) == place)
        def _(place=place):
            for piece in range(pieces):
                out_ref[0, piece * height : (piece + 1) * height, columns:] = product[
                    place * height : (place + 1) * height, piece * rest : (piece + 1) * rest
                ]


def att_grads(normed, qkv_grad, attended, hidden_grad, groups):
    count, model = normed.shape
    local = attended.shape[1]
    columns = 3 * local
    tall = model // groups
    per_tile = HEAD_DIM // (local // groups)
    once = pl.Buffered(1)
    whole = lambda i: (0, 0)
    if tall % HEAD_DIM == 0:
        normed_spec = pl.BlockSpec((count, tall), lambda i: (0, i))
        operand = normed
    else:
        normed_spec = pl.BlockSpec((None, count, tall), lambda i: (i, 0, 0))
        operand = normed.reshape(count, groups, tall).swapaxes(0, 1)
    return pl.pallas_call(
        att_grads_kernel,
        grid=(groups,),
        in_specs=[
            normed_spec,
            *[pl.BlockSpec((count, local), whole, pipeline_mode=once)] * 3,
            pl.BlockSpec((count, HEAD_DIM), lambda i: (0, i // per_tile)),
            pl.BlockSpec((count, model), whole, pipeline_mode=once),
        ],
        out_specs=pl.BlockSpec((1, tall, model), lambda i: (i, 0, 0)),
        out_shape=jax.ShapeDtypeStruct((groups, tall, model), bf16),
        compiler_params=params(32),
        cost_estimate=cost(1000, 1000),
        name="att_grads",
    )(operand, *qkv_grad, attended, hidden_grad)


def mlp_grads_kernel(*refs):
    *operands, out_ref = refs
    count = len(operands) // 2
    total = transposed_times(operands[0][...], operands[count][...])
    for part in range(1, count):
        total += transposed_times(operands[part][...], operands[count + part][...])
    out_ref[0] = total.astype(bf16)


def mlp_grads(which, left, right, before=None):
    rows = left[0].shape[0]
    model, hidden_units = left[0].shape[1], right[0].shape[1]
    once = pl.Buffered(1)
    specs = [pl.BlockSpec((rows, BLOCK), lambda i: (0, i)) for _ in left]
    specs += [
        pl.BlockSpec((rows, hidden_units), lambda i: (0, 0), pipeline_mode=once) for _ in right
    ]
    operands = [*left, *right]
    body = mlp_grads_kernel
    aliases = {}
    if before is not None:
        aliases = {len(operands): 0}
        specs.append(pl.BlockSpec(memory_space=pl.ANY))
        operands.append(before)
        body = lambda *refs: mlp_grads_kernel(*refs[:-2], refs[-1])
    count = rows * len(left)
    return pl.pallas_call(
        body,
        grid=(model // BLOCK,),
        in_specs=specs,
        out_specs=pl.BlockSpec((1, BLOCK, hidden_units), lambda i: (which, i, 0)),
        out_shape=jax.ShapeDtypeStruct((3, model, hidden_units), bf16),
        input_output_aliases=aliases,
        compiler_params=params(32),
        cost_estimate=cost(
            2 * count * model * hidden_units, 2 * model * hidden_units + 4 * count * model
        ),
        name="mlp_grads",
    )(*operands)


def after(value, *others):
    return lax.optimization_barrier((value, *others))[0]


def line_step(block, axis, size, step):
    from_low, from_high = block
    up = [(i, i + 1) for i in range(step - 1, size - 1)]
    down = [(i, i - 1) for i in range(size - step, 0, -1)]
    return lax.ppermute(from_low, axis, up), lax.ppermute(from_high, axis, down)


def chain_gather(block, axis, size, begun=None):
    arrived = list(begun or [])
    for step in range(len(arrived) + 1, size):
        arrived.append(line_step(arrived[-1] if arrived else (block, block), axis, size, step))
    return arrived


def line_whole(own, arrived, axis, size):
    me = lax.axis_index(axis)
    low, high = [pair[0] for pair in arrived], [pair[1] for pair in arrived]
    return [pick(me, owner, own, low, high) for owner in range(size)]


def far_first(size):
    return sorted(range(1, size), key=lambda step: -min(step, size - step))


def sent_on(term, axis, size, step):
    return lax.ppermute(term, axis, [(i, (i + step) % size) for i in range(size)])


def added(own, came):
    for piece in came:
        own = own + piece.astype(f32)
    return own


def on_device(
    tokens,
    cotangent,
    w_query,
    w_key,
    w_value,
    w_out,
    w_gate,
    w_up,
    w_down,
    seq_lengths,
    deal,
    row_dest,
):
    groups = lax.axis_size("fsdp")
    shards = lax.axis_size("tp")
    own_group = lax.axis_index("fsdp")
    own_shard = lax.axis_index("tp")
    capacity = GROUP_CAP
    per_pair = capacity // groups
    quarter = capacity // shards
    head_dim = HEAD_DIM
    given, width = tokens.shape
    model = width * shards
    local_width = w_query.shape[1]
    shard_rows = w_query.shape[0]

    steps = far_first(shards)
    order = jnp.stack([lax.rem(own_shard + step, shards) for step in (*steps, 0)])
    around = jnp.stack([lax.rem(own_shard + step, shards) for step in range(shards)])
    place_of = [0] * shards
    for index, step in enumerate((*steps, 0)):
        place_of[step] = index
    place = jnp.stack(
        [
            sum(
                jnp.where(lax.rem(own_shard + step, shards) == j, place_of[step], 0)
                for step in range(shards)
            )
            for j in range(shards)
        ]
    )

    target = row_dest // capacity
    within = row_dest - target * capacity
    given_index = jnp.arange(given, dtype=jnp.int32)
    earlier = (target[:, None] == target[None, :]) & (
        given_index[None, :] < given_index[:, None]
    )
    slot_of = target * per_pair + jnp.sum(earlier.astype(jnp.int32), axis=1)
    slots = jnp.arange(capacity, dtype=jnp.int32)
    deal_hit = slots[:, None] == slot_of[None, :]
    deal_out = deal_hit.astype(bf16)
    place_high, place_low = (within + 1) // 32, (within + 1) % 32
    lane = jnp.arange(HEAD_DIM, dtype=jnp.int32)[None, :]
    place_columns = jnp.where(
        lane == 0, place_high[:, None], jnp.where(lane == 1, place_low[:, None], 0)
    ).astype(bf16)

    def over_fsdp(rows):
        return lax.all_to_all(rows, "fsdp", split_axis=0, concat_axis=0, tiled=True)

    sent_rows = matmul(deal_out, jnp.concatenate([tokens, place_columns], axis=1)).astype(bf16)
    sent_grads = matmul(deal_out, cotangent).astype(bf16)

    qkv_shard = jnp.concatenate([w_query, w_key, w_value], axis=1)
    full_qkv = lax.all_gather(qkv_shard, "fsdp", axis=0, tiled=True)
    out_came = [sent_on(w_out, "tp", shards, step) for step in range(1, shards)]
    came_rows = over_fsdp(sent_rows)
    mlp_shard = jnp.stack([w_gate, w_up, w_down])
    *out_came, came_rows, sent_grads, mlp_shard = lax.optimization_barrier(
        (*out_came, came_rows, sent_grads, mlp_shard)
    )
    came_place = came_rows[:, width : width + 2].astype(jnp.int32)
    recv_place = came_place[:, 0] * 32 + came_place[:, 1] - 1
    place_in = (slots[:, None] == recv_place[None, :]).astype(bf16)
    out_came = [w_out] + out_came
    out_rows = []
    for owner in range(shards):
        piece = w_out
        for step in range(1, shards):
            piece = jnp.where(own_shard == (owner + step) % shards, out_came[step], piece)
        out_rows.append(piece)
    out_rows = jnp.stack(out_rows)
    full_out = lax.all_gather(out_rows, "fsdp", axis=1, tiled=True).reshape(model, model)

    full_mlp = lax.all_gather(mlp_shard, "fsdp", axis=1, tiled=True)
    buffer_rows = matmul(place_in, came_rows[:, :width]).astype(bf16)
    buffer_grads = matmul(place_in, over_fsdp(after(sent_grads, buffer_rows))).astype(bf16)
    rows_come = chain_gather(buffer_rows, "tp", shards)
    list_index = jnp.sum(jnp.where(deal == own_group, jnp.arange(groups, dtype=jnp.int32), 0))
    lengths = lax.dynamic_index_in_dim(seq_lengths, list_index, 0, keepdims=False)
    segment, position = segments(lengths)
    cosine, sine = rope_tables(position, head_dim)
    segment_column, segment_row = segment[:, None], segment[None, :]
    rows_come[-1], first_grads, segment_column, segment_row, cosine, sine = (
        lax.optimization_barrier(
            (rows_come[-1], buffer_grads, segment_column, segment_row, cosine, sine)
        )
    )
    segment = (segment_column, segment_row)
    me = own_shard[None].astype(jnp.int32)

    full_rows, normed_one, inverse_one = gathered_norm(me, buffer_rows, rows_come)
    first_grads, normed_one = lax.optimization_barrier((first_grads, normed_one))
    grads_begun = line_step((first_grads, first_grads), "tp", shards, 1)
    qkv = project_qkv(normed_one, full_qkv, cosine, sine)
    attended = attend(qkv, segment)
    attended, *grads_begun = lax.optimization_barrier((attended, *grads_begun))
    att_come = chain_gather(attended, "tp", shards)
    *grads_begun, last_low, last_high = lax.optimization_barrier((*grads_begun, *att_come[-1]))
    att_come[-1] = (last_low, last_high)
    grads_come = [grads_begun, line_step(grads_begun, "tp", shards, 2)]
    hidden, normed_two, inverse_two = hidden_and_norm(me, attended, att_come, full_out, full_rows)
    *grads_come[1], normed_two = lax.optimization_barrier((*grads_come[1], normed_two))
    grads_come = chain_gather(first_grads, "tp", shards, grads_come)
    gate, up, activated = mlp_up(normed_two, full_mlp)
    def features_of(rows, owner):
        return lax.dynamic_slice_in_dim(rows, owner * width, width, 1)

    *last, activated = lax.optimization_barrier((*grads_come[-1], activated))
    grads_come[-1] = tuple(last)
    two_first = first_two_grad(
        jnp.stack([order[0], own_shard]),
        first_grads,
        grads_come,
        full_mlp,
        gate,
        up,
        normed_two,
        inverse_two,
        quarter,
    )
    full_grads, gate_grad, up_grad = mlp_down_back(
        me, first_grads, grads_come, full_mlp, after(gate, two_first), up
    )

    def rows_of(rows, owner):
        return lax.dynamic_slice_in_dim(rows, owner * quarter, quarter, 0)

    two_rest = two_grad_pieces(
        order[1:], gate_grad, up_grad, full_mlp, normed_two, inverse_two, quarter
    )
    two_came = [
        sent_on(term, "tp", shards, step)
        for term, step in zip((two_first, *two_rest), steps)
    ]
    grad_mlp = mlp_grads(0, [normed_two], [after(gate_grad, *two_rest)])
    grad_mlp = mlp_grads(1, [normed_two], [up_grad], grad_mlp)
    grad_mlp = mlp_grads(2, [activated], [full_grads], grad_mlp)
    *two_came, grad_mlp = lax.optimization_barrier((*two_came, grad_mlp))
    sum_mlp = lax.psum_scatter(grad_mlp, "fsdp", scatter_dimension=1, tiled=True)
    back_low = added(
        rows_of(full_grads, own_shard).astype(f32) + two_rest[-1].astype(f32), two_came
    ).astype(bf16)
    back_come = [line_step((back_low, back_low), "tp", shards, 1)]
    own_out = lax.dynamic_slice_in_dim(full_out, own_shard * local_width, local_width, 0)

    def att_piece(block):
        return times_transposed(block, own_out).astype(bf16)

    def merged(step):
        low, high = back_come[step - 1]
        if 2 * step < shards:
            return low, high
        both = jnp.where(own_shard >= step, low, high)
        return both, both

    att_pieces = [att_piece(back_low)]
    terms = mlp_pieces(around, after(activated, grad_mlp, back_low), full_mlp, width)
    mlp_come = []
    for step in range(1, shards):
        back_come[-1], mlp_come, terms = lax.optimization_barrier(
            (back_come[-1], mlp_come, terms)
        )
        if step < shards - 1:
            back_come.append(line_step(back_come[-1], "tp", shards, step + 1))
            att_pieces += [att_piece(block) for block in merged(step)]
        low, high = terms[shards - step], terms[step]
        if mlp_come:
            low, high = (
                (term.astype(f32) + came.astype(f32)).astype(bf16)
                for term, came in zip((low, high), mlp_come)
            )
        up = [(i, i + 1) for i in range(step)]
        down = [(i, i - 1) for i in range(shards - 1, shards - 1 - step, -1)]
        mlp_come = [lax.ppermute(low, "tp", up), lax.ppermute(high, "tp", down)]
    att_pieces += [att_piece(block) for block in merged(shards - 1)]
    qkv_grad = attend_back(
        me,
        qkv,
        [att_pieces[0], *att_pieces[1::2], *att_pieces[2::2]],
        segment,
        cosine,
        sine,
    )
    one_terms = one_grad_pieces(place, qkv_grad, full_qkv, normed_one, inverse_one)
    one_came = [
        sent_on(term, "tp", shards, step) for term, step in list(zip(one_terms, steps))[::-1]
    ]
    full_hidden_grad = jnp.concatenate(
        line_whole(after(back_low, *one_terms[:3]), back_come, "tp", shards), axis=0
    )
    *mlp_come, late_grad, _ = lax.optimization_barrier(
        (*mlp_come, tuple(qkv_grad), tuple(one_terms[:3]))
    )
    grad_att = att_grads(
        normed_one, late_grad, attended, full_hidden_grad, groups
    )
    sum_mlp, grad_att = lax.optimization_barrier((sum_mlp, grad_att))
    sum_att = lax.psum_scatter(grad_att, "fsdp", scatter_dimension=0, tiled=False)

    sum_att = sum_att.astype(f32)
    out_part = sum_att[:, 3 * local_width :]
    out_pieces = model // out_part.shape[1]
    out_height = shard_rows // out_pieces
    sum_out = jnp.concatenate(
        [out_part[i * out_height : (i + 1) * out_height] for i in range(out_pieces)], axis=1
    )
    sum_gate, sum_up, sum_down = sum_mlp.astype(f32)
    back_here = added(one_terms[-1].astype(f32), one_came)
    input_here = features_of(full_hidden_grad, own_shard).astype(f32) + back_here
    output_here = (hidden + added(terms[0].astype(f32), mlp_come)).astype(bf16)
    out_came = over_fsdp(
        transposed_times(place_in, after(output_here, grad_att)).astype(bf16)
    )
    output = transposed_times(deal_out, out_came).astype(bf16)
    sent_back = transposed_times(place_in, input_here.astype(bf16)).astype(bf16)
    sums = (
        sum_att[:, : local_width],
        sum_att[:, local_width : 2 * local_width],
        sum_att[:, 2 * local_width : 3 * local_width],
        sum_out,
        sum_gate,
        sum_up,
        sum_down,
    )
    came_back, *sums = lax.optimization_barrier((over_fsdp(sent_back), *sums))
    input_grad = transposed_times(deal_out, came_back).astype(bf16)
    return (output, input_grad, *sums)


def solution(mesh):
    in_specs = (
        P("fsdp", "tp"),
        P("fsdp", "tp"),
        P("fsdp", "tp"),
        P("fsdp", "tp"),
        P("fsdp", "tp"),
        P(("tp", "fsdp"), None),
        P("fsdp", "tp"),
        P("fsdp", "tp"),
        P(("tp", "fsdp"), None),
        P(),
        P(),
        P("fsdp"),
    )
    out_specs = (
        P("fsdp", "tp"),
        P("fsdp", "tp"),
        P("fsdp", "tp"),
        P("fsdp", "tp"),
        P("fsdp", "tp"),
        P(("tp", "fsdp"), None),
        P("fsdp", "tp"),
        P("fsdp", "tp"),
        P(("tp", "fsdp"), None),
    )
    return jax.shard_map(
        on_device, mesh=mesh, in_specs=in_specs, out_specs=out_specs, check_vma=False
    )
```
